128 devices in a mesh: dp: 8 (over x_hi, z), expert: 16 (over x_lo, y, core).
Axes of the slice: x: 4 (x_hi: 2, x_lo: 2; x = x_hi * 2 + x_lo), y: 4, z: 4, core: 2. Of those that a mesh axis runs over, the one named last changes fastest.
Arguments:
- tokens: bfloat16 [16384, 2048], P(('dp', 'expert')), may hold values from -6 to 6
- grad_out: bfloat16 [16384, 2048], P(('dp', 'expert')), may hold values from -6 to 6
- combine_weights: bfloat16 [16384, 3], P(('dp', 'expert')), may hold values from 0.099609375 to 1
- expert_ids: int32 [16384, 3], P(('dp', 'expert')), may hold values from 0 to 15, as said below
- w_in: bfloat16 [16, 2048, 1536], P('expert'), may hold values from -0.125 to 0.125
- w_out: bfloat16 [16, 2048, 768], P('expert'), may hold values from -0.21875 to 0.21875
Outputs:
- d_tokens: bfloat16 [16384, 2048], P(('dp', 'expert'))
- d_combine: bfloat16 [16384, 3], P(('dp', 'expert'))
- d_w_in: float32 [16, 2048, 1536], P('expert', 'dp')
- d_w_out: float32 [16, 2048, 768], P('expert', 'dp')
The draws below stay inside these ranges and needn't reach their ends.
Inputs may be any that keep to these rules, and one draw needn't show every extreme that they name: `expert_ids`: each row names 3 different experts; within the 128 rows of one device no expert is named more than 48 times.
All inputs are finite; a program needn't handle non-finite values.
Results may differ from the reference program's by a relative error of at most 0.01.
Values may be sent and summed in bfloat16 or wider, within the bound.
No kernel may reach another device: no remote copies, remote signals or barrier semaphores. Data moves between devices by JAX's collectives and lax.ppermute only.
A program may use at most 128 MiB of HBM per device.

```python
import math
import jax
import jax.numpy as jnp
from jax import lax

D = 2048
FF = 768
TOK_DEV = 128
TOP = 3
TILE = 128
EXPERTS = 16
GROUP_TOK = 2048
TOKENS = 16384
CAP = 48


def draw_expert_ids(key, part):
    block_count = TOKENS // TOK_DEV
    group_count = block_count // EXPERTS
    key_hot, key_blocks = jax.random.split(jax.random.fold_in(key, 7))
    hot_group = jax.random.randint(key_hot, (group_count,), 0, EXPERTS).astype(jnp.int32)
    hot_block = jnp.repeat(hot_group, EXPERTS)
    block_keys = jax.random.split(key_blocks, block_count)

    def one_block(block_key, hot_expert):
        key_pool, key_order = jax.random.split(block_key)
        others = jnp.repeat(jnp.arange(EXPERTS - 1, dtype=jnp.int32), CAP)
        others = others + (others >= hot_expert).astype(jnp.int32)
        others = jax.random.permutation(key_pool, others)
        remain = TOK_DEV * TOP - CAP
        sequence = jnp.concatenate([others[:remain], jnp.full((CAP,), 1, jnp.int32) * hot_expert])
        sequence = jnp.sort(sequence)
        chosen = sequence.reshape(TOP, TOK_DEV).T
        order = jax.random.permutation(key_order, TOK_DEV)
        return chosen[order]
    result = jax.vmap(one_block)(block_keys, hot_block)
    return result.reshape(TOKENS, TOP).astype(jnp.int32)


def shard_levels(stream_key, extent, shards, smallest, top_value):
    level, own = 1.0, jax.random.fold_in(stream_key, 6)
    for position, parts in shards:
        steps = jnp.exp(jax.random.uniform(jax.random.fold_in(own, position), (parts,), jnp.float32, smallest / len(shards), top_value / len(shards)))
        level = level * jnp.repeat(steps, extent[position] // parts).reshape([-1 if axis == position else 1 for axis in range(len(extent))])
    return level


def gaussian(rng, extent, deviation, most, pieces=(), kind=jnp.bfloat16):
    entries = jax.random.normal(rng, extent, jnp.float32) * deviation
    if len(pieces) > 0:
        entries = shard_levels(rng, extent, pieces, -0.22, 0.18) * entries
    return jnp.clip(entries, min=-most, max=most).astype(kind)


def setup_inputs(seed: int = 0) -> dict:
    keys = jax.random.split(jax.random.key(seed), 7)
    tokens = gaussian(keys[0], (TOKENS, D), 1.0, 6.0, ((0, 128),))
    grad_out = gaussian(keys[1], (TOKENS, D), 1.0, 6.0, ((0, 128),))
    combine_weights = jnp.clip(jnp.exp(math.log(1.0) - 2.306499 * jax.random.uniform(keys[2], (TOKENS, TOP), jnp.float32) ** shard_levels(keys[2], (TOKENS, TOP), ((0, 128),), -0.2, 0.2)), 0.099609375, 1.0).astype(jnp.bfloat16)
    expert_ids = draw_expert_ids(jax.random.fold_in(keys[6], 71), 0)
    w_in = gaussian(keys[4], (EXPERTS, D, 2 * FF), D ** -0.5, 0.125, ((0, 16),))
    w_out = gaussian(keys[5], (EXPERTS, D, FF), FF ** -0.5, 0.21875, ((0, 16),))
    return dict(tokens=tokens, grad_out=grad_out, combine_weights=combine_weights, expert_ids=expert_ids, w_in=w_in, w_out=w_out)


def rows_backward(x_rows, dy_rows, p_rows, w_in_e, w_out_e):
    hidden_width = w_out_e.shape[1]
    gate_up = jnp.dot(x_rows, w_in_e, preferred_element_type=jnp.float32)
    gate_pre = gate_up[:, :hidden_width]
    up_pre = gate_up[:, hidden_width:]
    sigmoid_gate = jax.nn.sigmoid(gate_pre)
    gate_act = gate_pre * sigmoid_gate
    hidden = (gate_act * up_pre).astype(jnp.bfloat16)
    output = jnp.dot(hidden, w_out_e.T, preferred_element_type=jnp.float32)
    d_prob = jnp.sum(dy_rows.astype(jnp.float32) * output, axis=1)
    d_output = (p_rows.astype(jnp.float32)[:, None] * dy_rows.astype(jnp.float32)).astype(jnp.bfloat16)
    d_hidden = jnp.dot(d_output, w_out_e, preferred_element_type=jnp.float32)
    d_gate = d_hidden * up_pre * (sigmoid_gate * (1.0 + gate_pre * (1.0 - sigmoid_gate)))
    d_up = d_hidden * gate_act
    d_gate_up = jnp.concatenate([d_gate, d_up], axis=1).astype(jnp.bfloat16)
    d_rows = jnp.dot(d_gate_up, w_in_e.T, preferred_element_type=jnp.float32).astype(jnp.bfloat16)
    return d_rows, d_prob, d_gate_up, d_output, hidden


def reference(tokens, grad_out, combine_weights, expert_ids, w_in, w_out):
    group_count = TOKENS // GROUP_TOK
    slot_count = GROUP_TOK * TOP
    tile_count = slot_count // TILE + EXPERTS + 1
    padded_rows = tile_count * TILE

    def group_pass(total, group_index):
        first = (group_index * GROUP_TOK).astype(jnp.int32)
        x_group = lax.dynamic_slice_in_dim(tokens, first, GROUP_TOK, 0)
        dy_group = lax.dynamic_slice_in_dim(grad_out, first, GROUP_TOK, 0)
        p_group = lax.dynamic_slice_in_dim(combine_weights, first, GROUP_TOK, 0).reshape(-1)
        ids_flat = lax.dynamic_slice_in_dim(expert_ids, first, GROUP_TOK, 0).reshape(-1)
        one_hot = (ids_flat[:, None] == jnp.arange(EXPERTS, dtype=jnp.int32)[None, :]).astype(jnp.int32)
        counts = jnp.sum(one_hot, axis=0)
        earlier = jnp.cumsum(one_hot, axis=0) - one_hot
        rank = jnp.sum(earlier * one_hot, axis=1)
        padded = ((counts + TILE - 1) // TILE) * TILE
        pad_start = jnp.cumsum(padded) - padded
        target = (jnp.take(pad_start, ids_flat) + rank).astype(jnp.int32)
        source = jnp.full((padded_rows,), slot_count, jnp.int32).at[target].set(jnp.arange(slot_count, dtype=jnp.int32))
        tile_first = jnp.arange(tile_count, dtype=jnp.int32) * TILE
        tile_expert = jnp.minimum(jnp.sum((tile_first[:, None] >= (pad_start + padded)[None, :]).astype(jnp.int32), axis=1), EXPERTS - 1)
        valid = source < slot_count
        safe = jnp.minimum(source, slot_count - 1)
        owner = safe // TOP
        x_rows = jnp.where(valid[:, None], x_group[owner], jnp.zeros((), tokens.dtype))
        dy_rows = jnp.where(valid[:, None], dy_group[owner], jnp.zeros((), grad_out.dtype))
        p_rows = jnp.where(valid, p_group[safe], jnp.zeros((), combine_weights.dtype))
        x_tiles = x_rows.reshape(tile_count, TILE, D)
        dy_tiles = dy_rows.reshape(tile_count, TILE, D)
        p_tiles = p_rows.reshape(tile_count, TILE)

        def tile_pass(accum, item):
            x_tile, dy_tile, p_tile, expert_now = item
            w_in_e = w_in[expert_now]
            w_out_e = w_out[expert_now]
            d_rows, d_prob, d_gate_up, d_output, hidden = rows_backward(x_tile, dy_tile, p_tile, w_in_e, w_out_e)
            term_in = jnp.dot(x_tile.T, d_gate_up, preferred_element_type=jnp.float32)
            term_out = jnp.dot(d_output.T, hidden, preferred_element_type=jnp.float32)
            accum = accum.at[expert_now].add(jnp.concatenate([term_in, term_out], axis=1))
            return accum, (d_rows, d_prob)

        accum_start = jnp.zeros((EXPERTS, D, 3 * FF), jnp.float32)
        accum, (d_rows, d_prob) = lax.scan(tile_pass, accum_start, (x_tiles, dy_tiles, p_tiles, tile_expert))
        rounded = lax.optimization_barrier(accum.astype(jnp.bfloat16))
        total = total + rounded.astype(jnp.float32)
        d_slot = d_rows.reshape(padded_rows, D)[target]
        d_tok = jnp.sum(d_slot.reshape(GROUP_TOK, TOP, D).astype(jnp.float32), axis=1).astype(jnp.bfloat16)
        d_comb = d_prob.reshape(padded_rows)[target].reshape(GROUP_TOK, TOP).astype(jnp.bfloat16)
        return total, (d_tok, d_comb)

    total_start = jnp.zeros((EXPERTS, D, 3 * FF), jnp.float32)
    total, (d_tok, d_comb) = lax.scan(group_pass, total_start, jnp.arange(group_count, dtype=jnp.int32))
    d_tokens = d_tok.reshape(TOKENS, D)
    d_combine = d_comb.reshape(TOKENS, TOP)
    return d_tokens, d_combine, total[:, :, :2 * FF], total[:, :, 2 * FF:]
```

```python
import functools

import jax
import jax.numpy as jnp
from jax import lax
from jax.experimental import pallas as pl
from jax.experimental.pallas import tpu as pltpu
from jax.sharding import PartitionSpec as P

BF = jnp.bfloat16
F32 = jnp.float32
CAP = 48
SIDE = 4
VMEM_LIMIT = 58 * 1024 * 1024
NEAR = ((0, 0), (0, -1), (0, 1), (1, 0))
FAR = ((0, 2), (1, -1), (1, 1), (1, 2))


def params(**kw):
    return pltpu.CompilerParams(vmem_limit_bytes=VMEM_LIMIT, **kw)


def cost(flops, nbytes):
    return pl.CostEstimate(flops=int(flops), bytes_accessed=int(nbytes), transcendentals=0)


def spec(shape, index=None):
    zeros = (0,) * len(shape)
    return pl.BlockSpec(shape, index if index is not None else (lambda *_: zeros))


def smem():
    return pl.BlockSpec(memory_space=pltpu.SMEM)


def expert_index(x, y, c):
    return (x % 2) * 8 + (y % SIDE) * 2 + c % 2


def expert_move(value, dx=0, dy=0, dc=0):
    pairs = [
        (expert_index(x, y, c), expert_index(x + dx, y + dy, c + dc))
        for x in range(2)
        for y in range(SIDE)
        for c in range(2)
    ]
    return lax.ppermute(value, "expert", pairs)


def dp_move(value, dx=0, dy=0):
    pairs = [
        (x * SIDE + z, ((x + dx) % 2) * SIDE + (z + dy) % SIDE)
        for x in range(2)
        for z in range(SIDE)
    ]
    return lax.ppermute(value, "dp", pairs)


def mix_kernel(minus, plus, across, up, down, over):
    half = minus.shape[0] // 2
    up[:half] = minus[:half]
    up[half:] = across[:half]
    down[:half] = plus[half:]
    down[half:] = across[half:]
    over[:half] = plus[:half]
    over[half:] = minus[half:]


def mix(minus, plus, across):
    shape = minus.shape
    out = jax.ShapeDtypeStruct(shape, minus.dtype)
    cols = 512
    one = pl.BlockSpec((shape[0], cols), lambda j: (0, j))
    return pl.pallas_call(
        mix_kernel,
        grid=(shape[1] // cols,),
        in_specs=[one] * 3,
        out_specs=[one] * 3,
        out_shape=[out] * 3,
        cost_estimate=cost(0, 6 * minus.size * 2),
        compiler_params=params(),
        name="mix",
    )(minus, plus, across)


def slot_one_hot(pos_ref, sender):
    pos = pos_ref[pl.ds(sender, 1), :]
    slots = lax.broadcasted_iota(jnp.int32, (CAP, pos.shape[1]), 0).astype(F32)
    return jnp.where(slots == pos, 1.0, 0.0)


def pack_rows(sender_ref, pos_ref, sib_ref, blocks, own, sib, row0):
    for r, block in enumerate(blocks):
        sender = sender_ref[r]
        hot = jnp.concatenate(
            [slot_one_hot(pos_ref, sender), slot_one_hot(sib_ref, sender)], axis=0
        ).astype(BF)
        rows = jnp.dot(hot, block, preferred_element_type=F32).astype(BF)
        own[row0 + r * CAP : row0 + (r + 1) * CAP, :] = rows[:CAP]
        sib[row0 + r * CAP : row0 + (r + 1) * CAP, :] = rows[CAP:]


def pack_near_kernel(sender_ref, pos_ref, sib_ref, *refs):
    ins, (own, sib) = refs[:8], refs[8:]
    for part in range(2):
        blocks = [ref[...] for ref in ins[4 * part : 4 * part + 4]]
        pack_rows(sender_ref, pos_ref, sib_ref, blocks, own, sib, part * 4 * CAP)


def pack_far_kernel(sender_ref, pos_ref, sib_ref, *refs):
    ins, (own, sib) = refs[:10], refs[10:]
    for part in range(2):
        up, down, over, last_up, last_down = [ref[...] for ref in ins[5 * part : 5 * part + 5]]
        half = last_up.shape[0]
        blocks = [
            jnp.concatenate([up[:half], down[:half]], axis=0),
            jnp.concatenate([up[half:], over[half:]], axis=0),
            jnp.concatenate([over[:half], down[half:]], axis=0),
            jnp.concatenate([last_up, last_down], axis=0),
        ]
        pack_rows(sender_ref, pos_ref, sib_ref, blocks, own, sib, part * 4 * CAP)


def pack(kernel, senders, pos, sib_pos, arrays, name):
    width = arrays[0].shape[1]
    cols = 512
    col = lambda rows: pl.BlockSpec((rows, cols), lambda j: (0, j))
    out = jax.ShapeDtypeStruct((8 * CAP, width), BF)
    return pl.pallas_call(
        kernel,
        grid=(width // cols,),
        in_specs=[smem(), spec(pos.shape), spec(pos.shape)] + [col(a.shape[0]) for a in arrays],
        out_specs=[col(8 * CAP)] * 2,
        out_shape=[out] * 2,
        cost_estimate=cost(8 * 2 * 96 * 128 * width, 8 * 128 * width * 2 + 2 * 8 * CAP * width * 2),
        compiler_params=params(),
        name=name,
    )(senders, pos, sib_pos, *arrays)


def expert_kernel(
    sender_ref, pos_ref, weight_ref, own, rec, w_gate, w_up, w_out,
    d_gate, d_up, p_hidden, d_prob_rows,
    x_all, dy_all, p_all, d_prob,
):
    step = pl.program_id(0)
    half = 4 * CAP

    @pl.when(step == 0)
    def _():
        x_all[:half] = own[:half]
        x_all[half:] = rec[:half]
        dy_all[:half] = own[half:]
        dy_all[half:] = rec[half:]
        for r in range(8):
            hot = slot_one_hot(pos_ref, sender_ref[r])
            weight = weight_ref[pl.ds(sender_ref[r], 1), :]
            p_all[r * CAP : (r + 1) * CAP, :] = jnp.sum(hot * weight, axis=1, keepdims=True)
        d_prob[...] = jnp.zeros_like(d_prob)

    x = x_all[...]
    a = jnp.dot(x, w_gate[...], preferred_element_type=F32)
    b = jnp.dot(x, w_up[...], preferred_element_type=F32)
    g = jnp.dot(dy_all[...], w_out[...], preferred_element_type=F32)
    p = p_all[...]
    s = jax.nn.sigmoid(a)
    silu = a * s
    hidden = silu * b
    d_prob[...] += jnp.sum(hidden.astype(BF).astype(F32) * g, axis=1, keepdims=True)
    d_hidden = g * p
    d_gate[...] = (d_hidden * b * (s * (1.0 + a * (1.0 - s)))).astype(BF)
    d_up[...] = (d_hidden * silu).astype(BF)
    p_hidden[...] = (hidden * p).astype(BF)

    @pl.when(step == pl.num_programs(0) - 1)
    def _():
        for r in range(8):
            hot = slot_one_hot(pos_ref, sender_ref[r])
            column = d_prob[r * CAP : (r + 1) * CAP, :]
            d_prob_rows[r : r + 1, :] = jnp.sum(hot * column, axis=0, keepdims=True)


def expert_rows(senders, pos, weight, own, rec, w_in, w_out, name):
    model, hidden = w_out.shape
    rows, chunk = 8 * CAP, 256
    steps = hidden // chunk
    out = jax.ShapeDtypeStruct((rows, hidden), BF)
    out_col = pl.BlockSpec((rows, chunk), lambda j: (0, j))
    return pl.pallas_call(
        expert_kernel,
        grid=(steps,),
        in_specs=[
            smem(),
            spec(pos.shape),
            spec(pos.shape),
            spec(own.shape),
            spec(rec.shape),
            pl.BlockSpec((model, chunk), lambda j: (0, j)),
            pl.BlockSpec((model, chunk), lambda j: (0, j + steps)),
            pl.BlockSpec((model, chunk), lambda j: (0, j)),
        ],
        out_specs=[out_col] * 3 + [spec((8, 128))],
        out_shape=[out] * 3 + [jax.ShapeDtypeStruct((8, 128), F32)],
        scratch_shapes=[
            pltpu.VMEM((rows, model), BF),
            pltpu.VMEM((rows, model), BF),
            pltpu.VMEM((rows, 1), F32),
            pltpu.VMEM((rows, 1), F32),
        ],
        cost_estimate=cost(2 * rows * model * 3 * hidden, 2 * model * 3 * hidden + 4 * rows * model),
        compiler_params=params(),
        name=name,
    )(senders, pos, weight, own, rec, w_in, w_in, w_out)


def row_grad_kernel(d_gate, d_up, w_in, own, sib):
    hidden = d_gate.shape[1]
    half = 4 * CAP
    dims = (((1,), (1,)), ((), ()))
    total = lax.dot_general(d_gate[...], w_in[:, :hidden], dims, preferred_element_type=F32)
    total += lax.dot_general(d_up[...], w_in[:, hidden:], dims, preferred_element_type=F32)
    own[...] = total[:half].astype(BF)
    sib[...] = total[half:].astype(BF)


def row_grad(d_gate, d_up, w_in, name):
    model, wide = w_in.shape
    rows, chunk = d_gate.shape[0], 512
    out = jax.ShapeDtypeStruct((rows // 2, model), BF)
    out_col = pl.BlockSpec((rows // 2, chunk), lambda j: (0, j))
    return pl.pallas_call(
        row_grad_kernel,
        grid=(model // chunk,),
        in_specs=[
            spec(d_gate.shape),
            spec(d_up.shape),
            pl.BlockSpec((chunk, wide), lambda j: (j, 0)),
        ],
        out_specs=[out_col] * 2,
        out_shape=[out] * 2,
        cost_estimate=cost(2 * rows * model * wide, 2 * model * wide + 2 * rows * (model + wide)),
        compiler_params=params(),
        name=name,
    )(d_gate, d_up, w_in)


def unpack_rows(sender_ref, pos_ref, sib_ref, own, rec, r):
    sender = sender_ref[r]
    hot = jnp.concatenate(
        [slot_one_hot(pos_ref, sender), slot_one_hot(sib_ref, sender)], axis=0
    ).astype(BF)
    rows = jnp.concatenate([own[r * CAP : (r + 1) * CAP], rec[r * CAP : (r + 1) * CAP]], axis=0)
    dims = (((0,), (0,)), ((), ()))
    return lax.dot_general(hot, rows, dims, preferred_element_type=F32).astype(BF)


def unpack_near_kernel(sender_ref, pos_ref, sib_ref, own, rec, out):
    for at, r in enumerate((2, 1, 3, 0)):
        out[at] = unpack_rows(sender_ref, pos_ref, sib_ref, own, rec, r)


def unpack_far_kernel(sender_ref, pos_ref, sib_ref, own, rec, up, down, over, keep, second):
    half = up.shape[0]
    values = [unpack_rows(sender_ref, pos_ref, sib_ref, own, rec, r) for r in range(4)]
    second[...] = values[0]
    over[half:] = values[1][:half]
    keep[half:] = values[1][half:]
    keep[:half] = values[2][:half]
    over[:half] = values[2][half:]
    up[...] = values[3][:half]
    down[...] = values[3][half:]


def unpack(kernel, senders, pos, sib_pos, own, rec, shapes, name):
    model = own.shape[1]
    cols = 512
    outs = [jax.ShapeDtypeStruct(s, BF) for s in shapes]
    col2 = lambda rows: pl.BlockSpec((rows, cols), lambda j: (0, j))
    col3 = lambda n, rows: pl.BlockSpec((n, rows, cols), lambda j: (0, 0, j))
    return pl.pallas_call(
        kernel,
        grid=(model // cols,),
        in_specs=[smem(), spec(pos.shape), spec(pos.shape), col2(own.shape[0]), col2(rec.shape[0])],
        out_specs=[col2(s[0]) if len(s) == 2 else col3(s[0], s[1]) for s in shapes],
        out_shape=outs,
        cost_estimate=cost(4 * 2 * 128 * 96 * model, 2 * model * (2 * own.shape[0] + 512)),
        compiler_params=params(),
        name=name,
    )(senders, pos, sib_pos, own, rec)


def weight_block(all_grads, xs):
    half = 4 * CAP
    x = jnp.concatenate([ref[:half] for ref in xs], axis=0)
    dy = jnp.concatenate([ref[half:] for ref in xs], axis=0)
    wide = 2 * all_grads.shape[1] // 3
    dims = (((0,), (0,)), ((), ()))
    into = lax.dot_general(x, all_grads[:, :wide], dims, preferred_element_type=F32).astype(BF)
    out = lax.dot_general(dy, all_grads[:, wide:], dims, preferred_element_type=F32).astype(BF)
    return into, out


def collect(grads, all_grads):
    hidden = grads[0].shape[1]
    rows = grads[0].shape[0]
    for half in range(2):
        for k in range(3):
            all_grads[half * rows : (half + 1) * rows, k * hidden : (k + 1) * hidden] = grads[3 * half + k][...]


def weight_first_kernel(dest, *refs):
    xs, grads = refs[:4], refs[4:10]
    up, down, over, keep, all_grads = refs[10:]
    step = pl.program_id(0)

    @pl.when(step == 0)
    def _():
        collect(grads, all_grads)

    into, out = weight_block(all_grads, xs)
    wide = into.shape[1]
    half = up.shape[0]

    def store(ref, at, lo):
        ref[at : at + half, :wide] = into[lo : lo + half]
        ref[at : at + half, wide:] = out[lo : lo + half]

    @pl.when(step == 0)
    def _():
        store(up, 0, 0)
        store(down, 0, half)

    @pl.when(step == 1)
    def _():
        store(keep, 0, 0)
        store(over, 0, half)

    @pl.when(step == 2)
    def _():
        store(over, half, 0)
        store(keep, half, half)


def weight_rest_kernel(dest, *refs):
    xs, grads = refs[:4], refs[4:10]
    block, all_grads = refs[10:]

    @pl.when(pl.program_id(0) == 0)
    def _():
        collect(grads, all_grads)

    into, out = weight_block(all_grads, xs)
    block[0, :, : into.shape[1]] = into
    block[0, :, into.shape[1] :] = out


def weight_grads(kernel, dest, xs, grads, first, name):
    steps = dest.shape[0]
    model = xs[0].shape[1]
    rows = 16 * CAP
    hidden = grads[0].shape[1]
    block, wide = model // 8, 3 * hidden
    whole = lambda shape: pl.BlockSpec(shape, lambda i, d: (0,) * len(shape))
    if first:
        shapes = [(block // 2, wide)] * 2 + [(block, wide)] * 2
        out_specs = [whole(s) for s in shapes]
    else:
        shapes = [(steps, block, wide)]
        out_specs = [pl.BlockSpec((1, block, wide), lambda i, d: (i, 0, 0))]
    return pl.pallas_call(
        kernel,
        grid_spec=pltpu.PrefetchScalarGridSpec(
            num_scalar_prefetch=1,
            grid=(steps,),
            in_specs=[pl.BlockSpec((x.shape[0], block), lambda i, d: (0, d[i])) for x in xs]
            + [whole(g.shape) for g in grads],
            out_specs=out_specs,
            scratch_shapes=[pltpu.VMEM((rows, wide), BF)],
        ),
        out_shape=[jax.ShapeDtypeStruct(s, BF) for s in shapes],
        cost_estimate=cost(2 * rows * block * wide * steps, 2 * steps * block * (wide + 2 * rows) + 2 * rows * wide),
        compiler_params=params(),
        name=name,
    )(dest, *xs, *grads)


def added(a, b):
    return a.astype(F32) + b.astype(F32)


def second_kernel(keep, from_minus, from_plus, straight, up, down):
    half = from_minus.shape[0]
    up[:half] = added(keep[:half], from_minus[...]).astype(BF)
    up[half:] = straight[0, :half]
    down[:half] = added(keep[half:], from_plus[...]).astype(BF)
    down[half:] = straight[0, half:]


def second(keep, from_minus, from_plus, straight, cols, name):
    rows, width = keep.shape
    col = lambda r: pl.BlockSpec((r, cols), lambda j: (0, j))
    return pl.pallas_call(
        second_kernel,
        grid=(width // cols,),
        in_specs=[
            col(rows),
            col(rows // 2),
            col(rows // 2),
            pl.BlockSpec((1, rows, cols), lambda j: (straight.shape[0] - 1, 0, j)),
        ],
        out_specs=[col(rows)] * 2,
        out_shape=[jax.ShapeDtypeStruct((rows, width), BF)] * 2,
        cost_estimate=cost(2 * rows * width, 10 * rows * width),
        compiler_params=params(),
        name=name,
    )(keep, from_minus, from_plus, straight)


def third_kernel(blocks, from_minus, from_plus, from_over, up, down, over):
    half = blocks.shape[1] // 2
    up[:half] = added(blocks[0, :half], from_minus[half:]).astype(BF)
    up[half:] = added(blocks[0, half:], from_over[:half]).astype(BF)
    down[:half] = added(blocks[1, :half], from_over[half:]).astype(BF)
    down[half:] = added(blocks[1, half:], from_plus[half:]).astype(BF)
    over[:half] = added(blocks[2, :half], from_minus[:half]).astype(BF)
    over[half:] = added(blocks[2, half:], from_plus[:half]).astype(BF)


def third(blocks, from_minus, from_plus, from_over, cols, name):
    count, rows, width = blocks.shape
    col = pl.BlockSpec((rows, cols), lambda j: (0, j))
    return pl.pallas_call(
        third_kernel,
        grid=(width // cols,),
        in_specs=[pl.BlockSpec((3, rows, cols), lambda j: (0, 0, j))] + [col] * 3,
        out_specs=[col] * 3,
        out_shape=[jax.ShapeDtypeStruct((rows, width), BF)] * 3,
        cost_estimate=cost(3 * rows * width, 18 * rows * width),
        compiler_params=params(),
        name=name,
    )(blocks, from_minus, from_plus, from_over)


def last_rows_kernel(block, a, b, c, out):
    out[...] = (added(block[0], a[...]) + added(b[...], c[...])).astype(out.dtype)


def last_rows(blocks, a, b, c):
    count, rows, width = blocks.shape
    cols = 512
    col = pl.BlockSpec((rows, cols), lambda j: (0, j))
    return pl.pallas_call(
        last_rows_kernel,
        grid=(width // cols,),
        in_specs=[pl.BlockSpec((1, rows, cols), lambda j: (3, 0, j))] + [col] * 3,
        out_specs=col,
        out_shape=jax.ShapeDtypeStruct((rows, width), BF),
        cost_estimate=cost(3 * rows * width, 10 * rows * width),
        compiler_params=params(),
        name="last_rows",
    )(blocks, a, b, c)


def last_weights_kernel(block, a, b, c, into, out):
    wide = into.shape[2]
    total = added(block[0], a[...]) + added(b[...], c[...])
    into[0] = total[:, :wide]
    out[0] = total[:, wide:]


def last_weights(blocks, a, b, c):
    count, rows, width = blocks.shape
    wide, part = 2 * width // 3, 64
    row = pl.BlockSpec((part, width), lambda j: (j, 0))
    return pl.pallas_call(
        last_weights_kernel,
        grid=(rows // part,),
        in_specs=[pl.BlockSpec((1, part, width), lambda j: (3, j, 0))] + [row] * 3,
        out_specs=[
            pl.BlockSpec((1, part, wide), lambda j: (0, j, 0)),
            pl.BlockSpec((1, part, width - wide), lambda j: (0, j, 0)),
        ],
        out_shape=[
            jax.ShapeDtypeStruct((1, rows, wide), F32),
            jax.ShapeDtypeStruct((1, rows, width - wide), F32),
        ],
        cost_estimate=cost(3 * rows * width, 12 * rows * width),
        compiler_params=params(),
        name="last_weights",
    )(blocks, a, b, c)


def body(tokens, grad_out, combine_weights, expert_ids, w_in, w_out):
    me = lax.axis_index("expert")
    group = lax.axis_index("dp")
    x, y, c = me // 8, (me // 2) % SIDE, me % 2
    gx, gz = group // SIDE, group % SIDE
    tok_rows, routed = expert_ids.shape
    senders = 16
    w_in_e, w_out_e = w_in[0], w_out[0]
    half = tok_rows // 2

    arrays = (tokens, grad_out)
    near = []
    for value in arrays:
        minus = expert_move(value, dy=1)
        plus = expert_move(value, dy=-1)
        across = expert_move(value, dx=1)
        near.append((minus, plus, across))

    routing = jnp.concatenate(
        [expert_ids.T.astype(BF), combine_weights.T, jnp.zeros((8 - 2 * routed, tok_rows), BF)], axis=0
    )
    routing = lax.all_gather(routing, "expert", axis=0, tiled=True).astype(F32)
    routing = routing.reshape(senders, 8, tok_rows)
    ids, probs = routing[:, :routed], routing[:, routed : 2 * routed]
    sib = me + 1 - 2 * c
    earlier = jnp.triu(jnp.ones((tok_rows, tok_rows), BF), 1)

    def positions(expert):
        hit = ids == expert.astype(F32)
        any_hit = jnp.any(hit, axis=1)
        rank = jnp.dot(any_hit.astype(BF), earlier, preferred_element_type=F32)
        return hit, jnp.where(any_hit, rank, -1.0)

    hit, pos = positions(me)
    _, sib_pos = positions(sib)
    weight = jnp.sum(jnp.where(hit, probs, 0.0), axis=1)

    def sender_list(offsets, core):
        return jnp.stack([expert_index(x + dx, y + dy + SIDE, core) for dx, dy in offsets]).astype(jnp.int32)

    near_ids = jnp.concatenate([sender_list(NEAR, c), sender_list(NEAR, 1 - c)])
    far_ids = jnp.concatenate([sender_list(FAR, c), sender_list(FAR, 1 - c)])

    far = []
    for minus, plus, across in near:
        up, down, over = mix(minus, plus, across)
        up = expert_move(up, dy=1)
        down = expert_move(down, dy=-1)
        over = expert_move(over, dx=1)
        last_up = expert_move(up[half:], dy=1)
        last_down = expert_move(down[half:], dy=-1)
        far.append((up, down, over, last_up, last_down))

    near_arrays = [v for own, rest in zip(arrays, near) for v in (own, *rest)]
    own_a, sib_a = pack(pack_near_kernel, near_ids, pos, sib_pos, near_arrays, "pack_near")
    rec_a = expert_move(sib_a, dc=1)
    *grads_a, dp_a = expert_rows(near_ids, pos, weight, own_a, rec_a, w_in_e, w_out_e, "expert_near")
    row_own_a, row_sib_a = row_grad(grads_a[0], grads_a[1], w_in_e, "row_grad_near")
    row_rec_a = expert_move(row_sib_a, dc=1)
    model = tokens.shape[1]
    near_rows = unpack(
        unpack_near_kernel, near_ids, pos, sib_pos, row_own_a, row_rec_a, [(4, tok_rows, model)], "unpack_near"
    )[0]

    far_arrays = [v for rest in far for v in rest]
    own_b, sib_b = pack(pack_far_kernel, far_ids, pos, sib_pos, far_arrays, "pack_far")
    rec_b = expert_move(sib_b, dc=1)
    *grads_b, dp_b = expert_rows(far_ids, pos, weight, own_b, rec_b, w_in_e, w_out_e, "expert_far")

    def dest(dx, dz):
        return ((gx + dx) % 2) * SIDE + (gz + dz + SIDE) % SIDE

    first = jnp.stack([dest(1, 2), dest(1, 1), dest(1, -1)]).astype(jnp.int32)
    rest = jnp.stack([dest(0, 1), dest(0, -1), dest(1, 0), dest(0, 0), dest(0, 2)]).astype(jnp.int32)
    xs = (own_a, rec_a, own_b, rec_b)
    grads = (*grads_a, *grads_b)
    w_up1, w_down1, w_over, w_keep = weight_grads(weight_first_kernel, first, xs, grads, True, "weights_first")
    w_up1 = dp_move(w_up1, dy=1)
    w_down1 = dp_move(w_down1, dy=-1)
    w_over = dp_move(w_over, dx=1)
    (w_rest,) = weight_grads(weight_rest_kernel, rest, xs, grads, False, "weights_rest")

    row_own_b, row_sib_b = row_grad(grads_b[0], grads_b[1], w_in_e, "row_grad_far")
    row_rec_b = expert_move(row_sib_b, dc=1)
    r_up1, r_down1, r_over, r_keep, r_second = unpack(
        unpack_far_kernel, far_ids, pos, sib_pos, row_own_b, row_rec_b,
        [(half, model)] * 2 + [(tok_rows, model)] * 3, "unpack_far",
    )
    r_up1 = expert_move(r_up1, dy=1)
    r_down1 = expert_move(r_down1, dy=-1)
    r_over = expert_move(r_over, dx=1)

    w_up2, w_down2 = second(w_keep, w_up1, w_down1, w_rest, 768, "second_w")
    w_up2 = dp_move(w_up2, dy=1)
    w_down2 = dp_move(w_down2, dy=-1)

    r_up2, r_down2 = second(r_keep, r_up1, r_down1, r_second[None], 512, "second_r")
    r_up2 = expert_move(r_up2, dy=1)
    r_down2 = expert_move(r_down2, dy=-1)
    r_up3, r_down3, r_over3 = third(near_rows, r_up2, r_down2, r_over, 512, "third_r")
    r_up3 = expert_move(r_up3, dy=1)
    r_down3 = expert_move(r_down3, dy=-1)
    r_over3 = expert_move(r_over3, dx=1)
    d_tokens = last_rows(near_rows, r_up3, r_down3, r_over3)

    order = jnp.concatenate([near_ids, far_ids])
    place = (jnp.arange(senders, dtype=jnp.int32)[:, None] == order[None, :]).astype(BF)
    dp_rows = jnp.dot(place, jnp.concatenate([dp_a, dp_b]).astype(BF), preferred_element_type=F32)
    parts = jnp.where(hit, dp_rows[:, None, :], 0.0).astype(BF)
    parts = jnp.pad(parts, ((0, 0), (0, 8 - routed), (0, 0))).reshape(senders * 8, tok_rows)
    d_combine = lax.psum_scatter(parts, "expert", scatter_dimension=0, tiled=True)[:routed].T

    w_up3, w_down3, w_over3 = third(w_rest, w_up2, w_down2, w_over, 768, "third_w")
    w_up3 = dp_move(w_up3, dy=1)
    w_down3 = dp_move(w_down3, dy=-1)
    w_over3 = dp_move(w_over3, dx=1)
    d_w_in, d_w_out = last_weights(w_rest, w_up3, w_down3, w_over3)
    return d_tokens, d_combine, d_w_in, d_w_out


def solution(mesh):
    rows = P(("dp", "expert"), None)
    return jax.shard_map(
        body,
        mesh=mesh,
        in_specs=(rows, rows, rows, rows, P("expert", None, None), P("expert", None, None)),
        out_specs=(rows, rows, P("expert", "dp", None), P("expert", "dp", None)),
        check_vma=False,
    )
```

```python
import functools

import jax
import jax.numpy as jnp
from jax import lax
from jax.experimental import pallas as pl
from jax.experimental.pallas import tpu as pltpu
from jax.sharding import PartitionSpec as P

BF = jnp.bfloat16
F32 = jnp.float32
CAP = 48
CHUNK = 256
SIDE = 4
VMEM_LIMIT = 58 * 1024 * 1024


def params(**kw):
    return pltpu.CompilerParams(vmem_limit_bytes=VMEM_LIMIT, **kw)


def cost(flops, nbytes):
    return pl.CostEstimate(flops=int(flops), bytes_accessed=int(nbytes), transcendentals=0)


def spec(shape, index=None):
    zeros = (0,) * len(shape)
    return pl.BlockSpec(shape, index if index is not None else (lambda *_: zeros))


def smem():
    return pl.BlockSpec(memory_space=pltpu.SMEM)


def unread(count):
    return [pl.BlockSpec(memory_space=pl.ANY)] * count


def col(rows, cols, first=0):
    return pl.BlockSpec((rows, cols), lambda j: (0, j + first))


def fixed(rows, cols, at):
    return pl.BlockSpec((rows, cols), lambda j: (0, at))


def shaped(*shape, dtype=BF):
    return jax.ShapeDtypeStruct(shape, dtype)


def expert_index(x, y, c):
    return (x % 2) * 8 + (y % SIDE) * 2 + c % 2


def expert_move(value, dx=0, dy=0, dc=0):
    pairs = [
        (expert_index(x, y, c), expert_index(x + dx, y + dy, c + dc))
        for x in range(2)
        for y in range(SIDE)
        for c in range(2)
    ]
    return lax.ppermute(value, "expert", pairs)


def dp_move(value, dx=0, dy=0):
    pairs = [
        (x * SIDE + z, ((x + dx) % 2) * SIDE + (z + dy) % SIDE)
        for x in range(2)
        for z in range(SIDE)
    ]
    return lax.ppermute(value, "dp", pairs)


def attach_kernel(tokens, extra, out):
    width = tokens.shape[1]
    out[:, :width] = tokens[...]
    out[:, width:] = extra[...]


def attach(tokens, extra):
    rows, width = tokens.shape
    wide = width + extra.shape[1]
    part = rows // 2
    row = lambda w: pl.BlockSpec((part, w), lambda j: (j, 0))
    return pl.pallas_call(
        attach_kernel,
        grid=(2,),
        in_specs=[row(width), row(extra.shape[1])],
        out_specs=row(wide),
        out_shape=shaped(rows, wide),
        cost_estimate=cost(0, 4 * rows * wide),
        compiler_params=params(),
        name="attach",
    )(tokens, extra)


def mix_kernel(minus, plus, across, up, down):
    half = minus.shape[1]
    up[0] = minus[0]
    up[1] = across[0]
    down[0] = plus[1]
    down[1] = across[1]


def halves(value):
    return value.reshape(2, value.shape[0] // 2, value.shape[1])


def mix(minus, plus, across):
    rows, width = minus.shape
    half, part = rows // 2, 32
    one = pl.BlockSpec((2, part, width), lambda j: (0, j, 0))
    up, down = pl.pallas_call(
        mix_kernel,
        grid=(half // part,),
        in_specs=[one] * 3,
        out_specs=[one] * 2,
        out_shape=[shaped(2, half, width)] * 2,
        cost_estimate=cost(0, 5 * minus.size * 2),
        compiler_params=params(),
        name="mix",
    )(halves(minus), halves(plus), halves(across))
    return up.reshape(rows, width), down.reshape(rows, width)


def mix_over_kernel(minus, plus, across, minus_d, plus_d, after, up, down, over):
    mix_kernel(minus, plus, across, up, down)
    first = minus_d.shape[2]
    over[0, :, :first] = plus_d[0]
    over[1, :, :first] = minus_d[1]
    over[0, :, first:] = plus[0]
    over[1, :, first:] = minus[1]


def mix_over(minus, plus, across, minus_d, plus_d, after):
    rows, width = minus.shape
    first = minus_d.shape[1]
    half, part = rows // 2, 32
    one = lambda w: pl.BlockSpec((2, part, w), lambda j: (0, j, 0))
    up, down, over = pl.pallas_call(
        mix_over_kernel,
        grid=(half // part,),
        in_specs=[one(width)] * 3 + [one(first)] * 2 + unread(1),
        out_specs=[one(width)] * 2 + [one(width + first)],
        out_shape=[shaped(2, half, width)] * 2 + [shaped(2, half, width + first)],
        cost_estimate=cost(0, 9 * minus.size * 2),
        compiler_params=params(),
        name="mix_over",
    )(halves(minus), halves(plus), halves(across), halves(minus_d), halves(plus_d), after)
    return up.reshape(rows, width), down.reshape(rows, width), over.reshape(rows, width + first)


def tail_kernel(up_d, up_x, down_d, down_x, after, up, down):
    first = up_d.shape[2]
    up[:, :first] = up_d[0]
    up[:, first:] = up_x[0]
    down[:, :first] = down_d[0]
    down[:, first:] = down_x[0]


def tail(up_d, up_x, down_d, down_x, after):
    rows, first = up_d.shape
    width = up_x.shape[1]
    half = rows // 2
    part = 32
    one = lambda w: pl.BlockSpec((1, part, w), lambda j: (1, j, 0))
    out = pl.BlockSpec((part, first + width), lambda j: (j, 0))
    return pl.pallas_call(
        tail_kernel,
        grid=(half // part,),
        in_specs=[one(first), one(width)] * 2 + unread(1),
        out_specs=[out] * 2,
        out_shape=[shaped(half, first + width)] * 2,
        cost_estimate=cost(0, 8 * half * (first + width)),
        compiler_params=params(),
        name="tail",
    )(halves(up_d), halves(up_x), halves(down_d), halves(down_x), after)


def slot_one_hot(pos):
    slots = lax.broadcasted_iota(jnp.int32, (CAP, pos.shape[1]), 0).astype(F32)
    return jnp.where(slots == pos, 1.0, 0.0)


def both_hot(pos_ref, r):
    return jnp.concatenate(
        [slot_one_hot(pos_ref[r : r + 1, :]), slot_one_hot(pos_ref[r + 4 : r + 5, :])], axis=0
    ).astype(BF)


def place_slots(experts, routes, pos_ref, hot_ref):
    tokens = routes[0].shape[0]
    turned = [route.astype(F32).T for route in routes]
    rows = []
    for which in range(2):
        expert = experts[which].astype(F32)
        for t in turned:
            hit = (t[0:1] == expert) | (t[1:2] == expert) | (t[2:3] == expert)
            rows.append(jnp.where(hit, 1.0, 0.0))
    hits = jnp.concatenate(rows, axis=0)
    earlier = lax.broadcasted_iota(jnp.int32, (tokens, tokens), 0) < lax.broadcasted_iota(
        jnp.int32, (tokens, tokens), 1
    )
    rank = jnp.dot(hits.astype(BF), jnp.where(earlier, 1.0, 0.0).astype(BF), preferred_element_type=F32)
    pos_ref[...] = jnp.where(hits > 0.5, rank, -1.0)
    for r in range(4):
        hot_ref[r] = both_hot(pos_ref, r)


def pack_rows(hot_ref, blocks, own, sib, row0):
    for r, block in enumerate(blocks):
        rows = jnp.dot(hot_ref[r], block, preferred_element_type=F32).astype(BF)
        own[row0 + r * CAP : row0 + (r + 1) * CAP, :] = rows[:CAP]
        sib[row0 + r * CAP : row0 + (r + 1) * CAP, :] = rows[CAP:]


def near_blocks(refs):
    return [ref[...] for ref in refs]


def far_blocks(refs):
    up, down, over, last_up, last_down = [ref[...] for ref in refs]
    half = last_up.shape[0]
    return [
        jnp.concatenate([up[:half], down[:half]], axis=0),
        jnp.concatenate([up[half:], over[half:]], axis=0),
        jnp.concatenate([over[:half], down[half:]], axis=0),
        jnp.concatenate([last_up, last_down], axis=0),
    ]


def pack_kernel(blocks_of, count, experts, *refs):
    routes, dys, xs = refs[:count], refs[count : 2 * count], refs[2 * count : 3 * count]
    own, sib, own_ex, sib_ex, pos, hot = refs[3 * count + 1 :]

    @pl.when(pl.program_id(0) == 0)
    def _():
        route = blocks_of(routes)
        place_slots((experts[0], experts[1]), route, pos, hot)
        pack_rows(hot, route, own_ex, sib_ex, 0)

    pack_rows(hot, blocks_of(dys), own, sib, 0)
    pack_rows(hot, blocks_of(xs), own, sib, 4 * CAP)


def pack(blocks_of, experts, routes, dys, xs, width, after, name):
    operands = [*routes, *dys, *xs]
    rows = 4 * CAP
    tokens = 128
    return pl.pallas_call(
        functools.partial(pack_kernel, blocks_of, len(dys)),
        grid=(4,),
        in_specs=[smem()] + [s for _, s in operands] + unread(1),
        out_specs=[col(2 * rows, width // 4)] * 2 + [spec((rows, 128))] * 2 + [spec((8, tokens))],
        out_shape=[shaped(2 * rows, width)] * 2
        + [shaped(rows, 128)] * 2
        + [shaped(8, tokens, dtype=F32)],
        scratch_shapes=[pltpu.VMEM((4, 2 * CAP, tokens), BF)],
        cost_estimate=cost(8 * 2 * 96 * 128 * width, 8 * 128 * width * 2 + 8 * rows * width),
        compiler_params=params(),
        name=name,
    )(experts, *[a for a, _ in operands], after)


def expert_kernel(
    experts, own, rec, own_ex, rec_ex, w_gate, w_up, w_out,
    grads, own_prob, sib_prob,
    x_all, dy_all, p_all, d_prob,
):
    step = pl.program_id(0)
    half = own_ex.shape[0]
    me = experts[0].astype(F32)

    @pl.when(step == 0)
    def _():
        dy_all[:half] = own[:half]
        dy_all[half:] = rec[:half]
        x_all[:half] = own[half:]
        x_all[half:] = rec[half:]
        for at, ref in ((0, own_ex), (half, rec_ex)):
            route = ref[...].astype(F32)
            weight = jnp.zeros((half, 1), F32)
            for k in range(3):
                weight += jnp.where(route[:, k : k + 1] == me, route[:, 3 + k : 4 + k], 0.0)
            p_all[at : at + half, :] = weight
        d_prob[...] = jnp.zeros_like(d_prob)

    x = x_all[...]
    a = jnp.dot(x, w_gate[...], preferred_element_type=F32)
    b = jnp.dot(x, w_up[...], preferred_element_type=F32)
    g = jnp.dot(dy_all[...], w_out[...], preferred_element_type=F32)
    p = p_all[...]
    s = jax.nn.sigmoid(a)
    silu = a * s
    hidden = silu * b
    d_prob[...] += jnp.sum(hidden.astype(BF).astype(F32) * g, axis=1, keepdims=True)
    d_hidden = g * p
    chunk = a.shape[1]
    grads[:, :chunk] = (d_hidden * b * (s * (1.0 + a * (1.0 - s)))).astype(BF)
    grads[:, chunk : 2 * chunk] = (d_hidden * silu).astype(BF)
    grads[:, 2 * chunk :] = (hidden * p).astype(BF)

    @pl.when(step == pl.num_programs(0) - 1)
    def _():
        for at, ref, out in ((0, own_ex, own_prob), (half, rec_ex, sib_prob)):
            route = ref[...].astype(F32)
            lane = lax.broadcasted_iota(jnp.int32, route.shape, 1)
            value = jnp.where((route == me) & (lane < 3), d_prob[at : at + half, :], 0.0)
            out[...] = value.astype(BF)


def expert_rows(experts, own, rec, own_ex, rec_ex, w_in, w_out, name):
    model, hidden = w_out.shape
    rows, chunk = own.shape[0], CHUNK
    steps = hidden // chunk
    return pl.pallas_call(
        expert_kernel,
        grid=(steps,),
        in_specs=[
            smem(),
            spec(own.shape),
            spec(rec.shape),
            spec(own_ex.shape),
            spec(rec_ex.shape),
            col(model, chunk),
            col(model, chunk, steps),
            col(model, chunk),
        ],
        out_specs=[col(rows, 3 * chunk)] + [spec(own_ex.shape)] * 2,
        out_shape=[shaped(rows, 3 * hidden)] + [shaped(*own_ex.shape)] * 2,
        scratch_shapes=[
            pltpu.VMEM((rows, model), BF),
            pltpu.VMEM((rows, model), BF),
            pltpu.VMEM((rows, 1), F32),
            pltpu.VMEM((rows, 1), F32),
        ],
        cost_estimate=cost(2 * rows * model * 3 * hidden, 2 * model * 3 * hidden + 4 * rows * model),
        compiler_params=params(),
        name=name,
    )(experts, own, rec, own_ex, rec_ex, w_in, w_in, w_out)


def row_grad_kernel(grads, w_in, after, own, sib):
    hidden = w_in.shape[1] // 2
    half = own.shape[0]
    dims = (((1,), (1,)), ((), ()))
    total = jnp.zeros((2 * half, own.shape[1]), F32)
    for f in range(hidden // CHUNK):
        for k in range(2):
            left = grads[:, (3 * f + k) * CHUNK : (3 * f + k + 1) * CHUNK]
            right = w_in[:, k * hidden + f * CHUNK : k * hidden + (f + 1) * CHUNK]
            total += lax.dot_general(left, right, dims, preferred_element_type=F32)
    own[...] = total[:half].astype(BF)
    sib[...] = total[half:].astype(BF)


def row_grad(grads, w_in, after, name):
    model, wide = w_in.shape
    rows, chunk = grads.shape[0], 512
    return pl.pallas_call(
        row_grad_kernel,
        grid=(model // chunk,),
        in_specs=[spec(grads.shape), pl.BlockSpec((chunk, wide), lambda j: (j, 0))] + unread(1),
        out_specs=[col(rows // 2, chunk)] * 2,
        out_shape=[shaped(rows // 2, model)] * 2,
        cost_estimate=cost(2 * rows * model * wide, 2 * model * wide + 2 * rows * (model + wide)),
        compiler_params=params(),
        name=name,
    )(grads, w_in, after)


def unpack_rows(pos_ref, own, rec, own_ex, rec_ex, r):
    hot = both_hot(pos_ref, r)
    dims = (((0,), (0,)), ((), ()))
    values = []
    for a, b in ((own, rec), (own_ex, rec_ex)):
        rows = jnp.concatenate([a[r * CAP : (r + 1) * CAP], b[r * CAP : (r + 1) * CAP]], axis=0)
        values.append(lax.dot_general(hot, rows, dims, preferred_element_type=F32).astype(BF))
    return values


def unpack_near_kernel(pos, own, rec, own_ex, rec_ex, after, out):
    width = own.shape[1]
    for at, r in enumerate((2, 1, 3, 0)):
        main, extra = unpack_rows(pos, own, rec, own_ex, rec_ex, r)
        out[at, :, :width] = main
        out[at, :, width:] = extra


def unpack_far_kernel(pos, own, rec, own_ex, rec_ex, after, up, down, over, keep, second):
    half, width = up.shape[0], own.shape[1]

    def put(ref, at, values, lo, count):
        main, extra = values
        ref[at : at + count, :width] = main[lo : lo + count]
        ref[at : at + count, width:] = extra[lo : lo + count]

    values = unpack_rows(pos, own, rec, own_ex, rec_ex, 3)
    put(up, 0, values, 0, half)
    put(down, 0, values, half, half)
    values = unpack_rows(pos, own, rec, own_ex, rec_ex, 1)
    put(over, half, values, 0, half)
    put(keep, half, values, half, half)
    values = unpack_rows(pos, own, rec, own_ex, rec_ex, 2)
    put(keep, 0, values, 0, half)
    put(over, 0, values, half, half)
    put(second, 0, unpack_rows(pos, own, rec, own_ex, rec_ex, 0), 0, 2 * half)


def unpack(kernel, pos, own, rec, own_ex, rec_ex, after, shapes, name):
    model = own.shape[1]
    vmem = pl.BlockSpec(memory_space=pltpu.VMEM)
    return pl.pallas_call(
        kernel,
        in_specs=[vmem] * 5 + unread(1),
        out_specs=[vmem] * len(shapes),
        out_shape=[shaped(*s) for s in shapes],
        cost_estimate=cost(4 * 2 * 128 * 96 * model, 2 * model * (2 * own.shape[0] + 512)),
        compiler_params=params(),
        name=name,
    )(pos, own, rec, own_ex, rec_ex, after)


def weight_block(all_grads, xs):
    half = xs[0].shape[0] // 2
    dy = jnp.concatenate([ref[:half] for ref in xs], axis=0)
    x = jnp.concatenate([ref[half:] for ref in xs], axis=0)
    dims = (((0,), (0,)), ((), ()))
    values = []
    for f in range(all_grads.shape[1] // (3 * CHUNK)):
        at = 3 * f * CHUNK
        values.append(
            lax.dot_general(x, all_grads[:, at : at + 2 * CHUNK], dims, preferred_element_type=F32).astype(BF)
        )
        values.append(
            lax.dot_general(
                dy, all_grads[:, at + 2 * CHUNK : at + 3 * CHUNK], dims, preferred_element_type=F32
            ).astype(BF)
        )
    return values


def store_parts(ref, at, values, lo, count):
    left = 0
    for value in values:
        ref[at : at + count, left : left + value.shape[1]] = value[lo : lo + count]
        left += value.shape[1]


def collect(near, far, all_grads):
    rows = near.shape[0]
    all_grads[:rows] = near[...]
    all_grads[rows:] = far[...]


def weight_first_kernel(dest, *refs):
    xs, near, far = refs[:4], refs[4], refs[5]
    up, down, over, keep, all_grads = refs[7:]
    step = pl.program_id(0)

    @pl.when(step == 0)
    def _():
        collect(near, far, all_grads)

    values = weight_block(all_grads, xs)
    half = up.shape[0]

    @pl.when(step == 0)
    def _():
        store_parts(up, 0, values, 0, half)
        store_parts(down, 0, values, half, half)

    @pl.when(step == 1)
    def _():
        store_parts(keep, 0, values, 0, half)
        store_parts(over, 0, values, half, half)

    @pl.when(step == 2)
    def _():
        store_parts(over, half, values, 0, half)
        store_parts(keep, half, values, half, half)


def weight_rest_kernel(dest, *refs):
    xs, near, far = refs[:4], refs[4], refs[5]
    block, all_grads = refs[7:]

    @pl.when(pl.program_id(0) == 0)
    def _():
        collect(near, far, all_grads)

    store_parts(block.at[0], 0, weight_block(all_grads, xs), 0, block.shape[1])


def weight_grads(kernel, dest, xs, near, far, after, first, name):
    steps = dest.shape[0]
    model = xs[0].shape[1]
    rows, wide = 2 * near.shape[0], near.shape[1]
    block = model // 8
    whole = lambda shape: pl.BlockSpec(shape, lambda i, d: (0,) * len(shape))
    if first:
        shapes = [(block // 2, wide)] * 2 + [(block, wide)] * 2
        out_specs = [whole(s) for s in shapes]
    else:
        shapes = [(steps, block, wide)]
        out_specs = [pl.BlockSpec((1, block, wide), lambda i, d: (i, 0, 0))]
    return pl.pallas_call(
        kernel,
        grid_spec=pltpu.PrefetchScalarGridSpec(
            num_scalar_prefetch=1,
            grid=(steps,),
            in_specs=[pl.BlockSpec((x.shape[0], block), lambda i, d: (0, d[i])) for x in xs]
            + [whole(near.shape), whole(far.shape)]
            + unread(1),
            out_specs=out_specs,
            scratch_shapes=[pltpu.VMEM((rows, wide), BF)],
        ),
        out_shape=[shaped(*s) for s in shapes],
        cost_estimate=cost(2 * rows * block * wide * steps, 2 * steps * block * (wide + 2 * rows) + 2 * rows * wide),
        compiler_params=params(),
        name=name,
    )(dest, *xs, near, far, after)


def added(a, b):
    return a.astype(F32) + b.astype(F32)


def second_kernel(keep, from_minus, from_plus, straight, after, up, down):
    up[0] = added(keep[0], from_minus[...]).astype(BF)
    up[1] = straight[0, 0]
    down[0] = added(keep[1], from_plus[...]).astype(BF)
    down[1] = straight[0, 1]


def second(keep, from_minus, from_plus, blocks, after, part, name):
    rows, width = keep.shape
    half = rows // 2
    count = blocks.shape[0]
    pair = pl.BlockSpec((2, part, width), lambda j: (0, j, 0))
    single = pl.BlockSpec((part, width), lambda j: (j, 0))
    up, down = pl.pallas_call(
        second_kernel,
        grid=(half // part,),
        in_specs=[
            pair,
            single,
            single,
            pl.BlockSpec((1, 2, part, width), lambda j: (count - 1, 0, j, 0)),
            *unread(1),
        ],
        out_specs=[pair] * 2,
        out_shape=[shaped(2, half, width)] * 2,
        cost_estimate=cost(2 * rows * width, 10 * rows * width),
        compiler_params=params(),
        name=name,
    )(halves(keep), from_minus, from_plus, blocks.reshape(count, 2, half, width), after)
    return up.reshape(rows, width), down.reshape(rows, width)


def third_kernel(blocks, from_minus, from_plus, from_over, after, up, down, over):
    up[0] = added(blocks[0, 0], from_minus[1]).astype(BF)
    up[1] = added(blocks[0, 1], from_over[0]).astype(BF)
    down[0] = added(blocks[1, 0], from_over[1]).astype(BF)
    down[1] = added(blocks[1, 1], from_plus[1]).astype(BF)
    over[0] = added(blocks[2, 0], from_minus[0]).astype(BF)
    over[1] = added(blocks[2, 1], from_plus[0]).astype(BF)


def third(blocks, from_minus, from_plus, from_over, after, part, name):
    count, rows, width = blocks.shape
    half = rows // 2
    pair = pl.BlockSpec((2, part, width), lambda j: (0, j, 0))
    outs = pl.pallas_call(
        third_kernel,
        grid=(half // part,),
        in_specs=[pl.BlockSpec((3, 2, part, width), lambda j: (0, 0, j, 0))] + [pair] * 3 + unread(1),
        out_specs=[pair] * 3,
        out_shape=[shaped(2, half, width)] * 3,
        cost_estimate=cost(3 * rows * width, 18 * rows * width),
        compiler_params=params(),
        name=name,
    )(blocks.reshape(count, 2, half, width), halves(from_minus), halves(from_plus), halves(from_over), after)
    return [v.reshape(rows, width) for v in outs]


def last_rows_kernel(block, a, b, c, out, prob):
    total = (added(block[0], a[...]) + added(b[...], c[...])).astype(out.dtype)
    width, routed = out.shape[1], prob.shape[1]
    out[...] = total[:, :width]
    prob[...] = total[:, width : width + routed]


def last_rows(blocks, a, b, c, width, routed):
    count, rows, wide = blocks.shape
    part = 32
    row = lambda w: pl.BlockSpec((part, w), lambda j: (j, 0))
    return pl.pallas_call(
        last_rows_kernel,
        grid=(rows // part,),
        in_specs=[pl.BlockSpec((1, part, wide), lambda j: (3, j, 0))] + [row(wide)] * 3,
        out_specs=[row(width), row(routed)],
        out_shape=[shaped(rows, width), shaped(rows, routed)],
        cost_estimate=cost(3 * rows * wide, 10 * rows * wide),
        compiler_params=params(),
        name="last_rows",
    )(blocks, a, b, c)


def last_weights_kernel(block, a, b, c, into, out):
    total = added(block[0], a[...]) + added(b[...], c[...])
    hidden = out.shape[2]
    for f in range(hidden // CHUNK):
        for k in range(3):
            part = total[:, (3 * f + k) * CHUNK : (3 * f + k + 1) * CHUNK]
            if k < 2:
                into[0, :, k * hidden + f * CHUNK : k * hidden + (f + 1) * CHUNK] = part
            else:
                out[0, :, f * CHUNK : (f + 1) * CHUNK] = part


def last_weights(blocks, a, b, c):
    count, rows, width = blocks.shape
    wide, part = 2 * width // 3, 64
    row = pl.BlockSpec((part, width), lambda j: (j, 0))
    return pl.pallas_call(
        last_weights_kernel,
        grid=(rows // part,),
        in_specs=[pl.BlockSpec((1, part, width), lambda j: (3, j, 0))] + [row] * 3,
        out_specs=[
            pl.BlockSpec((1, part, wide), lambda j: (0, j, 0)),
            pl.BlockSpec((1, part, width - wide), lambda j: (0, j, 0)),
        ],
        out_shape=[shaped(1, rows, wide, dtype=F32), shaped(1, rows, width - wide, dtype=F32)],
        cost_estimate=cost(3 * rows * width, 12 * rows * width),
        compiler_params=params(),
        name="last_weights",
    )(blocks, a, b, c)


def body(tokens, grad_out, combine_weights, expert_ids, w_in, w_out):
    me = lax.axis_index("expert")
    group = lax.axis_index("dp")
    gx, gz = group // SIDE, group % SIDE
    experts = jnp.stack([me, me + 1 - 2 * (me % 2)]).astype(jnp.int32)
    tok_rows, routed = expert_ids.shape
    model = tokens.shape[1]
    w_in_e, w_out_e = w_in[0], w_out[0]
    half = tok_rows // 2

    def around(value):
        return expert_move(value, dy=1), expert_move(value, dy=-1), expert_move(value, dx=1)

    d_minus, d_plus, d_across = around(grad_out)
    route = jnp.concatenate([expert_ids.astype(BF), combine_weights], axis=1)
    x_wide = attach(tokens, jnp.pad(route, ((0, 0), (0, 128 - 2 * routed))))
    x_minus, x_plus, x_across = around(x_wide)
    d_up, d_down = mix(d_minus, d_plus, d_across)
    d_up2 = expert_move(d_up, dy=1)
    d_down2 = expert_move(d_down, dy=-1)
    x_up, x_down, over = mix_over(x_minus, x_plus, x_across, d_minus, d_plus, d_up)
    x_up2 = expert_move(x_up, dy=1)
    x_down2 = expert_move(x_down, dy=-1)
    over2 = expert_move(over, dx=1)

    cols = model // 4
    near_d = (grad_out, d_minus, d_plus, d_across)
    near_x = (x_wide, x_minus, x_plus, x_across)
    own_a, sib_a, own_ex_a, sib_ex_a, pos_a = pack(
        near_blocks, experts,
        [(v, fixed(tok_rows, 128, model // 128)) for v in near_x],
        [(v, col(tok_rows, cols)) for v in near_d],
        [(v, col(tok_rows, cols)) for v in near_x],
        model, over, "pack_near",
    )
    rec_a, rec_ex_a = expert_move(sib_a, dc=1), expert_move(sib_ex_a, dc=1)
    grads_a, prob_a, sib_prob_a = expert_rows(
        experts, own_a, rec_a, own_ex_a, rec_ex_a, w_in_e, w_out_e, "expert_near"
    )
    rec_prob_a = expert_move(sib_prob_a, dc=1)

    last_up, last_down = tail(d_up2, x_up2, d_down2, x_down2, grads_a)
    last_up2 = expert_move(last_up, dy=1)
    last_down2 = expert_move(last_down, dy=-1)

    row_own_a, row_sib_a = row_grad(grads_a, w_in_e, last_up, "row_grad_near")
    row_rec_a = expert_move(row_sib_a, dc=1)
    wide = model + 128
    near_rows = unpack(
        unpack_near_kernel, pos_a, row_own_a, row_rec_a, prob_a, rec_prob_a, row_own_a,
        [(4, tok_rows, wide)], "unpack_near",
    )[0]

    at_end = lambda rows: fixed(rows, 128, 2 * model // 128)
    own_b, sib_b, own_ex_b, sib_ex_b, pos_b = pack(
        far_blocks, experts,
        [(x_up2, fixed(tok_rows, 128, model // 128)), (x_down2, fixed(tok_rows, 128, model // 128)),
         (over2, at_end(tok_rows)), (last_up2, at_end(half)), (last_down2, at_end(half))],
        [(d_up2, col(tok_rows, cols)), (d_down2, col(tok_rows, cols)),
         (over2, col(tok_rows, cols)), (last_up2, col(half, cols)), (last_down2, col(half, cols))],
        [(x_up2, col(tok_rows, cols)), (x_down2, col(tok_rows, cols)),
         (over2, col(tok_rows, cols, 4)), (last_up2, col(half, cols, 4)), (last_down2, col(half, cols, 4))],
        model, near_rows, "pack_far",
    )
    rec_b, rec_ex_b = expert_move(sib_b, dc=1), expert_move(sib_ex_b, dc=1)
    grads_b, prob_b, sib_prob_b = expert_rows(
        experts, own_b, rec_b, own_ex_b, rec_ex_b, w_in_e, w_out_e, "expert_far"
    )
    rec_prob_b = expert_move(sib_prob_b, dc=1)

    def dest(dx, dz):
        return ((gx + dx) % 2) * SIDE + (gz + dz + SIDE) % SIDE

    first = jnp.stack([dest(1, 2), dest(1, 1), dest(1, -1)]).astype(jnp.int32)
    rest = jnp.stack([dest(0, 1), dest(0, -1), dest(1, 0), dest(0, 0), dest(0, 2)]).astype(jnp.int32)
    xs = (own_a, rec_a, own_b, rec_b)
    w_up, w_down, w_over, w_keep = weight_grads(
        weight_first_kernel, first, xs, grads_a, grads_b, grads_b, True, "weights_first"
    )
    w_up1 = dp_move(w_up, dy=1)
    w_down1 = dp_move(w_down, dy=-1)
    w_over1 = dp_move(w_over, dx=1)
    (w_rest,) = weight_grads(weight_rest_kernel, rest, xs, grads_a, grads_b, w_keep, False, "weights_rest")
    w_up, w_down = second(w_keep, w_up1, w_down1, w_rest, w_rest, 32, "second_w")
    w_up2 = dp_move(w_up, dy=1)
    w_down2 = dp_move(w_down, dy=-1)

    row_own_b, row_sib_b = row_grad(grads_b, w_in_e, w_up, "row_grad_far")
    row_rec_b = expert_move(row_sib_b, dc=1)
    r_up, r_down, r_over, r_keep, r_second = unpack(
        unpack_far_kernel, pos_b, row_own_b, row_rec_b, prob_b, rec_prob_b, row_own_b,
        [(half, wide)] * 2 + [(tok_rows, wide)] * 3, "unpack_far",
    )
    r_up1 = expert_move(r_up, dy=1)
    r_down1 = expert_move(r_down, dy=-1)
    r_over1 = expert_move(r_over, dx=1)
    r_up, r_down = second(r_keep, r_up1, r_down1, r_second[None], r_over, 32, "second_r")
    r_up2 = expert_move(r_up, dy=1)
    r_down2 = expert_move(r_down, dy=-1)

    w_up, w_down, w_over = third(w_rest, w_up2, w_down2, w_over1, r_up, 32, "third_w")
    w_up3 = dp_move(w_up, dy=1)
    w_down3 = dp_move(w_down, dy=-1)
    w_over3 = dp_move(w_over, dx=1)

    r_up, r_down, r_over = third(near_rows, r_up2, r_down2, r_over1, w_over, 32, "third_r")
    r_up3 = expert_move(r_up, dy=1)
    r_down3 = expert_move(r_down, dy=-1)
    r_over3 = expert_move(r_over, dx=1)
    d_tokens, d_combine = last_rows(near_rows, r_up3, r_down3, r_over3, model, routed)
    d_w_in, d_w_out = last_weights(w_rest, w_up3, w_down3, w_over3)
    return d_tokens, d_combine, d_w_in, d_w_out


def solution(mesh):
    rows = P(("dp", "expert"), None)
    return jax.shard_map(
        body,
        mesh=mesh,
        in_specs=(rows, rows, rows, rows, P("expert", None, None), P("expert", None, None)),
        out_specs=(rows, rows, P("expert", "dp", None), P("expert", "dp", None)),
        check_vma=False,
    )
```

```python
import functools

import jax
import jax.numpy as jnp
from jax import lax
from jax.experimental import pallas as pl
from jax.experimental.pallas import tpu as pltpu
from jax.sharding import PartitionSpec as P

BF = jnp.bfloat16
F32 = jnp.float32
CAP = 48
CHUNK = 256
SIDE = 4
VMEM_LIMIT = 58 * 1024 * 1024


def params(**kw):
    return pltpu.CompilerParams(vmem_limit_bytes=VMEM_LIMIT, **kw)


def cost(flops, nbytes):
    return pl.CostEstimate(flops=int(flops), bytes_accessed=int(nbytes), transcendentals=0)


def spec(shape, index=None):
    zeros = (0,) * len(shape)
    return pl.BlockSpec(shape, index if index is not None else (lambda *_: zeros))


def smem():
    return pl.BlockSpec(memory_space=pltpu.SMEM)


def unread(count):
    return [pl.BlockSpec(memory_space=pl.ANY)] * count


def col(rows, cols, first=0):
    return pl.BlockSpec((rows, cols), lambda j: (0, j + first))


def fixed(rows, cols, at):
    return pl.BlockSpec((rows, cols), lambda j: (0, at))


def shaped(*shape, dtype=BF):
    return jax.ShapeDtypeStruct(shape, dtype)


def expert_index(x, y, c):
    return (x % 2) * 8 + (y % SIDE) * 2 + c % 2


def expert_move(value, dx=0, dy=0, dc=0):
    pairs = [
        (expert_index(x, y, c), expert_index(x + dx, y + dy, c + dc))
        for x in range(2)
        for y in range(SIDE)
        for c in range(2)
    ]
    return lax.ppermute(value, "expert", pairs)


def dp_move(value, dx=0, dy=0):
    pairs = [
        (x * SIDE + z, ((x + dx) % 2) * SIDE + (z + dy) % SIDE)
        for x in range(2)
        for z in range(SIDE)
    ]
    return lax.ppermute(value, "dp", pairs)


def attach_kernel(grad_out, tokens, ids, weights, out):
    width = tokens.shape[1]
    out[:, :width] = grad_out[...]
    out[:, width : 2 * width] = tokens[...]
    rows, routed = ids.shape[1], ids.shape[0]
    turned = jnp.concatenate(
        [ids[...].astype(F32), weights[...].astype(F32), jnp.zeros((128 - 2 * routed, rows), F32)], axis=0
    )
    out[:, 2 * width :] = turned.T.astype(BF)


def attach(grad_out, tokens, ids, weights):
    rows, width = tokens.shape
    wide = 2 * width + 128
    vmem = pl.BlockSpec(memory_space=pltpu.VMEM)
    return pl.pallas_call(
        attach_kernel,
        in_specs=[vmem] * 4,
        out_specs=vmem,
        out_shape=shaped(rows, wide),
        cost_estimate=cost(0, 4 * rows * wide),
        compiler_params=params(),
        name="attach",
    )(grad_out, tokens, ids.T, weights.T)


def halves(value):
    return value.reshape(2, value.shape[0] // 2, value.shape[1])


def tail_kernel(up, down, after, last_up, last_down):
    last_up[...] = up[0]
    last_down[...] = down[0]


def tail(up, down, after):
    rows, width = up.shape
    half, part = rows // 2, 32
    one = pl.BlockSpec((1, part, width), lambda j: (1, j, 0))
    out = pl.BlockSpec((part, width), lambda j: (j, 0))
    return pl.pallas_call(
        tail_kernel,
        grid=(half // part,),
        in_specs=[one] * 2 + unread(1),
        out_specs=[out] * 2,
        out_shape=[shaped(half, width)] * 2,
        cost_estimate=cost(0, 8 * half * width),
        compiler_params=params(),
        name="tail",
    )(halves(up), halves(down), after)


def slot_one_hot(pos):
    slots = lax.broadcasted_iota(jnp.int32, (CAP, pos.shape[1]), 0).astype(F32)
    return jnp.where(slots == pos, 1.0, 0.0)


def both_hot(pos_ref, r):
    return jnp.concatenate(
        [slot_one_hot(pos_ref[r : r + 1, :]), slot_one_hot(pos_ref[r + 4 : r + 5, :])], axis=0
    ).astype(BF)


def place_slots(experts, routes, pos_ref, hot_ref):
    tokens = routes[0].shape[0]
    turned = [route.astype(F32).T for route in routes]
    rows = []
    for which in range(2):
        expert = experts[which].astype(F32)
        for t in turned:
            hit = (t[0:1] == expert) | (t[1:2] == expert) | (t[2:3] == expert)
            rows.append(jnp.where(hit, 1.0, 0.0))
    hits = jnp.concatenate(rows, axis=0)
    earlier = lax.broadcasted_iota(jnp.int32, (tokens, tokens), 0) < lax.broadcasted_iota(
        jnp.int32, (tokens, tokens), 1
    )
    rank = jnp.dot(hits.astype(BF), jnp.where(earlier, 1.0, 0.0).astype(BF), preferred_element_type=F32)
    pos_ref[...] = jnp.where(hits > 0.5, rank, -1.0)
    for r in range(4):
        hot_ref[r] = both_hot(pos_ref, r)


def pack_rows(hot_ref, blocks, own, sib, row0):
    for r, block in enumerate(blocks):
        rows = jnp.dot(hot_ref[r], block, preferred_element_type=F32).astype(BF)
        own[row0 + r * CAP : row0 + (r + 1) * CAP, :] = rows[:CAP]
        sib[row0 + r * CAP : row0 + (r + 1) * CAP, :] = rows[CAP:]


def near_blocks(refs):
    return [ref[...] for ref in refs]


def far_blocks(refs):
    up, down, over, last_up, last_down = [ref[...] for ref in refs]
    half = last_up.shape[0]
    return [
        jnp.concatenate([up[:half], down[:half]], axis=0),
        jnp.concatenate([up[half:], over[half:]], axis=0),
        jnp.concatenate([over[:half], down[half:]], axis=0),
        jnp.concatenate([last_up, last_down], axis=0),
    ]


def pack_kernel(blocks_of, count, experts, *refs):
    routes, dys, xs = refs[:count], refs[count : 2 * count], refs[2 * count : 3 * count]
    own, sib, own_ex, sib_ex, pos, hot = refs[3 * count + 1 :]

    @pl.when(pl.program_id(0) == 0)
    def _():
        route = blocks_of(routes)
        place_slots((experts[0], experts[1]), route, pos, hot)
        pack_rows(hot, route, own_ex, sib_ex, 0)

    pack_rows(hot, blocks_of(dys), own, sib, 0)
    pack_rows(hot, blocks_of(xs), own, sib, 4 * CAP)


def pack_mix_kernel(blocks_of, count, *refs):
    minus, plus, across = refs[1 + 3 * count : 4 + 3 * count]
    up, down, over, hot, sems = refs[-5:]
    half = minus.shape[0] // 2
    low, high = pl.ds(0, half), pl.ds(half, half)
    moves = [
        (minus.at[low], up.at[low]),
        (across.at[low], up.at[high]),
        (plus.at[high], down.at[low]),
        (across.at[high], down.at[high]),
        (plus.at[low], over.at[low]),
        (minus.at[high], over.at[high]),
    ]
    copies = [pltpu.make_async_copy(a, b, sems.at[i]) for i, (a, b) in enumerate(moves)]

    @pl.when(pl.program_id(0) == 0)
    def _():
        for copy in copies:
            copy.start()

    pack_kernel(blocks_of, count, *refs[: 1 + 3 * count], None, *refs[4 + 3 * count : -5], hot)

    @pl.when(pl.program_id(0) == pl.num_programs(0) - 1)
    def _():
        for copy in copies:
            copy.wait()


def pack(blocks_of, experts, routes, dys, xs, width, after, name):
    operands = [*routes, *dys, *xs]
    rows = 4 * CAP
    tokens = 128
    mixed = len(after) > 1
    return pl.pallas_call(
        functools.partial(pack_mix_kernel if mixed else pack_kernel, blocks_of, len(dys)),
        grid=(4,),
        in_specs=[smem()] + [s for _, s in operands] + unread(len(after)),
        out_specs=[col(2 * rows, width // 4)] * 2
        + [spec((rows, 128))] * 2
        + [spec((8, tokens))]
        + (unread(3) if mixed else []),
        out_shape=[shaped(2 * rows, width)] * 2
        + [shaped(rows, 128)] * 2
        + [shaped(8, tokens, dtype=F32)]
        + ([shaped(*after[0].shape)] * 3 if mixed else []),
        scratch_shapes=[pltpu.VMEM((4, 2 * CAP, tokens), BF)]
        + ([pltpu.SemaphoreType.DMA((6,))] if mixed else []),
        cost_estimate=cost(8 * 2 * 96 * 128 * width, 8 * 128 * width * 2 + 8 * rows * width),
        compiler_params=params(),
        name=name,
    )(experts, *[a for a, _ in operands], *after)


def expert_kernel(count, scalars, own, rec, own_ex, rec_ex, w_gate, w_up, w_out, *refs):
    near_grads, near_xs, refs = refs[0], refs[1 : 1 + 2 * count], refs[1 + 2 * count :]
    grads, own_row, sib_row, own_prob, sib_prob = refs[:5]
    first, refs = refs[5 : 5 + (4 if count else 0)], refs[5 + (4 if count else 0) :]
    x_all, dy_all, p_all, d_prob, rows_sum = refs[:5]
    step = pl.program_id(0)
    half = own_ex.shape[0]
    me = scalars[0].astype(F32)
    block = x_all.shape[1] // 8

    @pl.when(step == 0)
    def _():
        dy_all[:half] = own[:half]
        dy_all[half:] = rec[:half]
        x_all[:half] = own[half:]
        x_all[half:] = rec[half:]
        for at, ref in ((0, own_ex), (half, rec_ex)):
            route = ref[...].astype(F32)
            weight = jnp.zeros((half, 1), F32)
            for k in range(3):
                weight += jnp.where(route[:, k : k + 1] == me, route[:, 3 + k : 4 + k], 0.0)
            p_all[at : at + half, :] = weight
        d_prob[...] = jnp.zeros_like(d_prob)
        if count:
            x_turned, dy_turned, all_grads = refs[5:]
            for i in range(count):
                own_a, rec_a = near_xs[2 * i], near_xs[2 * i + 1]
                columns = pl.ds(pl.multiple_of(scalars[2 + i] * block, block), block)
                dy = jnp.concatenate([own_a[:half], rec_a[:half], dy_all[:, columns]], axis=0)
                x = jnp.concatenate([own_a[half:], rec_a[half:], x_all[:, columns]], axis=0)
                x_turned[i * block : (i + 1) * block, :] = x.T
                dy_turned[i * block : (i + 1) * block, :] = dy.T

    x = x_all[...]
    a = jnp.dot(x, w_gate[...], preferred_element_type=F32)
    b = jnp.dot(x, w_up[...], preferred_element_type=F32)
    g = jnp.dot(dy_all[...], w_out[...], preferred_element_type=F32)
    p = p_all[...]
    s = jax.nn.sigmoid(a)
    silu = a * s
    hidden = silu * b
    d_prob[...] += jnp.sum(hidden.astype(BF).astype(F32) * g, axis=1, keepdims=True)
    d_hidden = g * p
    d_gate = (d_hidden * b * (s * (1.0 + a * (1.0 - s)))).astype(BF)
    d_up = (d_hidden * silu).astype(BF)
    p_hidden = (hidden * p).astype(BF)
    chunk = a.shape[1]
    grads[:, :chunk] = d_gate
    grads[:, chunk : 2 * chunk] = d_up
    grads[:, 2 * chunk :] = p_hidden

    dims = (((1,), (1,)), ((), ()))
    row_term = lax.dot_general(d_gate, w_gate[...], dims, preferred_element_type=F32)
    row_term += lax.dot_general(d_up, w_up[...], dims, preferred_element_type=F32)

    @pl.when(step == 0)
    def _():
        rows_sum[...] = row_term

    @pl.when(step > 0)
    def _():
        rows_sum[...] += row_term

    if count:
        x_turned, dy_turned, all_grads = refs[5:]
        up, down, over, keep = first
        all_grads[: 2 * half] = near_grads[...]
        all_grads[2 * half :] = grads[...]
        into = jnp.dot(x_turned[...], all_grads[:, : 2 * chunk], preferred_element_type=F32).astype(BF)
        out = jnp.dot(dy_turned[...], all_grads[:, 2 * chunk :], preferred_element_type=F32).astype(BF)
        part = block // 2
        places = ((up, 0), (down, 0), (keep, 0), (over, 0), (over, part), (keep, part))
        for i, (ref, at) in enumerate(places):
            ref[at : at + part, : 2 * chunk] = into[i * part : (i + 1) * part]
            ref[at : at + part, 2 * chunk :] = out[i * part : (i + 1) * part]

    @pl.when(step == pl.num_programs(0) - 1)
    def _():
        own_row[...] = rows_sum[:half].astype(BF)
        sib_row[...] = rows_sum[half:].astype(BF)
        for at, ref, out in ((0, own_ex, own_prob), (half, rec_ex, sib_prob)):
            route = ref[...].astype(F32)
            lane = lax.broadcasted_iota(jnp.int32, route.shape, 1)
            value = jnp.where((route == me) & (lane < 3), d_prob[at : at + half, :], 0.0)
            out[...] = value.astype(BF)


def expert_rows(scalars, own, rec, own_ex, rec_ex, w_in, w_out, near, name):
    model, hidden = w_out.shape
    rows, chunk = own.shape[0], CHUNK
    steps, block = hidden // chunk, model // 8
    count = 0 if near is None else 3
    whole = lambda shape: pl.BlockSpec(shape, lambda j, d: (0,) * len(shape))
    col = lambda r, c, at=0: pl.BlockSpec((r, c), lambda j, d: (0, j + at))
    in_specs = [
        whole(own.shape),
        whole(rec.shape),
        whole(own_ex.shape),
        whole(rec_ex.shape),
        col(model, chunk),
        col(model, chunk, steps),
        col(model, chunk),
    ]
    operands = [own, rec, own_ex, rec_ex, w_in, w_in, w_out]
    out_specs = [col(rows, 3 * chunk)] + [whole((rows // 2, model))] * 2 + [whole(own_ex.shape)] * 2
    out_shape = [shaped(rows, 3 * hidden)] + [shaped(rows // 2, model)] * 2 + [shaped(*own_ex.shape)] * 2
    scratch = [
        pltpu.VMEM((rows, model), BF),
        pltpu.VMEM((rows, model), BF),
        pltpu.VMEM((rows, 1), F32),
        pltpu.VMEM((rows, 1), F32),
        pltpu.VMEM((rows, model), F32),
    ]
    if count:
        near_grads, own_a, rec_a = near
        in_specs.append(col(rows, 3 * chunk))
        operands.append(near_grads)
        for i in range(count):
            for value in (own_a, rec_a):
                in_specs.append(pl.BlockSpec((rows, block), lambda j, d, i=i: (0, d[2 + i])))
                operands.append(value)
        out_specs += [col(block // 2, 3 * chunk)] * 2 + [col(block, 3 * chunk)] * 2
        out_shape += [shaped(block // 2, 3 * hidden)] * 2 + [shaped(block, 3 * hidden)] * 2
        scratch += [
            pltpu.VMEM((count * block, 2 * rows), BF),
            pltpu.VMEM((count * block, 2 * rows), BF),
            pltpu.VMEM((2 * rows, 3 * chunk), BF),
        ]
    else:
        in_specs.append(whole(own_ex.shape))
        operands.append(own_ex)
    return pl.pallas_call(
        functools.partial(expert_kernel, count),
        grid_spec=pltpu.PrefetchScalarGridSpec(
            num_scalar_prefetch=1,
            grid=(steps,),
            in_specs=in_specs,
            out_specs=out_specs,
            scratch_shapes=scratch,
        ),
        out_shape=out_shape,
        cost_estimate=cost(2 * rows * model * 5 * hidden, 2 * model * 3 * hidden + 8 * rows * model),
        compiler_params=params(),
        name=name,
    )(scalars, *operands)


def unpack_rows(pos_ref, own, rec, own_ex, rec_ex, r):
    hot = both_hot(pos_ref, r)
    dims = (((0,), (0,)), ((), ()))
    values = []
    for a, b in ((own, rec), (own_ex, rec_ex)):
        rows = jnp.concatenate([a[r * CAP : (r + 1) * CAP], b[r * CAP : (r + 1) * CAP]], axis=0)
        values.append(lax.dot_general(hot, rows, dims, preferred_element_type=F32).astype(BF))
    return values


def unpack_near_kernel(pos, own, rec, own_ex, rec_ex, after, out):
    width = own.shape[1]
    for at, r in enumerate((2, 1, 3, 0)):
        main, extra = unpack_rows(pos, own, rec, own_ex, rec_ex, r)
        out[at, :, :width] = main
        out[at, :, width:] = extra


def unpack_far_kernel(pos, own, rec, own_ex, rec_ex, after, up, down, over, keep, second):
    half, width = up.shape[0], own.shape[1]

    def put(ref, at, values, lo, count):
        main, extra = values
        ref[at : at + count, :width] = main[lo : lo + count]
        ref[at : at + count, width:] = extra[lo : lo + count]

    values = unpack_rows(pos, own, rec, own_ex, rec_ex, 3)
    put(up, 0, values, 0, half)
    put(down, 0, values, half, half)
    values = unpack_rows(pos, own, rec, own_ex, rec_ex, 1)
    put(over, half, values, 0, half)
    put(keep, half, values, half, half)
    values = unpack_rows(pos, own, rec, own_ex, rec_ex, 2)
    put(keep, 0, values, 0, half)
    put(over, 0, values, half, half)
    put(second, 0, unpack_rows(pos, own, rec, own_ex, rec_ex, 0), 0, 2 * half)


def unpack(kernel, pos, own, rec, own_ex, rec_ex, after, shapes, name):
    model = own.shape[1]
    vmem = pl.BlockSpec(memory_space=pltpu.VMEM)
    return pl.pallas_call(
        kernel,
        in_specs=[vmem] * 5 + unread(1),
        out_specs=[vmem] * len(shapes),
        out_shape=[shaped(*s) for s in shapes],
        cost_estimate=cost(4 * 2 * 128 * 96 * model, 2 * model * (2 * own.shape[0] + 512)),
        compiler_params=params(),
        name=name,
    )(pos, own, rec, own_ex, rec_ex, after)


def weight_block(all_grads, xs):
    half = xs[0].shape[0] // 2
    dy = jnp.concatenate([ref[:half] for ref in xs], axis=0)
    x = jnp.concatenate([ref[half:] for ref in xs], axis=0)
    dims = (((0,), (0,)), ((), ()))
    values = []
    for f in range(all_grads.shape[1] // (3 * CHUNK)):
        at = 3 * f * CHUNK
        values.append(
            lax.dot_general(x, all_grads[:, at : at + 2 * CHUNK], dims, preferred_element_type=F32).astype(BF)
        )
        values.append(
            lax.dot_general(
                dy, all_grads[:, at + 2 * CHUNK : at + 3 * CHUNK], dims, preferred_element_type=F32
            ).astype(BF)
        )
    return values


def store_parts(ref, at, values, lo, count):
    left = 0
    for value in values:
        ref[at : at + count, left : left + value.shape[1]] = value[lo : lo + count]
        left += value.shape[1]


def collect(near, far, all_grads):
    rows = near.shape[0]
    all_grads[:rows] = near[...]
    all_grads[rows:] = far[...]


def weight_rest_kernel(dest, *refs):
    xs, near, far = refs[:4], refs[4], refs[5]
    block, all_grads = refs[7:]

    @pl.when(pl.program_id(0) == 0)
    def _():
        collect(near, far, all_grads)

    store_parts(block.at[0], 0, weight_block(all_grads, xs), 0, block.shape[1])


def weight_grads(dest, xs, near, far, after, name):
    steps = dest.shape[0]
    model = xs[0].shape[1]
    rows, wide = 2 * near.shape[0], near.shape[1]
    block = model // 8
    whole = lambda shape: pl.BlockSpec(shape, lambda i, d: (0,) * len(shape))
    shapes = [(steps, block, wide)]
    out_specs = [pl.BlockSpec((1, block, wide), lambda i, d: (i, 0, 0))]
    return pl.pallas_call(
        weight_rest_kernel,
        grid_spec=pltpu.PrefetchScalarGridSpec(
            num_scalar_prefetch=1,
            grid=(steps,),
            in_specs=[pl.BlockSpec((x.shape[0], block), lambda i, d: (0, d[i])) for x in xs]
            + [whole(near.shape), whole(far.shape)]
            + unread(1),
            out_specs=out_specs,
            scratch_shapes=[pltpu.VMEM((rows, wide), BF)],
        ),
        out_shape=[shaped(*s) for s in shapes],
        cost_estimate=cost(2 * rows * block * wide * steps, 2 * steps * block * (wide + 2 * rows) + 2 * rows * wide),
        compiler_params=params(),
        name=name,
    )(dest, *xs, near, far, after)


def added(a, b):
    return a.astype(F32) + b.astype(F32)


def second_kernel(keep, from_minus, from_plus, straight, after, up, down):
    up[0] = added(keep[0], from_minus[...]).astype(BF)
    up[1] = straight[0, 0]
    down[0] = added(keep[1], from_plus[...]).astype(BF)
    down[1] = straight[0, 1]


def second(keep, from_minus, from_plus, blocks, after, part, name):
    rows, width = keep.shape
    half = rows // 2
    count = blocks.shape[0]
    pair = pl.BlockSpec((2, part, width), lambda j: (0, j, 0))
    single = pl.BlockSpec((part, width), lambda j: (j, 0))
    up, down = pl.pallas_call(
        second_kernel,
        grid=(half // part,),
        in_specs=[
            pair,
            single,
            single,
            pl.BlockSpec((1, 2, part, width), lambda j: (count - 1, 0, j, 0)),
            *unread(1),
        ],
        out_specs=[pair] * 2,
        out_shape=[shaped(2, half, width)] * 2,
        cost_estimate=cost(2 * rows * width, 10 * rows * width),
        compiler_params=params(),
        name=name,
    )(halves(keep), from_minus, from_plus, blocks.reshape(count, 2, half, width), after)
    return up.reshape(rows, width), down.reshape(rows, width)


def third_kernel(blocks, from_minus, from_plus, from_over, after, up, down, over):
    up[0] = added(blocks[0, 0], from_minus[1]).astype(BF)
    up[1] = added(blocks[0, 1], from_over[0]).astype(BF)
    down[0] = added(blocks[1, 0], from_over[1]).astype(BF)
    down[1] = added(blocks[1, 1], from_plus[1]).astype(BF)
    over[0] = added(blocks[2, 0], from_minus[0]).astype(BF)
    over[1] = added(blocks[2, 1], from_plus[0]).astype(BF)


def third(blocks, from_minus, from_plus, from_over, after, part, name):
    count, rows, width = blocks.shape
    half = rows // 2
    pair = pl.BlockSpec((2, part, width), lambda j: (0, j, 0))
    outs = pl.pallas_call(
        third_kernel,
        grid=(half // part,),
        in_specs=[pl.BlockSpec((3, 2, part, width), lambda j: (0, 0, j, 0))] + [pair] * 3 + unread(1),
        out_specs=[pair] * 3,
        out_shape=[shaped(2, half, width)] * 3,
        cost_estimate=cost(3 * rows * width, 18 * rows * width),
        compiler_params=params(),
        name=name,
    )(blocks.reshape(count, 2, half, width), halves(from_minus), halves(from_plus), halves(from_over), after)
    return [v.reshape(rows, width) for v in outs]


def last_rows_kernel(block, a, b, c, out, prob):
    total = (added(block[0], a[...]) + added(b[...], c[...])).astype(out.dtype)
    width, routed = out.shape[1], prob.shape[1]
    out[...] = total[:, :width]
    prob[...] = total[:, width : width + routed]


def last_rows(blocks, a, b, c, width, routed):
    count, rows, wide = blocks.shape
    part = 64
    row = lambda w: pl.BlockSpec((part, w), lambda j: (j, 0))
    return pl.pallas_call(
        last_rows_kernel,
        grid=(rows // part,),
        in_specs=[pl.BlockSpec((1, part, wide), lambda j: (3, j, 0))] + [row(wide)] * 3,
        out_specs=[row(width), row(routed)],
        out_shape=[shaped(rows, width), shaped(rows, routed)],
        cost_estimate=cost(3 * rows * wide, 10 * rows * wide),
        compiler_params=params(),
        name="last_rows",
    )(blocks, a, b, c)


def last_weights_kernel(block, a, b, c, into, out):
    total = added(block[0], a[...]) + added(b[...], c[...])
    hidden = out.shape[2]
    for f in range(hidden // CHUNK):
        for k in range(3):
            part = total[:, (3 * f + k) * CHUNK : (3 * f + k + 1) * CHUNK]
            if k < 2:
                into[0, :, k * hidden + f * CHUNK : k * hidden + (f + 1) * CHUNK] = part
            else:
                out[0, :, f * CHUNK : (f + 1) * CHUNK] = part


def last_weights(blocks, a, b, c):
    count, rows, width = blocks.shape
    wide, part = 2 * width // 3, 128
    row = pl.BlockSpec((part, width), lambda j: (j, 0))
    return pl.pallas_call(
        last_weights_kernel,
        grid=(rows // part,),
        in_specs=[pl.BlockSpec((1, part, width), lambda j: (3, j, 0))] + [row] * 3,
        out_specs=[
            pl.BlockSpec((1, part, wide), lambda j: (0, j, 0)),
            pl.BlockSpec((1, part, width - wide), lambda j: (0, j, 0)),
        ],
        out_shape=[shaped(1, rows, wide, dtype=F32), shaped(1, rows, width - wide, dtype=F32)],
        cost_estimate=cost(3 * rows * width, 12 * rows * width),
        compiler_params=params(),
        name="last_weights",
    )(blocks, a, b, c)


def body(tokens, grad_out, combine_weights, expert_ids, w_in, w_out):
    me = lax.axis_index("expert")
    group = lax.axis_index("dp")
    gx, gz = group // SIDE, group % SIDE

    def dest(dx, dz):
        return ((gx + dx) % 2) * SIDE + (gz + dz + SIDE) % SIDE

    experts = jnp.stack([me, me + 1 - 2 * (me % 2)]).astype(jnp.int32)
    first = jnp.stack([dest(1, 2), dest(1, 1), dest(1, -1)]).astype(jnp.int32)
    rest = jnp.stack([dest(0, 1), dest(0, -1), dest(1, 0), dest(0, 0), dest(0, 2)]).astype(jnp.int32)
    scalars = jnp.concatenate([experts, first])
    tok_rows, routed = expert_ids.shape
    model = tokens.shape[1]
    w_in_e, w_out_e = w_in[0], w_out[0]
    half = tok_rows // 2

    mine = attach(grad_out, tokens, expert_ids, combine_weights)
    minus, plus, across = expert_move(mine, dy=1), expert_move(mine, dy=-1), expert_move(mine, dx=1)
    cols = model // 4

    def packed(blocks_of, values, after, name):
        return pack(
            blocks_of, experts,
            [(v, fixed(v.shape[0], 128, 2 * model // 128)) for v in values],
            [(v, col(v.shape[0], cols)) for v in values],
            [(v, col(v.shape[0], cols, 4)) for v in values],
            model, after, name,
        )

    own_a, sib_a, own_ex_a, sib_ex_a, pos_a, up, down, over = packed(
        near_blocks, (mine, minus, plus, across), (minus, plus, across), "pack_near"
    )
    up2 = expert_move(up, dy=1)
    down2 = expert_move(down, dy=-1)
    over2 = expert_move(over, dx=1)
    rec_a, rec_ex_a = expert_move(sib_a, dc=1), expert_move(sib_ex_a, dc=1)
    grads_a, row_own_a, row_sib_a, prob_a, sib_prob_a = expert_rows(
        scalars, own_a, rec_a, own_ex_a, rec_ex_a, w_in_e, w_out_e, None, "expert_near"
    )
    rec_prob_a = expert_move(sib_prob_a, dc=1)
    row_rec_a = expert_move(row_sib_a, dc=1)

    last_up, last_down = tail(up2, down2, row_own_a)
    last_up2 = expert_move(last_up, dy=1)
    last_down2 = expert_move(last_down, dy=-1)
    wide = model + 128
    near_rows = unpack(
        unpack_near_kernel, pos_a, row_own_a, row_rec_a, prob_a, rec_prob_a, last_up,
        [(4, tok_rows, wide)], "unpack_near",
    )[0]

    own_b, sib_b, own_ex_b, sib_ex_b, pos_b = packed(
        far_blocks, (up2, down2, over2, last_up2, last_down2), (near_rows,), "pack_far"
    )
    rec_b, rec_ex_b = expert_move(sib_b, dc=1), expert_move(sib_ex_b, dc=1)
    grads_b, row_own_b, row_sib_b, prob_b, sib_prob_b, w_up, w_down, w_over, w_keep = expert_rows(
        scalars, own_b, rec_b, own_ex_b, rec_ex_b, w_in_e, w_out_e, (grads_a, own_a, rec_a), "expert_far"
    )
    rec_prob_b = expert_move(sib_prob_b, dc=1)
    row_rec_b = expert_move(row_sib_b, dc=1)

    xs = (own_a, rec_a, own_b, rec_b)
    w_up1 = dp_move(w_up, dy=1)
    w_down1 = dp_move(w_down, dy=-1)
    w_over1 = dp_move(w_over, dx=1)
    (w_rest,) = weight_grads(rest, xs, grads_a, grads_b, w_keep, "weights_rest")
    w_up, w_down = second(w_keep, w_up1, w_down1, w_rest, w_rest, 64, "second_w")
    w_up2 = dp_move(w_up, dy=1)
    w_down2 = dp_move(w_down, dy=-1)

    r_up, r_down, r_over, r_keep, r_second = unpack(
        unpack_far_kernel, pos_b, row_own_b, row_rec_b, prob_b, rec_prob_b, w_up,
        [(half, wide)] * 2 + [(tok_rows, wide)] * 3, "unpack_far",
    )
    r_up1 = expert_move(r_up, dy=1)
    r_down1 = expert_move(r_down, dy=-1)
    r_over1 = expert_move(r_over, dx=1)
    r_up, r_down = second(r_keep, r_up1, r_down1, r_second[None], w_over1, 64, "second_r")
    r_up2 = expert_move(r_up, dy=1)
    r_down2 = expert_move(r_down, dy=-1)

    w_up, w_down, w_over = third(w_rest, w_up2, w_down2, w_over1, r_over1, 64, "third_w")
    w_up3 = dp_move(w_up, dy=1)
    w_down3 = dp_move(w_down, dy=-1)
    w_over3 = dp_move(w_over, dx=1)

    r_up, r_down, r_over = third(near_rows, r_up2, r_down2, r_over1, w_over, 64, "third_r")
    r_up3 = expert_move(r_up, dy=1)
    r_down3 = expert_move(r_down, dy=-1)
    r_over3 = expert_move(r_over, dx=1)
    d_tokens, d_combine = last_rows(near_rows, r_up3, r_down3, r_over3, model, routed)
    d_w_in, d_w_out = last_weights(w_rest, w_up3, w_down3, w_over3)
    return d_tokens, d_combine, d_w_in, d_w_out


def solution(mesh):
    rows = P(("dp", "expert"), None)
    return jax.shard_map(
        body,
        mesh=mesh,
        in_specs=(rows, rows, rows, rows, P("expert", None, None), P("expert", None, None)),
        out_specs=(rows, rows, P("expert", "dp", None), P("expert", "dp", None)),
        check_vma=False,
    )
```

```python
import functools

import jax
import jax.numpy as jnp
from jax import lax
from jax.experimental import pallas as pl
from jax.experimental.pallas import tpu as pltpu
from jax.sharding import PartitionSpec as P

BF = jnp.bfloat16
F32 = jnp.float32
CAP = 48
SIDE = 4
VMEM_LIMIT = 58 * 1024 * 1024


def params(**kw):
    return pltpu.CompilerParams(vmem_limit_bytes=VMEM_LIMIT, **kw)


def cost(flops, nbytes):
    return pl.CostEstimate(flops=int(flops), bytes_accessed=int(nbytes), transcendentals=0)


def spec(shape, index=None):
    zeros = (0,) * len(shape)
    return pl.BlockSpec(shape, index if index is not None else (lambda *_: zeros))


def smem():
    return pl.BlockSpec(memory_space=pltpu.SMEM)


def unread(count):
    return [pl.BlockSpec(memory_space=pl.ANY)] * count


def col(rows, cols, first=0):
    return pl.BlockSpec((rows, cols), lambda j: (0, j + first))


def fixed(rows, cols, at):
    return pl.BlockSpec((rows, cols), lambda j: (0, at))


def shaped(*shape, dtype=BF):
    return jax.ShapeDtypeStruct(shape, dtype)


def expert_index(x, y, c):
    return (x % 2) * 8 + (y % SIDE) * 2 + c % 2


def expert_move(value, dx=0, dy=0, dc=0):
    pairs = [
        (expert_index(x, y, c), expert_index(x + dx, y + dy, c + dc))
        for x in range(2)
        for y in range(SIDE)
        for c in range(2)
    ]
    return lax.ppermute(value, "expert", pairs)


def dp_move(value, dx=0, dy=0):
    pairs = [
        (x * SIDE + z, ((x + dx) % 2) * SIDE + (z + dy) % SIDE)
        for x in range(2)
        for z in range(SIDE)
    ]
    return lax.ppermute(value, "dp", pairs)


def attach_kernel(grad_out, tokens, ids, weights, out):
    width = tokens.shape[1]
    out[:, :width] = grad_out[...]
    out[:, width : 2 * width] = tokens[...]
    rows, routed = ids.shape[1], ids.shape[0]
    turned = jnp.concatenate(
        [ids[...].astype(F32), weights[...].astype(F32), jnp.zeros((128 - 2 * routed, rows), F32)], axis=0
    )
    out[:, 2 * width :] = turned.T.astype(BF)


def attach(grad_out, tokens, ids, weights):
    rows, width = tokens.shape
    wide = 2 * width + 128
    vmem = pl.BlockSpec(memory_space=pltpu.VMEM)
    return pl.pallas_call(
        attach_kernel,
        in_specs=[vmem] * 4,
        out_specs=vmem,
        out_shape=shaped(rows, wide),
        cost_estimate=cost(0, 4 * rows * wide),
        compiler_params=params(),
        name="attach",
    )(grad_out, tokens, ids.T, weights.T)


def halves(value):
    return value.reshape(2, value.shape[0] // 2, value.shape[1])


def tail_kernel(up, down, after, last_up, last_down):
    last_up[...] = up[0]
    last_down[...] = down[0]


def tail(up, down, after):
    rows, width = up.shape
    half, part = rows // 2, 32
    one = pl.BlockSpec((1, part, width), lambda j: (1, j, 0))
    out = pl.BlockSpec((part, width), lambda j: (j, 0))
    return pl.pallas_call(
        tail_kernel,
        grid=(half // part,),
        in_specs=[one] * 2 + unread(1),
        out_specs=[out] * 2,
        out_shape=[shaped(half, width)] * 2,
        cost_estimate=cost(0, 8 * half * width),
        compiler_params=params(),
        name="tail",
    )(halves(up), halves(down), after)


def slot_one_hot(pos):
    slots = lax.broadcasted_iota(jnp.int32, (CAP, pos.shape[1]), 0).astype(F32)
    return jnp.where(slots == pos, 1.0, 0.0)


def both_hot(pos_ref, r):
    return jnp.concatenate(
        [slot_one_hot(pos_ref[r : r + 1, :]), slot_one_hot(pos_ref[r + 4 : r + 5, :])], axis=0
    ).astype(BF)


def place_slots(experts, routes, pos_ref, hot_ref):
    tokens = routes[0].shape[0]
    turned = [route.astype(F32).T for route in routes]
    rows = []
    for which in range(2):
        expert = experts[which].astype(F32)
        for t in turned:
            hit = (t[0:1] == expert) | (t[1:2] == expert) | (t[2:3] == expert)
            rows.append(jnp.where(hit, 1.0, 0.0))
    hits = jnp.concatenate(rows, axis=0)
    earlier = lax.broadcasted_iota(jnp.int32, (tokens, tokens), 0) < lax.broadcasted_iota(
        jnp.int32, (tokens, tokens), 1
    )
    rank = jnp.dot(hits.astype(BF), jnp.where(earlier, 1.0, 0.0).astype(BF), preferred_element_type=F32)
    pos_ref[...] = jnp.where(hits > 0.5, rank, -1.0)
    for r in range(4):
        hot_ref[r] = both_hot(pos_ref, r)


def pack_rows(hot_ref, blocks, own, sib, row0):
    for r, block in enumerate(blocks):
        rows = jnp.dot(hot_ref[r], block, preferred_element_type=F32).astype(BF)
        own[row0 + r * CAP : row0 + (r + 1) * CAP, :] = rows[:CAP]
        sib[row0 + r * CAP : row0 + (r + 1) * CAP, :] = rows[CAP:]


def near_blocks(refs):
    return [ref[...] for ref in refs]


def far_blocks(refs):
    up, down, over, last_up, last_down = [ref[...] for ref in refs]
    half = last_up.shape[0]
    return [
        jnp.concatenate([up[:half], down[:half]], axis=0),
        jnp.concatenate([up[half:], over[half:]], axis=0),
        jnp.concatenate([over[:half], down[half:]], axis=0),
        jnp.concatenate([last_up, last_down], axis=0),
    ]


def pack_kernel(blocks_of, count, experts, *refs):
    routes, dys, xs = refs[:count], refs[count : 2 * count], refs[2 * count : 3 * count]
    own, sib, own_ex, sib_ex, pos, hot = refs[3 * count + 1 :]

    @pl.when(pl.program_id(0) == 0)
    def _():
        route = blocks_of(routes)
        place_slots((experts[0], experts[1]), route, pos, hot)
        pack_rows(hot, route, own_ex, sib_ex, 0)

    pack_rows(hot, blocks_of(dys), own, sib, 0)
    pack_rows(hot, blocks_of(xs), own, sib, 4 * CAP)


def pack_mix_kernel(blocks_of, count, *refs):
    up, down, over, hot = refs[-4:]
    pack_kernel(blocks_of, count, *refs[: 1 + 3 * count], None, *refs[2 + 3 * count : -4], hot)
    routes, dys, xs = [refs[1 + count * k : 1 + count * (k + 1)] for k in range(3)]
    step = pl.program_id(0)
    half, cols = dys[0].shape[0] // 2, dys[0].shape[1]
    width = 4 * cols

    def place(blocks, columns):
        _, minus, plus, across = blocks
        up[:half, columns] = minus[:half]
        up[half:, columns] = across[:half]
        down[:half, columns] = plus[half:]
        down[half:, columns] = across[half:]
        over[:half, columns] = plus[:half]
        over[half:, columns] = minus[half:]

    place(dys, pl.ds(pl.multiple_of(step * cols, cols), cols))
    place(xs, pl.ds(pl.multiple_of(step * cols + width, cols), cols))

    @pl.when(step == 0)
    def _():
        place(routes, pl.ds(2 * width, 128))


def pack(blocks_of, experts, routes, dys, xs, width, after, name):
    operands = [*routes, *dys, *xs]
    rows = 4 * CAP
    tokens = 128
    mixed = after is None
    wide = 2 * width + 128
    return pl.pallas_call(
        functools.partial(pack_mix_kernel if mixed else pack_kernel, blocks_of, len(dys)),
        grid=(4,),
        in_specs=[smem()] + [s for _, s in operands] + unread(1),
        out_specs=[col(2 * rows, width // 4)] * 2
        + [spec((rows, 128))] * 2
        + [spec((8, tokens))]
        + ([spec((tokens, wide))] * 3 if mixed else []),
        out_shape=[shaped(2 * rows, width)] * 2
        + [shaped(rows, 128)] * 2
        + [shaped(8, tokens, dtype=F32)]
        + ([shaped(tokens, wide)] * 3 if mixed else []),
        scratch_shapes=[pltpu.VMEM((4, 2 * CAP, tokens), BF)],
        cost_estimate=cost(8 * 2 * 96 * 128 * width, 8 * 128 * width * 2 + 8 * rows * width),
        compiler_params=params(),
        name=name,
    )(experts, *[a for a, _ in operands], experts if mixed else after)


def expert_kernel(count, scalars, own_ex, rec_ex, own, rec, w_in, w_out, *refs):
    near, refs = refs[:3], refs[3:]
    grads, own_row, sib_row, own_prob, sib_prob = refs[:5]
    first, refs = refs[5 : 5 + (4 if count else 0)], refs[5 + (4 if count else 0) :]
    x_all, dy_all, w_all, w_out_all, a_all, b_all, g_all, sems = refs[:8]
    half, (model, hidden) = own_ex.shape[0], w_out.shape
    block = model // 8
    base = grads.shape[0] - 2 * half
    me = scalars[0].astype(F32)
    low, high = pl.ds(0, half), pl.ds(half, half)
    gate, up_cols = pl.ds(0, hidden), pl.ds(hidden, hidden)
    moves = [
        (own.at[high], x_all.at[low]),
        (rec.at[high], x_all.at[high]),
        (w_in.at[:, gate], w_all.at[:, gate]),
        (w_in.at[:, up_cols], w_all.at[:, up_cols]),
        (own.at[low], dy_all.at[low]),
        (rec.at[low], dy_all.at[high]),
        (w_out, w_out_all),
    ]
    if count:
        near_grads, own_a, rec_a = near
        near_cols, x_turned, dy_turned = refs[8:]
        moves.append((near_grads, grads.at[pl.ds(0, base)]))
        for i in range(count):
            columns = pl.ds(pl.multiple_of(scalars[2 + i] * block, block), block)
            moves.append((own_a.at[:, columns], near_cols.at[2 * i]))
            moves.append((rec_a.at[:, columns], near_cols.at[2 * i + 1]))
    copies = [pltpu.make_async_copy(a, b, sems.at[i]) for i, (a, b) in enumerate(moves)]
    for copy in copies:
        copy.start()

    routes = [ref[...].astype(F32) for ref in (own_ex, rec_ex)]
    weights = []
    for route in routes:
        weight = jnp.zeros((half, 1), F32)
        for k in range(3):
            weight += jnp.where(route[:, k : k + 1] == me, route[:, 3 + k : 4 + k], 0.0)
        weights.append(weight)
    p = jnp.concatenate(weights, axis=0)

    for copy in copies[:3]:
        copy.wait()
    a_all[...] = jnp.dot(x_all[...], w_all[:, :hidden], preferred_element_type=F32)
    copies[3].wait()
    b_all[...] = jnp.dot(x_all[...], w_all[:, hidden:], preferred_element_type=F32)
    for copy in copies[4:7]:
        copy.wait()
    g_all[...] = jnp.dot(dy_all[...], w_out_all[...], preferred_element_type=F32)

    d_prob = jnp.zeros((2 * half, 1), F32)
    chunk = 256
    for f in range(hidden // chunk):
        at = slice(f * chunk, (f + 1) * chunk)
        a, b, g = a_all[:, at], b_all[:, at], g_all[:, at]
        s = jax.nn.sigmoid(a)
        silu = a * s
        value = silu * b
        d_prob += jnp.sum(value.astype(BF).astype(F32) * g, axis=1, keepdims=True)
        d_hidden = g * p
        grads[base:, at] = (d_hidden * b * (s * (1.0 + a * (1.0 - s)))).astype(BF)
        grads[base:, f * chunk + hidden : (f + 1) * chunk + hidden] = (d_hidden * silu).astype(BF)
        grads[base:, f * chunk + 2 * hidden : (f + 1) * chunk + 2 * hidden] = (value * p).astype(BF)

    for route, at, out in zip(routes, (0, half), (own_prob, sib_prob)):
        lane = lax.broadcasted_iota(jnp.int32, route.shape, 1)
        out[...] = jnp.where((route == me) & (lane < 3), d_prob[at : at + half], 0.0).astype(BF)

    if count:
        up, down, over, keep = first
        for copy in copies[7:]:
            copy.wait()
        for i in range(count):
            columns = pl.ds(pl.multiple_of(scalars[2 + i] * block, block), block)
            left, right = near_cols.at[2 * i], near_cols.at[2 * i + 1]
            dy = jnp.concatenate([left[:half], right[:half], dy_all[:, columns]], axis=0)
            x = jnp.concatenate([left[half:], right[half:], x_all[:, columns]], axis=0)
            x_turned[i * block : (i + 1) * block, :] = x.T
            dy_turned[i * block : (i + 1) * block, :] = dy.T
        part = block // 2
        places = ((up, 0), (down, 0), (keep, 0), (over, 0), (over, part), (keep, part))
        for k, turned in enumerate((x_turned, x_turned, dy_turned)):
            at = slice(k * hidden, (k + 1) * hidden)
            value = jnp.dot(turned[...], grads[:, at], preferred_element_type=F32).astype(BF)
            for i, (ref, to) in enumerate(places):
                ref[to : to + part, at] = value[i * part : (i + 1) * part]

    chunk = 512
    dims = (((1,), (1,)), ((), ()))
    for n in range(model // chunk):
        at = slice(n * chunk, (n + 1) * chunk)
        rows = lax.dot_general(
            grads[base:, : 2 * hidden], w_all[at, :], dims, preferred_element_type=F32
        ).astype(BF)
        own_row[:, at] = rows[:half]
        sib_row[:, at] = rows[half:]


def expert_rows(scalars, own, rec, own_ex, rec_ex, w_in, w_out, near, name):
    model, hidden = w_out.shape
    rows, block = own.shape[0], model // 8
    count = 0 if near is None else 3
    vmem = pl.BlockSpec(memory_space=pltpu.VMEM)
    total = 2 * rows if count else rows
    out_shape = [shaped(total, 3 * hidden)] + [shaped(rows // 2, model)] * 2 + [shaped(*own_ex.shape)] * 2
    scratch = [
        pltpu.VMEM((rows, model), BF),
        pltpu.VMEM((rows, model), BF),
        pltpu.VMEM((model, 2 * hidden), BF),
        pltpu.VMEM((model, hidden), BF),
        pltpu.VMEM((rows, hidden), F32),
        pltpu.VMEM((rows, hidden), F32),
        pltpu.VMEM((rows, hidden), F32),
        pltpu.SemaphoreType.DMA((8 + 2 * count,)),
    ]
    if count:
        out_shape += [shaped(block // 2, 3 * hidden)] * 2 + [shaped(block, 3 * hidden)] * 2
        scratch += [
            pltpu.VMEM((2 * count, rows, block), BF),
            pltpu.VMEM((count * block, 2 * rows), BF),
            pltpu.VMEM((count * block, 2 * rows), BF),
        ]
    return pl.pallas_call(
        functools.partial(expert_kernel, count),
        in_specs=[smem(), vmem, vmem] + unread(7),
        out_specs=[vmem] * len(out_shape),
        out_shape=out_shape,
        scratch_shapes=scratch,
        cost_estimate=cost(2 * rows * model * 5 * hidden, 2 * model * 3 * hidden + 8 * rows * model),
        compiler_params=params(),
        name=name,
    )(scalars, own_ex, rec_ex, own, rec, w_in, w_out, *(near if count else (own_ex,) * 3))


def unpack_rows(pos_ref, own, rec, own_ex, rec_ex, r):
    hot = both_hot(pos_ref, r)
    dims = (((0,), (0,)), ((), ()))
    values = []
    for a, b in ((own, rec), (own_ex, rec_ex)):
        rows = jnp.concatenate([a[r * CAP : (r + 1) * CAP], b[r * CAP : (r + 1) * CAP]], axis=0)
        values.append(lax.dot_general(hot, rows, dims, preferred_element_type=F32).astype(BF))
    return values


def unpack_near_kernel(pos, own, rec, own_ex, rec_ex, after, out):
    width = own.shape[1]
    for at, r in enumerate((2, 1, 3, 0)):
        main, extra = unpack_rows(pos, own, rec, own_ex, rec_ex, r)
        out[at, :, :width] = main
        out[at, :, width:] = extra


def unpack_far_kernel(pos, own, rec, own_ex, rec_ex, after, up, down, over, keep, second):
    half, width = up.shape[0], own.shape[1]

    def put(ref, at, values, lo, count):
        main, extra = values
        ref[at : at + count, :width] = main[lo : lo + count]
        ref[at : at + count, width:] = extra[lo : lo + count]

    values = unpack_rows(pos, own, rec, own_ex, rec_ex, 3)
    put(up, 0, values, 0, half)
    put(down, 0, values, half, half)
    values = unpack_rows(pos, own, rec, own_ex, rec_ex, 1)
    put(over, half, values, 0, half)
    put(keep, half, values, half, half)
    values = unpack_rows(pos, own, rec, own_ex, rec_ex, 2)
    put(keep, 0, values, 0, half)
    put(over, 0, values, half, half)
    put(second, 0, unpack_rows(pos, own, rec, own_ex, rec_ex, 0), 0, 2 * half)


def unpack(kernel, pos, own, rec, own_ex, rec_ex, after, shapes, name):
    model = own.shape[1]
    vmem = pl.BlockSpec(memory_space=pltpu.VMEM)
    return pl.pallas_call(
        kernel,
        in_specs=[vmem] * 5 + unread(1),
        out_specs=[vmem] * len(shapes),
        out_shape=[shaped(*s) for s in shapes],
        cost_estimate=cost(4 * 2 * 128 * 96 * model, 2 * model * (2 * own.shape[0] + 512)),
        compiler_params=params(),
        name=name,
    )(pos, own, rec, own_ex, rec_ex, after)


def weight_block(all_grads, xs):
    half = xs[0].shape[0] // 2
    dy = jnp.concatenate([ref[:half] for ref in xs], axis=0)
    x = jnp.concatenate([ref[half:] for ref in xs], axis=0)
    wide = 2 * all_grads.shape[1] // 3
    dims = (((0,), (0,)), ((), ()))
    into = lax.dot_general(x, all_grads[:, :wide], dims, preferred_element_type=F32)
    out = lax.dot_general(dy, all_grads[:, wide:], dims, preferred_element_type=F32)
    return into.astype(BF), out.astype(BF)


def weight_rest_kernel(dest, *refs):
    xs, all_grads, block = refs[:4], refs[4], refs[6]
    into, out = weight_block(all_grads, xs)
    wide = into.shape[1]
    block[0, :, :wide] = into
    block[0, :, wide:] = out


def weight_grads(dest, xs, grads, after, name):
    steps = dest.shape[0]
    model = xs[0].shape[1]
    rows, wide = grads.shape
    block = model // 8
    return pl.pallas_call(
        weight_rest_kernel,
        grid_spec=pltpu.PrefetchScalarGridSpec(
            num_scalar_prefetch=1,
            grid=(steps,),
            in_specs=[pl.BlockSpec((x.shape[0], block), lambda i, d: (0, d[i])) for x in xs]
            + [pl.BlockSpec(grads.shape, lambda i, d: (0, 0))]
            + unread(1),
            out_specs=pl.BlockSpec((1, block, wide), lambda i, d: (i, 0, 0)),
        ),
        out_shape=shaped(steps, block, wide),
        cost_estimate=cost(2 * rows * block * wide * steps, 2 * steps * block * (wide + 2 * rows) + 2 * rows * wide),
        compiler_params=params(),
        name=name,
    )(dest, *xs, grads, after)


def added(a, b):
    return a.astype(F32) + b.astype(F32)


def second_kernel(keep, from_minus, from_plus, straight, after, up, down):
    up[0] = added(keep[0], from_minus[...]).astype(BF)
    up[1] = straight[0, 0]
    down[0] = added(keep[1], from_plus[...]).astype(BF)
    down[1] = straight[0, 1]


def second(keep, from_minus, from_plus, blocks, after, part, name):
    rows, width = keep.shape
    half = rows // 2
    count = blocks.shape[0]
    pair = pl.BlockSpec((2, part, width), lambda j: (0, j, 0))
    single = pl.BlockSpec((part, width), lambda j: (j, 0))
    up, down = pl.pallas_call(
        second_kernel,
        grid=(half // part,),
        in_specs=[
            pair,
            single,
            single,
            pl.BlockSpec((1, 2, part, width), lambda j: (count - 1, 0, j, 0)),
            *unread(1),
        ],
        out_specs=[pair] * 2,
        out_shape=[shaped(2, half, width)] * 2,
        cost_estimate=cost(2 * rows * width, 10 * rows * width),
        compiler_params=params(),
        name=name,
    )(halves(keep), from_minus, from_plus, blocks.reshape(count, 2, half, width), after)
    return up.reshape(rows, width), down.reshape(rows, width)


def third_kernel(blocks, from_minus, from_plus, from_over, after, up, down, over):
    up[0] = added(blocks[0, 0], from_minus[1]).astype(BF)
    up[1] = added(blocks[0, 1], from_over[0]).astype(BF)
    down[0] = added(blocks[1, 0], from_over[1]).astype(BF)
    down[1] = added(blocks[1, 1], from_plus[1]).astype(BF)
    over[0] = added(blocks[2, 0], from_minus[0]).astype(BF)
    over[1] = added(blocks[2, 1], from_plus[0]).astype(BF)


def third(blocks, from_minus, from_plus, from_over, after, part, name):
    count, rows, width = blocks.shape
    half = rows // 2
    pair = pl.BlockSpec((2, part, width), lambda j: (0, j, 0))
    outs = pl.pallas_call(
        third_kernel,
        grid=(half // part,),
        in_specs=[pl.BlockSpec((3, 2, part, width), lambda j: (0, 0, j, 0))] + [pair] * 3 + unread(1),
        out_specs=[pair] * 3,
        out_shape=[shaped(2, half, width)] * 3,
        cost_estimate=cost(3 * rows * width, 18 * rows * width),
        compiler_params=params(),
        name=name,
    )(blocks.reshape(count, 2, half, width), halves(from_minus), halves(from_plus), halves(from_over), after)
    return [v.reshape(rows, width) for v in outs]


def last_rows_kernel(block, a, b, c, out, prob):
    total = (added(block[0], a[...]) + added(b[...], c[...])).astype(out.dtype)
    width, routed = out.shape[1], prob.shape[1]
    out[...] = total[:, :width]
    prob[...] = total[:, width : width + routed]


def last_rows(blocks, a, b, c, width, routed):
    count, rows, wide = blocks.shape
    part = 64
    row = lambda w: pl.BlockSpec((part, w), lambda j: (j, 0))
    return pl.pallas_call(
        last_rows_kernel,
        grid=(rows // part,),
        in_specs=[pl.BlockSpec((1, part, wide), lambda j: (3, j, 0))] + [row(wide)] * 3,
        out_specs=[row(width), row(routed)],
        out_shape=[shaped(rows, width), shaped(rows, routed)],
        cost_estimate=cost(3 * rows * wide, 10 * rows * wide),
        compiler_params=params(),
        name="last_rows",
    )(blocks, a, b, c)


def last_weights_kernel(block, a, b, c, into, out):
    total = added(block[0], a[...]) + added(b[...], c[...])
    wide = into.shape[2]
    into[0] = total[:, :wide]
    out[0] = total[:, wide:]


def last_weights(blocks, a, b, c):
    count, rows, width = blocks.shape
    wide, part = 2 * width // 3, 128
    row = pl.BlockSpec((part, width), lambda j: (j, 0))
    return pl.pallas_call(
        last_weights_kernel,
        grid=(rows // part,),
        in_specs=[pl.BlockSpec((1, part, width), lambda j: (3, j, 0))] + [row] * 3,
        out_specs=[
            pl.BlockSpec((1, part, wide), lambda j: (0, j, 0)),
            pl.BlockSpec((1, part, width - wide), lambda j: (0, j, 0)),
        ],
        out_shape=[shaped(1, rows, wide, dtype=F32), shaped(1, rows, width - wide, dtype=F32)],
        cost_estimate=cost(3 * rows * width, 12 * rows * width),
        compiler_params=params(),
        name="last_weights",
    )(blocks, a, b, c)


def body(tokens, grad_out, combine_weights, expert_ids, w_in, w_out):
    me = lax.axis_index("expert")
    group = lax.axis_index("dp")
    gx, gz = group // SIDE, group % SIDE

    def dest(dx, dz):
        return ((gx + dx) % 2) * SIDE + (gz + dz + SIDE) % SIDE

    experts = jnp.stack([me, me + 1 - 2 * (me % 2)]).astype(jnp.int32)
    first = jnp.stack([dest(1, 2), dest(1, 1), dest(1, -1)]).astype(jnp.int32)
    rest = jnp.stack([dest(0, 1), dest(0, -1), dest(1, 0), dest(0, 0), dest(0, 2)]).astype(jnp.int32)
    scalars = jnp.concatenate([experts, first])
    tok_rows, routed = expert_ids.shape
    model = tokens.shape[1]
    w_in_e, w_out_e = w_in[0], w_out[0]
    half = tok_rows // 2

    mine = attach(grad_out, tokens, expert_ids, combine_weights)
    minus, plus, across = expert_move(mine, dy=1), expert_move(mine, dy=-1), expert_move(mine, dx=1)
    cols = model // 4

    def packed(blocks_of, values, after, name):
        return pack(
            blocks_of, experts,
            [(v, fixed(v.shape[0], 128, 2 * model // 128)) for v in values],
            [(v, col(v.shape[0], cols)) for v in values],
            [(v, col(v.shape[0], cols, 4)) for v in values],
            model, after, name,
        )

    own_a, sib_a, own_ex_a, sib_ex_a, pos_a, up, down, over = packed(
        near_blocks, (mine, minus, plus, across), None, "pack_near"
    )
    up2 = expert_move(up, dy=1)
    down2 = expert_move(down, dy=-1)
    over2 = expert_move(over, dx=1)
    rec_a, rec_ex_a = expert_move(sib_a, dc=1), expert_move(sib_ex_a, dc=1)
    grads_a, row_own_a, row_sib_a, prob_a, sib_prob_a = expert_rows(
        scalars, own_a, rec_a, own_ex_a, rec_ex_a, w_in_e, w_out_e, None, "expert_near"
    )
    rec_prob_a = expert_move(sib_prob_a, dc=1)
    row_rec_a = expert_move(row_sib_a, dc=1)

    last_up, last_down = tail(up2, down2, row_own_a)
    last_up2 = expert_move(last_up, dy=1)
    last_down2 = expert_move(last_down, dy=-1)
    wide = model + 128
    near_rows = unpack(
        unpack_near_kernel, pos_a, row_own_a, row_rec_a, prob_a, rec_prob_a, last_up,
        [(4, tok_rows, wide)], "unpack_near",
    )[0]

    own_b, sib_b, own_ex_b, sib_ex_b, pos_b = packed(
        far_blocks, (up2, down2, over2, last_up2, last_down2), near_rows, "pack_far"
    )
    rec_b, rec_ex_b = expert_move(sib_b, dc=1), expert_move(sib_ex_b, dc=1)
    grads, row_own_b, row_sib_b, prob_b, sib_prob_b, w_up, w_down, w_over, w_keep = expert_rows(
        scalars, own_b, rec_b, own_ex_b, rec_ex_b, w_in_e, w_out_e, (grads_a, own_a, rec_a), "expert_far"
    )
    rec_prob_b = expert_move(sib_prob_b, dc=1)
    row_rec_b = expert_move(row_sib_b, dc=1)

    xs = (own_a, rec_a, own_b, rec_b)
    w_up1 = dp_move(w_up, dy=1)
    w_down1 = dp_move(w_down, dy=-1)
    w_over1 = dp_move(w_over, dx=1)
    w_rest = weight_grads(rest, xs, grads, w_keep, "weights_rest")
    w_up, w_down = second(w_keep, w_up1, w_down1, w_rest, w_rest, 64, "second_w")
    w_up2 = dp_move(w_up, dy=1)
    w_down2 = dp_move(w_down, dy=-1)

    r_up, r_down, r_over, r_keep, r_second = unpack(
        unpack_far_kernel, pos_b, row_own_b, row_rec_b, prob_b, rec_prob_b, w_up,
        [(half, wide)] * 2 + [(tok_rows, wide)] * 3, "unpack_far",
    )
    r_up1 = expert_move(r_up, dy=1)
    r_down1 = expert_move(r_down, dy=-1)
    r_over1 = expert_move(r_over, dx=1)
    r_up, r_down = second(r_keep, r_up1, r_down1, r_second[None], w_over1, 64, "second_r")
    r_up2 = expert_move(r_up, dy=1)
    r_down2 = expert_move(r_down, dy=-1)

    w_up, w_down, w_over = third(w_rest, w_up2, w_down2, w_over1, r_over1, 64, "third_w")
    w_up3 = dp_move(w_up, dy=1)
    w_down3 = dp_move(w_down, dy=-1)
    w_over3 = dp_move(w_over, dx=1)

    r_up, r_down, r_over = third(near_rows, r_up2, r_down2, r_over1, w_over, 64, "third_r")
    r_up3 = expert_move(r_up, dy=1)
    r_down3 = expert_move(r_down, dy=-1)
    r_over3 = expert_move(r_over, dx=1)
    d_tokens, d_combine = last_rows(near_rows, r_up3, r_down3, r_over3, model, routed)
    d_w_in, d_w_out = last_weights(w_rest, w_up3, w_down3, w_over3)
    return d_tokens, d_combine, d_w_in, d_w_out


def solution(mesh):
    rows = P(("dp", "expert"), None)
    return jax.shard_map(
        body,
        mesh=mesh,
        in_specs=(rows, rows, rows, rows, P("expert", None, None), P("expert", None, None)),
        out_specs=(rows, rows, P("expert", "dp", None), P("expert", "dp", None)),
        check_vma=False,
    )
```

```python
import functools

import jax
import jax.numpy as jnp
from jax import lax
from jax.experimental import pallas as pl
from jax.experimental.pallas import tpu as pltpu
from jax.sharding import PartitionSpec as P

BF = jnp.bfloat16
F32 = jnp.float32
CAP = 48
SIDE = 4
NEAR = ((0, 0), (0, -1), (0, 1), (1, 0))
FAR = ((0, 2), (1, -1), (1, 1), (1, 2))
VMEM_LIMIT = 58 * 1024 * 1024


def params(**kw):
    return pltpu.CompilerParams(vmem_limit_bytes=VMEM_LIMIT, **kw)


def cost(flops, nbytes):
    return pl.CostEstimate(flops=int(flops) // 10, bytes_accessed=int(nbytes) // 10, transcendentals=0)


def spec(shape, index=None):
    zeros = (0,) * len(shape)
    return pl.BlockSpec(shape, index if index is not None else (lambda *_: zeros))


def smem():
    return pl.BlockSpec(memory_space=pltpu.SMEM)


def unread(count):
    return [pl.BlockSpec(memory_space=pl.ANY)] * count


def col(rows, cols, first=0):
    return pl.BlockSpec((rows, cols), lambda j: (0, j + first))


def fixed(rows, cols, at):
    return pl.BlockSpec((rows, cols), lambda j: (0, at))


def shaped(*shape, dtype=BF):
    return jax.ShapeDtypeStruct(shape, dtype)


def expert_index(x, y, c):
    return (x % 2) * 8 + (y % SIDE) * 2 + c % 2


def expert_move(value, dx=0, dy=0, dc=0):
    pairs = [
        (expert_index(x, y, c), expert_index(x + dx, y + dy, c + dc))
        for x in range(2)
        for y in range(SIDE)
        for c in range(2)
    ]
    return lax.ppermute(value, "expert", pairs)


def dp_move(value, dx=0, dy=0):
    pairs = [
        (x * SIDE + z, ((x + dx) % 2) * SIDE + (z + dy) % SIDE)
        for x in range(2)
        for z in range(SIDE)
    ]
    return lax.ppermute(value, "dp", pairs)


def attach_kernel(grad_out, tokens, ids, weights, out):
    width = tokens.shape[1]
    out[:, :width] = grad_out[...]
    out[:, width : 2 * width] = tokens[...]
    rows, routed = ids.shape[1], ids.shape[0]
    turned = jnp.concatenate(
        [ids[...].astype(F32), weights[...].astype(F32), jnp.zeros((128 - 2 * routed, rows), F32)], axis=0
    )
    out[:, 2 * width :] = turned.T.astype(BF)


def attach(grad_out, tokens, ids, weights):
    rows, width = tokens.shape
    wide = 2 * width + 128
    vmem = pl.BlockSpec(memory_space=pltpu.VMEM)
    return pl.pallas_call(
        attach_kernel,
        in_specs=[vmem] * 4,
        out_specs=vmem,
        out_shape=shaped(rows, wide),
        cost_estimate=cost(0, 4 * rows * wide),
        compiler_params=params(),
        name="attach",
    )(grad_out, tokens, ids.T, weights.T)


def halves(value):
    return value.reshape(2, value.shape[0] // 2, value.shape[1])


def mix_kernel(minus, plus, across, up, down, over):
    up[0] = minus[0]
    up[1] = across[0]
    down[0] = plus[1]
    down[1] = across[1]
    over[0] = plus[0]
    over[1] = minus[1]


def mix(minus, plus, across):
    rows, width = minus.shape
    half, part = rows // 2, 32
    one = pl.BlockSpec((2, part, width), lambda j: (0, j, 0))
    outs = pl.pallas_call(
        mix_kernel,
        grid=(half // part,),
        in_specs=[one] * 3,
        out_specs=[one] * 3,
        out_shape=[shaped(2, half, width)] * 3,
        cost_estimate=cost(0, 6 * minus.size * 2),
        compiler_params=params(),
        name="mix",
    )(halves(minus), halves(plus), halves(across))
    return [v.reshape(rows, width) for v in outs]


def tail_kernel(up, down, after, last_up, last_down):
    last_up[...] = up[0]
    last_down[...] = down[0]


def tail(up, down, after):
    rows, width = up.shape
    half, part = rows // 2, 32
    one = pl.BlockSpec((1, part, width), lambda j: (1, j, 0))
    out = pl.BlockSpec((part, width), lambda j: (j, 0))
    return pl.pallas_call(
        tail_kernel,
        grid=(half // part,),
        in_specs=[one] * 2 + unread(1),
        out_specs=[out] * 2,
        out_shape=[shaped(half, width)] * 2,
        cost_estimate=cost(0, 8 * half * width),
        compiler_params=params(),
        name="tail",
    )(halves(up), halves(down), after)


def slot_one_hot(pos):
    slots = lax.broadcasted_iota(jnp.int32, (CAP, pos.shape[1]), 0).astype(F32)
    return jnp.where(slots == pos, 1.0, 0.0)


def both_hot(pos_ref, r):
    return jnp.concatenate(
        [slot_one_hot(pos_ref[r : r + 1, :]), slot_one_hot(pos_ref[r + 4 : r + 5, :])], axis=0
    ).astype(BF)


def place_slots(experts, routes, pos_ref, hot_ref):
    tokens = routes[0].shape[0]
    turned = [route.astype(F32).T for route in routes]
    rows = []
    for which in range(2):
        expert = experts[which].astype(F32)
        for t in turned:
            hit = (t[0:1] == expert) | (t[1:2] == expert) | (t[2:3] == expert)
            rows.append(jnp.where(hit, 1.0, 0.0))
    hits = jnp.concatenate(rows, axis=0)
    earlier = lax.broadcasted_iota(jnp.int32, (tokens, tokens), 0) < lax.broadcasted_iota(
        jnp.int32, (tokens, tokens), 1
    )
    rank = jnp.dot(hits.astype(BF), jnp.where(earlier, 1.0, 0.0).astype(BF), preferred_element_type=F32)
    pos_ref[...] = jnp.where(hits > 0.5, rank, -1.0)
    for r in range(4):
        hot_ref[r] = both_hot(pos_ref, r)


def pack_rows(hot_ref, blocks, own, sib, columns):
    for r, block in enumerate(blocks):
        rows = jnp.dot(hot_ref[r], block, preferred_element_type=F32).astype(BF)
        own[r * CAP : (r + 1) * CAP, columns] = rows[:CAP]
        sib[r * CAP : (r + 1) * CAP, columns] = rows[CAP:]


def near_blocks(refs):
    return [ref[...] for ref in refs]


def far_blocks(refs):
    up, down, over, last_up, last_down = [ref[...] for ref in refs]
    half = last_up.shape[0]
    return [
        jnp.concatenate([up[:half], down[:half]], axis=0),
        jnp.concatenate([up[half:], over[half:]], axis=0),
        jnp.concatenate([over[:half], down[half:]], axis=0),
        jnp.concatenate([last_up, last_down], axis=0),
    ]


def pack_kernel(blocks_of, count, experts, *refs):
    routes, dys, xs = refs[:count], refs[count : 2 * count], refs[2 * count : 3 * count]
    own_dy, sib_dy, own_x, sib_x, pos, hot = refs[3 * count + 1 :]
    step = pl.program_id(0)
    cols = dys[0].shape[1]

    @pl.when(step == 0)
    def _():
        route = blocks_of(routes)
        place_slots((experts[0], experts[1]), route, pos, hot)
        pack_rows(hot, route, own_x, sib_x, pl.ds(4 * cols, 128))

    pack_rows(hot, blocks_of(dys), own_dy, sib_dy, slice(None))
    pack_rows(hot, blocks_of(xs), own_x, sib_x, pl.ds(pl.multiple_of(step * cols, cols), cols))


def pack(blocks_of, experts, routes, dys, xs, width, after, name):
    operands = [*routes, *dys, *xs]
    rows = 4 * CAP
    tokens = 128
    return pl.pallas_call(
        functools.partial(pack_kernel, blocks_of, len(dys)),
        grid=(4,),
        in_specs=[smem()] + [s for _, s in operands] + unread(1),
        out_specs=[col(rows, width // 4)] * 2 + [spec((rows, width + 128))] * 2 + [spec((8, tokens))],
        out_shape=[shaped(rows, width)] * 2
        + [shaped(rows, width + 128)] * 2
        + [shaped(8, tokens, dtype=F32)],
        scratch_shapes=[pltpu.VMEM((4, 2 * CAP, tokens), BF)],
        cost_estimate=cost(8 * 2 * 96 * 128 * width, 8 * 128 * width * 2 + 8 * rows * width),
        compiler_params=params(),
        name=name,
    )(experts, *[a for a, _ in operands], after)


def expert_kernel(count, scalars, own_dy, rec_dy, own_x, rec_x, w_in, w_out, *refs):
    near, refs = refs[: 5 if count else 1], refs[5 if count else 1 :]
    grads, own_row, sib_row = refs[:3]
    first, refs = refs[3 : 3 + (4 if count else 0)], refs[3 + (4 if count else 0) :]
    x_all, dy_all, w_all, w_out_all, a_all, b_all, g_all, sems = refs[:8]
    half, (model, hidden) = own_dy.shape[0], w_out.shape
    block = model // 8
    base = grads.shape[0] - 2 * half
    me = scalars[0].astype(F32)
    low, high = pl.ds(0, half), pl.ds(half, half)
    gate, up_cols = pl.ds(0, hidden), pl.ds(hidden, hidden)
    moves = [
        (own_x, x_all.at[low]),
        (rec_x, x_all.at[high]),
        (w_in.at[:, gate], w_all.at[:, gate]),
        (w_in.at[:, up_cols], w_all.at[:, up_cols]),
        (own_dy, dy_all.at[low]),
        (rec_dy, dy_all.at[high]),
        (w_out, w_out_all),
    ]
    if count:
        near_grads, near_packed = near[0], near[1:]
        near_cols, x_turned, dy_turned = refs[8:]
        moves.append((near_grads, grads.at[pl.ds(0, base)]))
        for i in range(count):
            columns = pl.ds(pl.multiple_of(scalars[2 + i] * block, block), block)
            for k, value in enumerate(near_packed):
                moves.append((value.at[:, columns], near_cols.at[4 * i + k]))
    copies = [pltpu.make_async_copy(a, b, sems.at[i]) for i, (a, b) in enumerate(moves)]
    for copy in copies:
        copy.start()

    for copy in copies[:2]:
        copy.wait()
    routes = [x_all[rows, model:].astype(F32) for rows in (slice(0, half), slice(half, 2 * half))]
    weights = []
    for route in routes:
        weight = jnp.zeros((half, 1), F32)
        for k in range(3):
            weight += jnp.where(route[:, k : k + 1] == me, route[:, 3 + k : 4 + k], 0.0)
        weights.append(weight)
    p = jnp.concatenate(weights, axis=0)

    copies[2].wait()
    a_all[...] = jnp.dot(x_all[:, :model], w_all[:, :hidden], preferred_element_type=F32)
    copies[3].wait()
    b_all[...] = jnp.dot(x_all[:, :model], w_all[:, hidden:], preferred_element_type=F32)
    for copy in copies[4:7]:
        copy.wait()
    g_all[...] = jnp.dot(dy_all[...], w_out_all[...], preferred_element_type=F32)

    d_prob = jnp.zeros((2 * half, 1), F32)
    chunk = 256
    for f in range(hidden // chunk):
        at = slice(f * chunk, (f + 1) * chunk)
        a, b, g = a_all[:, at], b_all[:, at], g_all[:, at]
        s = jax.nn.sigmoid(a)
        silu = a * s
        value = silu * b
        d_prob += jnp.sum(value.astype(BF).astype(F32) * g, axis=1, keepdims=True)
        d_hidden = g * p
        grads[base:, at] = (d_hidden * b * (s * (1.0 + a * (1.0 - s)))).astype(BF)
        grads[base:, f * chunk + hidden : (f + 1) * chunk + hidden] = (d_hidden * silu).astype(BF)
        grads[base:, f * chunk + 2 * hidden : (f + 1) * chunk + 2 * hidden] = (value * p).astype(BF)

    for route, at, out in zip(routes, (0, half), (own_row, sib_row)):
        lane = lax.broadcasted_iota(jnp.int32, route.shape, 1)
        out[:, model:] = jnp.where((route == me) & (lane < 3), d_prob[at : at + half], 0.0).astype(BF)

    if count:
        up, down, over, keep = first
        for copy in copies[7:]:
            copy.wait()
        for i in range(count):
            columns = pl.ds(pl.multiple_of(scalars[2 + i] * block, block), block)
            dy = jnp.concatenate([near_cols[4 * i], near_cols[4 * i + 1], dy_all[:, columns]], axis=0)
            x = jnp.concatenate([near_cols[4 * i + 2], near_cols[4 * i + 3], x_all[:, columns]], axis=0)
            x_turned[i * block : (i + 1) * block, :] = x.T
            dy_turned[i * block : (i + 1) * block, :] = dy.T
        part = block // 2
        places = ((up, 0), (down, 0), (keep, 0), (over, 0), (over, part), (keep, part))
        for k, turned in enumerate((x_turned, x_turned, dy_turned)):
            at = slice(k * hidden, (k + 1) * hidden)
            value = jnp.dot(turned[...], grads[:, at], preferred_element_type=F32).astype(BF)
            for i, (ref, to) in enumerate(places):
                ref[to : to + part, at] = value[i * part : (i + 1) * part]

    chunk = 512
    dims = (((1,), (1,)), ((), ()))
    for n in range(model // chunk):
        at = slice(n * chunk, (n + 1) * chunk)
        rows = lax.dot_general(
            grads[base:, : 2 * hidden], w_all[at, :], dims, preferred_element_type=F32
        ).astype(BF)
        own_row[:, at] = rows[:half]
        sib_row[:, at] = rows[half:]


def expert_rows(scalars, packed, w_in, w_out, near, name):
    model, hidden = w_out.shape
    rows, block = 2 * packed[0].shape[0], model // 8
    count = 3 if len(near) > 1 else 0
    vmem = pl.BlockSpec(memory_space=pltpu.VMEM)
    total = 2 * rows if count else rows
    out_shape = [shaped(total, 3 * hidden)] + [shaped(rows // 2, model + 128)] * 2
    scratch = [
        pltpu.VMEM((rows, model + 128), BF),
        pltpu.VMEM((rows, model), BF),
        pltpu.VMEM((model, 2 * hidden), BF),
        pltpu.VMEM((model, hidden), BF),
        pltpu.VMEM((rows, hidden), F32),
        pltpu.VMEM((rows, hidden), F32),
        pltpu.VMEM((rows, hidden), F32),
        pltpu.SemaphoreType.DMA((8 + 4 * count,)),
    ]
    if count:
        out_shape += [shaped(block // 2, 3 * hidden)] * 2 + [shaped(block, 3 * hidden)] * 2
        scratch += [
            pltpu.VMEM((4 * count, rows // 2, block), BF),
            pltpu.VMEM((count * block, 2 * rows), BF),
            pltpu.VMEM((count * block, 2 * rows), BF),
        ]
    return pl.pallas_call(
        functools.partial(expert_kernel, count),
        in_specs=[smem()] + unread(6 + len(near)),
        out_specs=[vmem] * len(out_shape),
        out_shape=out_shape,
        scratch_shapes=scratch,
        cost_estimate=cost(2 * rows * model * 5 * hidden, 2 * model * 3 * hidden + 8 * rows * model),
        compiler_params=params(),
        name=name,
    )(scalars, *packed, w_in, w_out, *near)


def unpack_kernel(dest, pos, own, rec, *refs):
    out = refs[-1]
    step = pl.program_id(0)
    hot = jnp.concatenate(
        [slot_one_hot(pos[pl.ds(step, 1), :]), slot_one_hot(pos[pl.ds(step + 4, 1), :])], axis=0
    ).astype(BF)
    rows = jnp.concatenate([own[...], rec[...]], axis=0)
    dims = (((0,), (0,)), ((), ()))
    out[0] = lax.dot_general(hot, rows, dims, preferred_element_type=F32).astype(BF)


def unpack(dest, pos, own, rec, after, into, name):
    wide = own.shape[1]
    tokens = pos.shape[1]
    packed = pl.BlockSpec((CAP, wide), lambda i, d: (i, 0))
    extra = [after] + ([] if into is None else [into])
    return pl.pallas_call(
        unpack_kernel,
        grid_spec=pltpu.PrefetchScalarGridSpec(
            num_scalar_prefetch=1,
            grid=(4,),
            in_specs=[pl.BlockSpec(pos.shape, lambda i, d: (0, 0)), packed, packed, *unread(len(extra))],
            out_specs=pl.BlockSpec((1, tokens, wide), lambda i, d: (d[i], 0, 0)),
        ),
        out_shape=shaped(8, tokens, wide),
        input_output_aliases={} if into is None else {5: 0},
        cost_estimate=cost(4 * 2 * 128 * 96 * wide, 2 * wide * (2 * own.shape[0] + 512)),
        compiler_params=params(),
        name=name,
    )(dest, pos, own, rec, *extra)


def weight_block(all_grads, xs):
    dy = jnp.concatenate([ref[...] for ref in xs[:4]], axis=0)
    x = jnp.concatenate([ref[...] for ref in xs[4:]], axis=0)
    wide = 2 * all_grads.shape[1] // 3
    dims = (((0,), (0,)), ((), ()))
    into = lax.dot_general(x, all_grads[:, :wide], dims, preferred_element_type=F32)
    out = lax.dot_general(dy, all_grads[:, wide:], dims, preferred_element_type=F32)
    return into.astype(BF), out.astype(BF)


def weight_rest_kernel(dest, *refs):
    xs, all_grads, block = refs[:8], refs[8], refs[11]
    into, out = weight_block(all_grads, xs)
    wide = into.shape[1]
    block[0, :, :wide] = into
    block[0, :, wide:] = out


def weight_grads(dest, xs, grads, after, after_too, name):
    steps = dest.shape[0]
    model = xs[0].shape[1]
    rows, wide = grads.shape
    block = model // 8
    return pl.pallas_call(
        weight_rest_kernel,
        grid_spec=pltpu.PrefetchScalarGridSpec(
            num_scalar_prefetch=1,
            grid=(steps,),
            in_specs=[pl.BlockSpec((x.shape[0], block), lambda i, d: (0, d[i])) for x in xs]
            + [pl.BlockSpec(grads.shape, lambda i, d: (0, 0))]
            + unread(2),
            out_specs=pl.BlockSpec((1, block, wide), lambda i, d: (i, 0, 0)),
        ),
        out_shape=shaped(steps, block, wide),
        cost_estimate=cost(2 * rows * block * wide * steps, 2 * steps * block * (wide + 2 * rows) + 2 * rows * wide),
        compiler_params=params(),
        name=name,
    )(dest, *xs, grads, after, after_too)


def added(a, b):
    return a.astype(F32) + b.astype(F32)


def second_kernel(keep, from_minus, from_plus, straight, after, up, down):
    up[0] = added(keep[0], from_minus[...]).astype(BF)
    up[1] = straight[0, 0]
    down[0] = added(keep[1], from_plus[...]).astype(BF)
    down[1] = straight[0, 1]


def second(keep, from_minus, from_plus, blocks, after, part, name):
    rows, width = keep.shape
    half = rows // 2
    count = blocks.shape[0]
    pair = pl.BlockSpec((2, part, width), lambda j: (0, j, 0))
    single = pl.BlockSpec((part, width), lambda j: (j, 0))
    up, down = pl.pallas_call(
        second_kernel,
        grid=(half // part,),
        in_specs=[
            pair,
            single,
            single,
            pl.BlockSpec((1, 2, part, width), lambda j: (count - 1, 0, j, 0)),
            *unread(1),
        ],
        out_specs=[pair] * 2,
        out_shape=[shaped(2, half, width)] * 2,
        cost_estimate=cost(2 * rows * width, 10 * rows * width),
        compiler_params=params(),
        name=name,
    )(halves(keep), from_minus, from_plus, blocks.reshape(count, 2, half, width), after)
    return up.reshape(rows, width), down.reshape(rows, width)


def third_kernel(blocks, from_minus, from_plus, from_over, after, up, down, over):
    up[0] = added(blocks[0, 0], from_minus[1]).astype(BF)
    up[1] = added(blocks[0, 1], from_over[0]).astype(BF)
    down[0] = added(blocks[1, 0], from_over[1]).astype(BF)
    down[1] = added(blocks[1, 1], from_plus[1]).astype(BF)
    over[0] = added(blocks[2, 0], from_minus[0]).astype(BF)
    over[1] = added(blocks[2, 1], from_plus[0]).astype(BF)


def third(blocks, from_minus, from_plus, from_over, after, part, name):
    count, rows, width = blocks.shape
    half = rows // 2
    pair = pl.BlockSpec((2, part, width), lambda j: (0, j, 0))
    outs = pl.pallas_call(
        third_kernel,
        grid=(half // part,),
        in_specs=[pl.BlockSpec((3, 2, part, width), lambda j: (0, 0, j, 0))] + [pair] * 3 + unread(1),
        out_specs=[pair] * 3,
        out_shape=[shaped(2, half, width)] * 3,
        cost_estimate=cost(1e13, 18 * rows * width),
        compiler_params=params(),
        name=name,
    )(blocks.reshape(count, 2, half, width), halves(from_minus), halves(from_plus), halves(from_over), after)
    return [v.reshape(rows, width) for v in outs]


def last_rows_kernel(total, out, prob):
    width, routed = out.shape[1], prob.shape[1]
    out[...] = total[:, :width]
    prob[...] = total[:, width : width + routed]


def last_rows(total, width, routed):
    rows = total.shape[0]
    vmem = pl.BlockSpec(memory_space=pltpu.VMEM)
    return pl.pallas_call(
        last_rows_kernel,
        in_specs=[vmem],
        out_specs=[vmem] * 2,
        out_shape=[shaped(rows, width), shaped(rows, routed)],
        cost_estimate=cost(0, 4 * rows * width),
        compiler_params=params(),
        name="last_rows",
    )(total)


def last_weights_kernel(block, a, b, c, after, into, out):
    total = added(block[0], a[...]) + added(b[...], c[...])
    wide = into.shape[2]
    into[0] = total[:, :wide]
    out[0] = total[:, wide:]


def last_weights(blocks, a, b, c, after):
    count, rows, width = blocks.shape
    wide, part = 2 * width // 3, 128
    row = pl.BlockSpec((part, width), lambda j: (j, 0))
    return pl.pallas_call(
        last_weights_kernel,
        grid=(rows // part,),
        in_specs=[pl.BlockSpec((1, part, width), lambda j: (3, j, 0))] + [row] * 3 + unread(1),
        out_specs=[
            pl.BlockSpec((1, part, wide), lambda j: (0, j, 0)),
            pl.BlockSpec((1, part, width - wide), lambda j: (0, j, 0)),
        ],
        out_shape=[shaped(1, rows, wide, dtype=F32), shaped(1, rows, width - wide, dtype=F32)],
        cost_estimate=cost(3 * rows * width, 12 * rows * width),
        compiler_params=params(),
        name="last_weights",
    )(blocks, a, b, c, after)


def body(tokens, grad_out, combine_weights, expert_ids, w_in, w_out):
    me = lax.axis_index("expert")
    group = lax.axis_index("dp")
    gx, gz = group // SIDE, group % SIDE
    mx, my = me // 8, (me // 2) % SIDE

    def dest(dx, dz):
        return ((gx + dx) % 2) * SIDE + (gz + dz + SIDE) % SIDE

    experts = jnp.stack([me, me + 1 - 2 * (me % 2)]).astype(jnp.int32)
    first = jnp.stack([dest(1, 2), dest(1, 1), dest(1, -1)]).astype(jnp.int32)
    rest = jnp.stack([dest(0, 1), dest(0, -1), dest(1, 0), dest(0, 0), dest(0, 2)]).astype(jnp.int32)
    scalars = jnp.concatenate([experts, first])
    tok_rows, routed = expert_ids.shape
    model = tokens.shape[1]
    w_in_e, w_out_e = w_in[0], w_out[0]
    half = tok_rows // 2

    mine = attach(grad_out, tokens, expert_ids, combine_weights)
    minus, plus, across = expert_move(mine, dy=1), expert_move(mine, dy=-1), expert_move(mine, dx=1)
    up, down, over = mix(minus, plus, across)
    up2 = expert_move(up, dy=1)
    down2 = expert_move(down, dy=-1)
    over2 = expert_move(over, dx=1)

    cols = model // 4

    def packed(blocks_of, values, after, name):
        return pack(
            blocks_of, experts,
            [(v, fixed(v.shape[0], 128, 2 * model // 128)) for v in values],
            [(v, col(v.shape[0], cols)) for v in values],
            [(v, col(v.shape[0], cols, 4)) for v in values],
            model, after, name,
        )

    own_dy_a, sib_dy_a, own_x_a, sib_x_a, pos_a = packed(
        near_blocks, (mine, minus, plus, across), over, "pack_near"
    )
    rec_dy_a, rec_x_a = expert_move(sib_dy_a, dc=1), expert_move(sib_x_a, dc=1)
    near_packed = (own_dy_a, rec_dy_a, own_x_a, rec_x_a)

    last_up, last_down = tail(up2, down2, own_x_a)
    last_up2 = expert_move(last_up, dy=1)
    last_down2 = expert_move(last_down, dy=-1)

    grads_a, row_own_a, row_sib_a = expert_rows(
        scalars, near_packed, w_in_e, w_out_e, (last_up,), "expert_near"
    )
    row_rec_a = expert_move(row_sib_a, dc=1)

    own_dy_b, sib_dy_b, own_x_b, sib_x_b, pos_b = packed(
        far_blocks, (up2, down2, over2, last_up2, last_down2), grads_a, "pack_far"
    )
    rec_dy_b, rec_x_b = expert_move(sib_dy_b, dc=1), expert_move(sib_x_b, dc=1)
    far_packed = (own_dy_b, rec_dy_b, own_x_b, rec_x_b)
    grads, row_own_b, row_sib_b, w_up, w_down, w_over, w_keep = expert_rows(
        scalars, far_packed, w_in_e, w_out_e, (grads_a, *near_packed), "expert_far"
    )
    row_rec_b = expert_move(row_sib_b, dc=1)

    xs = (*near_packed[:2], *far_packed[:2], *near_packed[2:], *far_packed[2:])
    w_up1 = dp_move(w_up, dy=1)
    w_down1 = dp_move(w_down, dy=-1)
    w_over1 = dp_move(w_over, dx=1)
    straight = weight_grads(rest[4:], xs, grads, w_keep, w_keep, "weights_straight")

    w_up, w_down = second(w_keep, w_up1, w_down1, straight, straight, 64, "second_w")
    w_up2 = dp_move(w_up, dy=1)
    w_down2 = dp_move(w_down, dy=-1)

    near_dest, far_dest = [
        jnp.stack([((mx + dx) % 2) * SIDE + (my + dy + SIDE) % SIDE for dx, dy in offsets]).astype(jnp.int32)
        for offsets in (NEAR, FAR)
    ]
    rows = unpack(near_dest, pos_a, row_own_a, row_rec_a, w_up, None, "unpack_near")
    rows = unpack(far_dest, pos_b, row_own_b, row_rec_b, w_up, rows, "unpack_far")
    same_core = [[2 * i + c for i in range(8)] for c in range(2)]
    row_total = lax.psum_scatter(
        rows.reshape(8 * tok_rows, model + 128),
        "expert",
        scatter_dimension=0,
        axis_index_groups=same_core,
        tiled=True,
    )
    w_rest = weight_grads(rest[:4], xs, grads, rows, rows, "weights_rest")
    w_up, w_down, w_over = third(w_rest, w_up2, w_down2, w_over1, w_rest, 64, "third_w")
    w_up3 = dp_move(w_up, dy=1)
    w_down3 = dp_move(w_down, dy=-1)
    w_over3 = dp_move(w_over, dx=1)
    d_tokens, d_combine = last_rows(row_total, model, routed)
    d_w_in, d_w_out = last_weights(w_rest, w_up3, w_down3, w_over3, d_tokens)
    return d_tokens, d_combine, d_w_in, d_w_out


def solution(mesh):
    rows = P(("dp", "expert"), None)
    return jax.shard_map(
        body,
        mesh=mesh,
        in_specs=(rows, rows, rows, rows, P("expert", None, None), P("expert", None, None)),
        out_specs=(rows, rows, P("expert", "dp", None), P("expert", "dp", None)),
        check_vma=False,
    )
```

```python
import functools

import jax
import jax.numpy as jnp
from jax import lax
from jax.experimental import pallas as pl
from jax.experimental.pallas import tpu as pltpu
from jax.sharding import PartitionSpec as P

BF = jnp.bfloat16
F32 = jnp.float32
CAP = 48
SIDE = 4
VMEM_LIMIT = 58 * 1024 * 1024


def params(**kw):
    return pltpu.CompilerParams(vmem_limit_bytes=VMEM_LIMIT, **kw)


def cost(flops, nbytes):
    return pl.CostEstimate(flops=int(flops) // 10, bytes_accessed=int(nbytes) // 10, transcendentals=0)


def spec(shape, index=None):
    zeros = (0,) * len(shape)
    return pl.BlockSpec(shape, index if index is not None else (lambda *_: zeros))


def smem():
    return pl.BlockSpec(memory_space=pltpu.SMEM)


def unread(count):
    return [pl.BlockSpec(memory_space=pl.ANY)] * count


def col(rows, cols, first=0):
    return pl.BlockSpec((rows, cols), lambda j: (0, j + first))


def fixed(rows, cols, at):
    return pl.BlockSpec((rows, cols), lambda j: (0, at))


def shaped(*shape, dtype=BF):
    return jax.ShapeDtypeStruct(shape, dtype)


def expert_index(x, y, c):
    return (x % 2) * 8 + (y % SIDE) * 2 + c % 2


def expert_move(value, dx=0, dy=0, dc=0):
    pairs = [
        (expert_index(x, y, c), expert_index(x + dx, y + dy, c + dc))
        for x in range(2)
        for y in range(SIDE)
        for c in range(2)
    ]
    return lax.ppermute(value, "expert", pairs)


def dp_move(value, dx=0, dy=0):
    pairs = [
        (x * SIDE + z, ((x + dx) % 2) * SIDE + (z + dy) % SIDE)
        for x in range(2)
        for z in range(SIDE)
    ]
    return lax.ppermute(value, "dp", pairs)


def attach_kernel(grad_out, tokens, ids, weights, out):
    width = tokens.shape[1]
    out[:, :width] = grad_out[...]
    out[:, width : 2 * width] = tokens[...]
    rows, routed = ids.shape[1], ids.shape[0]
    turned = jnp.concatenate(
        [ids[...].astype(F32), weights[...].astype(F32), jnp.zeros((128 - 2 * routed, rows), F32)], axis=0
    )
    out[:, 2 * width :] = turned.T.astype(BF)


def attach(grad_out, tokens, ids, weights):
    rows, width = tokens.shape
    wide = 2 * width + 128
    vmem = pl.BlockSpec(memory_space=pltpu.VMEM)
    return pl.pallas_call(
        attach_kernel,
        in_specs=[vmem] * 4,
        out_specs=vmem,
        out_shape=shaped(rows, wide),
        cost_estimate=cost(0, 4 * rows * wide),
        compiler_params=params(),
        name="attach",
    )(grad_out, tokens, ids.T, weights.T)


def halves(value):
    return value.reshape(2, value.shape[0] // 2, value.shape[1])


def mix_kernel(minus, plus, across, up, down, over):
    up[0] = minus[0]
    up[1] = across[0]
    down[0] = plus[1]
    down[1] = across[1]
    over[0] = plus[0]
    over[1] = minus[1]


def mix(minus, plus, across):
    rows, width = minus.shape
    half, part = rows // 2, 32
    one = pl.BlockSpec((2, part, width), lambda j: (0, j, 0))
    outs = pl.pallas_call(
        mix_kernel,
        grid=(half // part,),
        in_specs=[one] * 3,
        out_specs=[one] * 3,
        out_shape=[shaped(2, half, width)] * 3,
        cost_estimate=cost(0, 6 * minus.size * 2),
        compiler_params=params(),
        name="mix",
    )(halves(minus), halves(plus), halves(across))
    return [v.reshape(rows, width) for v in outs]


def tail_kernel(up, down, after, last_up, last_down):
    last_up[...] = up[0]
    last_down[...] = down[0]


def tail(up, down, after):
    rows, width = up.shape
    half, part = rows // 2, 32
    one = pl.BlockSpec((1, part, width), lambda j: (1, j, 0))
    out = pl.BlockSpec((part, width), lambda j: (j, 0))
    return pl.pallas_call(
        tail_kernel,
        grid=(half // part,),
        in_specs=[one] * 2 + unread(1),
        out_specs=[out] * 2,
        out_shape=[shaped(half, width)] * 2,
        cost_estimate=cost(0, 8 * half * width),
        compiler_params=params(),
        name="tail",
    )(halves(up), halves(down), after)


def slot_one_hot(pos):
    slots = lax.broadcasted_iota(jnp.int32, (CAP, pos.shape[1]), 0).astype(F32)
    return jnp.where(slots == pos, 1.0, 0.0)


def both_hot(pos_ref, r):
    return jnp.concatenate(
        [slot_one_hot(pos_ref[r : r + 1, :]), slot_one_hot(pos_ref[r + 4 : r + 5, :])], axis=0
    ).astype(BF)


def place_slots(experts, routes, pos_ref, hot_ref):
    tokens = routes[0].shape[0]
    turned = [route.astype(F32).T for route in routes]
    rows = []
    for which in range(2):
        expert = experts[which].astype(F32)
        for t in turned:
            hit = (t[0:1] == expert) | (t[1:2] == expert) | (t[2:3] == expert)
            rows.append(jnp.where(hit, 1.0, 0.0))
    hits = jnp.concatenate(rows, axis=0)
    earlier = lax.broadcasted_iota(jnp.int32, (tokens, tokens), 0) < lax.broadcasted_iota(
        jnp.int32, (tokens, tokens), 1
    )
    rank = jnp.dot(hits.astype(BF), jnp.where(earlier, 1.0, 0.0).astype(BF), preferred_element_type=F32)
    pos_ref[...] = jnp.where(hits > 0.5, rank, -1.0)
    for r in range(4):
        hot_ref[r] = both_hot(pos_ref, r)


def pack_rows(hot_ref, blocks, own, sib, columns):
    for r, block in enumerate(blocks):
        rows = jnp.dot(hot_ref[r], block, preferred_element_type=F32).astype(BF)
        own[r * CAP : (r + 1) * CAP, columns] = rows[:CAP]
        sib[r * CAP : (r + 1) * CAP, columns] = rows[CAP:]


def near_blocks(refs):
    return [ref[...] for ref in refs]


def far_blocks(refs):
    up, down, over, last_up, last_down = [ref[...] for ref in refs]
    half = last_up.shape[0]
    return [
        jnp.concatenate([up[:half], down[:half]], axis=0),
        jnp.concatenate([up[half:], over[half:]], axis=0),
        jnp.concatenate([over[:half], down[half:]], axis=0),
        jnp.concatenate([last_up, last_down], axis=0),
    ]


def pack_kernel(blocks_of, count, experts, *refs):
    routes, dys, xs = refs[:count], refs[count : 2 * count], refs[2 * count : 3 * count]
    own_dy, sib_dy, own_x, sib_x, pos, hot = refs[3 * count + 1 :]
    step = pl.program_id(0)
    cols = dys[0].shape[1]

    @pl.when(step == 0)
    def _():
        route = blocks_of(routes)
        place_slots((experts[0], experts[1]), route, pos, hot)
        pack_rows(hot, route, own_x, sib_x, pl.ds(4 * cols, 128))

    pack_rows(hot, blocks_of(dys), own_dy, sib_dy, slice(None))
    pack_rows(hot, blocks_of(xs), own_x, sib_x, pl.ds(pl.multiple_of(step * cols, cols), cols))


def pack(blocks_of, experts, routes, dys, xs, width, after, name):
    operands = [*routes, *dys, *xs]
    rows = 4 * CAP
    tokens = 128
    return pl.pallas_call(
        functools.partial(pack_kernel, blocks_of, len(dys)),
        grid=(4,),
        in_specs=[smem()] + [s for _, s in operands] + unread(1),
        out_specs=[col(rows, width // 4)] * 2 + [spec((rows, width + 128))] * 2 + [spec((8, tokens))],
        out_shape=[shaped(rows, width)] * 2
        + [shaped(rows, width + 128)] * 2
        + [shaped(8, tokens, dtype=F32)],
        scratch_shapes=[pltpu.VMEM((4, 2 * CAP, tokens), BF)],
        cost_estimate=cost(8 * 2 * 96 * 128 * width, 8 * 128 * width * 2 + 8 * rows * width),
        compiler_params=params(),
        name=name,
    )(experts, *[a for a, _ in operands], after)


def expert_kernel(count, scalars, own_dy, rec_dy, own_x, rec_x, w_in, w_out, *refs):
    near, refs = refs[: 5 if count else 1], refs[5 if count else 1 :]
    grads, own_row, sib_row = refs[:3]
    first, refs = refs[3 : 3 + (4 if count else 0)], refs[3 + (4 if count else 0) :]
    x_all, dy_all, w_all, w_out_all, a_all, b_all, g_all, sems = refs[:8]
    half, (model, hidden) = own_dy.shape[0], w_out.shape
    block = model // 8
    base = grads.shape[0] - 2 * half
    me = scalars[0].astype(F32)
    low, high = pl.ds(0, half), pl.ds(half, half)
    gate, up_cols = pl.ds(0, hidden), pl.ds(hidden, hidden)
    moves = [
        (own_x, x_all.at[low]),
        (rec_x, x_all.at[high]),
        (w_in.at[:, gate], w_all.at[:, gate]),
        (w_in.at[:, up_cols], w_all.at[:, up_cols]),
        (own_dy, dy_all.at[low]),
        (rec_dy, dy_all.at[high]),
        (w_out, w_out_all),
    ]
    if count:
        near_grads, near_packed = near[0], near[1:]
        near_cols, x_turned, dy_turned = refs[8:]
        moves.append((near_grads, grads.at[pl.ds(0, base)]))
        for i in range(count):
            columns = pl.ds(pl.multiple_of(scalars[2 + i] * block, block), block)
            for k, value in enumerate(near_packed):
                moves.append((value.at[:, columns], near_cols.at[4 * i + k]))
    copies = [pltpu.make_async_copy(a, b, sems.at[i]) for i, (a, b) in enumerate(moves)]
    for copy in copies:
        copy.start()

    for copy in copies[:2]:
        copy.wait()
    routes = [x_all[rows, model:].astype(F32) for rows in (slice(0, half), slice(half, 2 * half))]
    weights = []
    for route in routes:
        weight = jnp.zeros((half, 1), F32)
        for k in range(3):
            weight += jnp.where(route[:, k : k + 1] == me, route[:, 3 + k : 4 + k], 0.0)
        weights.append(weight)
    p = jnp.concatenate(weights, axis=0)

    copies[2].wait()
    a_all[...] = jnp.dot(x_all[:, :model], w_all[:, :hidden], preferred_element_type=F32)
    copies[3].wait()
    b_all[...] = jnp.dot(x_all[:, :model], w_all[:, hidden:], preferred_element_type=F32)
    for copy in copies[4:7]:
        copy.wait()
    g_all[...] = jnp.dot(dy_all[...], w_out_all[...], preferred_element_type=F32)

    d_prob = jnp.zeros((2 * half, 1), F32)
    chunk = 256
    for f in range(hidden // chunk):
        at = slice(f * chunk, (f + 1) * chunk)
        a, b, g = a_all[:, at], b_all[:, at], g_all[:, at]
        s = jax.nn.sigmoid(a)
        silu = a * s
        value = silu * b
        d_prob += jnp.sum(value.astype(BF).astype(F32) * g, axis=1, keepdims=True)
        d_hidden = g * p
        grads[base:, at] = (d_hidden * b * (s * (1.0 + a * (1.0 - s)))).astype(BF)
        grads[base:, f * chunk + hidden : (f + 1) * chunk + hidden] = (d_hidden * silu).astype(BF)
        grads[base:, f * chunk + 2 * hidden : (f + 1) * chunk + 2 * hidden] = (value * p).astype(BF)

    for route, at, out in zip(routes, (0, half), (own_row, sib_row)):
        lane = lax.broadcasted_iota(jnp.int32, route.shape, 1)
        out[:, model:] = jnp.where((route == me) & (lane < 3), d_prob[at : at + half], 0.0).astype(BF)

    if count:
        up, down, over, keep = first
        for copy in copies[7:]:
            copy.wait()
        for i in range(count):
            columns = pl.ds(pl.multiple_of(scalars[2 + i] * block, block), block)
            dy = jnp.concatenate([near_cols[4 * i], near_cols[4 * i + 1], dy_all[:, columns]], axis=0)
            x = jnp.concatenate([near_cols[4 * i + 2], near_cols[4 * i + 3], x_all[:, columns]], axis=0)
            x_turned[i * block : (i + 1) * block, :] = x.T
            dy_turned[i * block : (i + 1) * block, :] = dy.T
        part = block // 2
        places = ((up, 0), (down, 0), (keep, 0), (over, 0), (over, part), (keep, part))
        for k, turned in enumerate((x_turned, x_turned, dy_turned)):
            at = slice(k * hidden, (k + 1) * hidden)
            value = jnp.dot(turned[...], grads[:, at], preferred_element_type=F32).astype(BF)
            for i, (ref, to) in enumerate(places):
                ref[to : to + part, at] = value[i * part : (i + 1) * part]

    chunk = 512
    dims = (((1,), (1,)), ((), ()))
    for n in range(model // chunk):
        at = slice(n * chunk, (n + 1) * chunk)
        rows = lax.dot_general(
            grads[base:, : 2 * hidden], w_all[at, :], dims, preferred_element_type=F32
        ).astype(BF)
        own_row[:, at] = rows[:half]
        sib_row[:, at] = rows[half:]


def expert_rows(scalars, packed, w_in, w_out, near, name):
    model, hidden = w_out.shape
    rows, block = 2 * packed[0].shape[0], model // 8
    count = 3 if len(near) > 1 else 0
    vmem = pl.BlockSpec(memory_space=pltpu.VMEM)
    total = 2 * rows if count else rows
    out_shape = [shaped(total, 3 * hidden)] + [shaped(rows // 2, model + 128)] * 2
    scratch = [
        pltpu.VMEM((rows, model + 128), BF),
        pltpu.VMEM((rows, model), BF),
        pltpu.VMEM((model, 2 * hidden), BF),
        pltpu.VMEM((model, hidden), BF),
        pltpu.VMEM((rows, hidden), F32),
        pltpu.VMEM((rows, hidden), F32),
        pltpu.VMEM((rows, hidden), F32),
        pltpu.SemaphoreType.DMA((8 + 4 * count,)),
    ]
    if count:
        out_shape += [shaped(block // 2, 3 * hidden)] * 2 + [shaped(block, 3 * hidden)] * 2
        scratch += [
            pltpu.VMEM((4 * count, rows // 2, block), BF),
            pltpu.VMEM((count * block, 2 * rows), BF),
            pltpu.VMEM((count * block, 2 * rows), BF),
        ]
    return pl.pallas_call(
        functools.partial(expert_kernel, count),
        in_specs=[smem()] + unread(6 + len(near)),
        out_specs=[vmem] * len(out_shape),
        out_shape=out_shape,
        scratch_shapes=scratch,
        cost_estimate=cost(2 * rows * model * 5 * hidden, 2 * model * 3 * hidden + 8 * rows * model),
        compiler_params=params(),
        name=name,
    )(scalars, *packed, w_in, w_out, *near)


def unpack_rows(pos_ref, own, rec, r):
    hot = jnp.concatenate(
        [slot_one_hot(pos_ref[r : r + 1, :]), slot_one_hot(pos_ref[r + 4 : r + 5, :])], axis=0
    ).astype(BF)
    rows = jnp.concatenate([own[r * CAP : (r + 1) * CAP], rec[r * CAP : (r + 1) * CAP]], axis=0)
    dims = (((0,), (0,)), ((), ()))
    return lax.dot_general(hot, rows, dims, preferred_element_type=F32).astype(BF)


def unpack_near_kernel(pos, own, rec, after, plus, minus, here, across):
    for r, ref in enumerate((here, minus, plus, across)):
        ref[...] = unpack_rows(pos, own, rec, r)


def unpack_far_kernel(pos, own, rec, after, up, down, across_plus, across_minus):
    half = up.shape[1]
    for i, r in enumerate((0, 3)):
        value = unpack_rows(pos, own, rec, r)
        up[i] = value[:half]
        down[i] = value[half:]
    across_minus[...] = unpack_rows(pos, own, rec, 1)
    across_plus[...] = unpack_rows(pos, own, rec, 2)


def unpack(kernel, pos, own, rec, after, shapes, name):
    wide = own.shape[1]
    vmem = pl.BlockSpec(memory_space=pltpu.VMEM)
    return pl.pallas_call(
        kernel,
        in_specs=[vmem] * 3 + unread(1),
        out_specs=[vmem] * len(shapes),
        out_shape=[shaped(*shape) for shape in shapes],
        cost_estimate=cost(4 * 2 * 128 * 96 * wide, 2 * wide * (2 * own.shape[0] + 512)),
        compiler_params=params(),
        name=name,
    )(pos, own, rec, after)


def weight_block(all_grads, xs):
    dy = jnp.concatenate([ref[...] for ref in xs[:4]], axis=0)
    x = jnp.concatenate([ref[...] for ref in xs[4:]], axis=0)
    wide = 2 * all_grads.shape[1] // 3
    dims = (((0,), (0,)), ((), ()))
    into = lax.dot_general(x, all_grads[:, :wide], dims, preferred_element_type=F32)
    out = lax.dot_general(dy, all_grads[:, wide:], dims, preferred_element_type=F32)
    return into.astype(BF), out.astype(BF)


def weight_rest_kernel(dest, *refs):
    xs, all_grads, block = refs[:8], refs[8], refs[10]
    into, out = weight_block(all_grads, xs)
    wide = into.shape[1]
    block[0, :, :wide] = into
    block[0, :, wide:] = out


def weight_grads(scalars, at, steps, xs, grads, after, name):
    model = xs[0].shape[1]
    rows, wide = grads.shape
    block = model // 8
    return pl.pallas_call(
        weight_rest_kernel,
        grid_spec=pltpu.PrefetchScalarGridSpec(
            num_scalar_prefetch=1,
            grid=(steps,),
            in_specs=[pl.BlockSpec((x.shape[0], block), lambda i, d: (0, d[at + i])) for x in xs]
            + [pl.BlockSpec(grads.shape, lambda i, d: (0, 0))]
            + unread(1),
            out_specs=pl.BlockSpec((1, block, wide), lambda i, d: (i, 0, 0)),
        ),
        out_shape=shaped(steps, block, wide),
        cost_estimate=cost(2 * rows * block * wide * steps, 2 * steps * block * (wide + 2 * rows) + 2 * rows * wide),
        compiler_params=params(),
        name=name,
    )(scalars, *xs, grads, after)


def added(a, b):
    return a.astype(F32) + b.astype(F32)


def second_kernel(keep, from_minus, from_plus, straight, after, up, down):
    up[0] = added(keep[0], from_minus[...]).astype(BF)
    up[1] = straight[0, 0]
    down[0] = added(keep[1], from_plus[...]).astype(BF)
    down[1] = straight[0, 1]


def second(keep, from_minus, from_plus, blocks, after, part, name):
    rows, width = keep.shape
    half = rows // 2
    count = blocks.shape[0]
    pair = pl.BlockSpec((2, part, width), lambda j: (0, j, 0))
    single = pl.BlockSpec((part, width), lambda j: (j, 0))
    up, down = pl.pallas_call(
        second_kernel,
        grid=(half // part,),
        in_specs=[
            pair,
            single,
            single,
            pl.BlockSpec((1, 2, part, width), lambda j: (count - 1, 0, j, 0)),
            *unread(1),
        ],
        out_specs=[pair] * 2,
        out_shape=[shaped(2, half, width)] * 2,
        cost_estimate=cost(2 * rows * width, 10 * rows * width),
        compiler_params=params(),
        name=name,
    )(halves(keep), from_minus, from_plus, blocks.reshape(count, 2, half, width), after)
    return up.reshape(rows, width), down.reshape(rows, width)


def third_kernel(blocks, from_minus, from_plus, from_over, after, up, down, over):
    up[0] = added(blocks[0, 0], from_minus[1]).astype(BF)
    up[1] = added(blocks[0, 1], from_over[0]).astype(BF)
    down[0] = added(blocks[1, 0], from_over[1]).astype(BF)
    down[1] = added(blocks[1, 1], from_plus[1]).astype(BF)
    over[0] = added(blocks[2, 0], from_minus[0]).astype(BF)
    over[1] = added(blocks[2, 1], from_plus[0]).astype(BF)


def third(blocks, from_minus, from_plus, from_over, after, part, name):
    count, rows, width = blocks.shape
    half = rows // 2
    pair = pl.BlockSpec((2, part, width), lambda j: (0, j, 0))
    outs = pl.pallas_call(
        third_kernel,
        grid=(half // part,),
        in_specs=[pl.BlockSpec((3, 2, part, width), lambda j: (0, 0, j, 0))] + [pair] * 3 + unread(1),
        out_specs=[pair] * 3,
        out_shape=[shaped(2, half, width)] * 3,
        cost_estimate=cost(3 * rows * width, 18 * rows * width),
        compiler_params=params(),
        name=name,
    )(blocks.reshape(count, 2, half, width), halves(from_minus), halves(from_plus), halves(from_over), after)
    return [v.reshape(rows, width) for v in outs]


def second_rows_kernel(plus, across_plus, minus, across_minus, from_minus, from_plus, up, down):
    half = from_minus.shape[1]
    for i, (above, below) in enumerate(((plus, minus), (across_plus, across_minus))):
        up[i, :half] = added(above[:half], from_minus[i]).astype(BF)
        up[i, half:] = above[half:]
        down[i, :half] = below[:half]
        down[i, half:] = added(below[half:], from_plus[i]).astype(BF)


def third_rows_kernel(across, from_minus, from_plus, after, out):
    out[...] = (added(from_minus[0], from_plus[0]) + across[...].astype(F32)).astype(BF)


def last_rows_kernel(here, from_minus, from_plus, from_over, out, prob):
    total = (added(here[...], from_minus[0]) + added(from_plus[0], from_over[...])).astype(BF)
    width, routed = out.shape[1], prob.shape[1]
    out[...] = total[:, :width]
    prob[...] = total[:, width : width + routed]


def second_rows(plus, across_plus, minus, across_minus, from_minus, from_plus):
    rows, width = plus.shape
    vmem = pl.BlockSpec(memory_space=pltpu.VMEM)
    return pl.pallas_call(
        second_rows_kernel,
        in_specs=[vmem] * 6,
        out_specs=[vmem] * 2,
        out_shape=[shaped(2, rows, width)] * 2,
        cost_estimate=cost(2 * rows * width, 20 * rows * width),
        compiler_params=params(),
        name="second_rows",
    )(plus, across_plus, minus, across_minus, from_minus, from_plus)


def third_rows(across, from_minus, from_plus, after):
    rows, width = across.shape
    part = rows // 2
    row = pl.BlockSpec((part, width), lambda j: (j, 0))
    other = pl.BlockSpec((1, part, width), lambda j: (1, j, 0))
    return pl.pallas_call(
        third_rows_kernel,
        grid=(2,),
        in_specs=[row, other, other] + unread(1),
        out_specs=row,
        out_shape=shaped(rows, width),
        cost_estimate=cost(2 * rows * width, 8 * rows * width),
        compiler_params=params(),
        name="third_rows",
    )(across, from_minus, from_plus, after)


def last_rows(here, from_minus, from_plus, from_over, width, routed):
    rows, wide = here.shape
    part = rows // 2
    row = lambda w: pl.BlockSpec((part, w), lambda j: (j, 0))
    other = pl.BlockSpec((1, part, wide), lambda j: (0, j, 0))
    return pl.pallas_call(
        last_rows_kernel,
        grid=(2,),
        in_specs=[row(wide), other, other, row(wide)],
        out_specs=[row(width), row(routed)],
        out_shape=[shaped(rows, width), shaped(rows, routed)],
        cost_estimate=cost(3 * rows * wide, 10 * rows * wide),
        compiler_params=params(),
        name="last_rows",
    )(here, from_minus, from_plus, from_over)


def last_weights_kernel(block, a, b, c, after, into, out):
    total = added(block[0], a[...]) + added(b[...], c[...])
    wide = into.shape[2]
    into[0] = total[:, :wide]
    out[0] = total[:, wide:]


def last_weights(blocks, a, b, c, after):
    count, rows, width = blocks.shape
    wide, part = 2 * width // 3, 128
    row = pl.BlockSpec((part, width), lambda j: (j, 0))
    return pl.pallas_call(
        last_weights_kernel,
        grid=(rows // part,),
        in_specs=[pl.BlockSpec((1, part, width), lambda j: (3, j, 0))] + [row] * 3 + unread(1),
        out_specs=[
            pl.BlockSpec((1, part, wide), lambda j: (0, j, 0)),
            pl.BlockSpec((1, part, width - wide), lambda j: (0, j, 0)),
        ],
        out_shape=[shaped(1, rows, wide, dtype=F32), shaped(1, rows, width - wide, dtype=F32)],
        cost_estimate=cost(3 * rows * width, 12 * rows * width),
        compiler_params=params(),
        name="last_weights",
    )(blocks, a, b, c, after)


def body(tokens, grad_out, combine_weights, expert_ids, w_in, w_out):
    me = lax.axis_index("expert")
    group = lax.axis_index("dp")
    gx, gz = group // SIDE, group % SIDE

    def dest(dx, dz):
        return ((gx + dx) % 2) * SIDE + (gz + dz + SIDE) % SIDE

    first = [dest(1, 2), dest(1, 1), dest(1, -1)]
    rest = [dest(0, 1), dest(0, -1), dest(1, 0), dest(0, 0), dest(0, 2)]
    scalars = jnp.stack([me, me + 1 - 2 * (me % 2), *first, *rest]).astype(jnp.int32)
    tok_rows, routed = expert_ids.shape
    model = tokens.shape[1]
    w_in_e, w_out_e = w_in[0], w_out[0]
    half = tok_rows // 2

    mine = attach(grad_out, tokens, expert_ids, combine_weights)
    minus, plus, across = expert_move(mine, dy=1), expert_move(mine, dy=-1), expert_move(mine, dx=1)
    up, down, over = mix(minus, plus, across)
    up2 = expert_move(up, dy=1)
    down2 = expert_move(down, dy=-1)
    over2 = expert_move(over, dx=1)

    cols = model // 4

    def packed(blocks_of, values, after, name):
        return pack(
            blocks_of, scalars,
            [(v, fixed(v.shape[0], 128, 2 * model // 128)) for v in values],
            [(v, col(v.shape[0], cols)) for v in values],
            [(v, col(v.shape[0], cols, 4)) for v in values],
            model, after, name,
        )

    own_dy_a, sib_dy_a, own_x_a, sib_x_a, pos_a = packed(
        near_blocks, (mine, minus, plus, across), over, "pack_near"
    )
    rec_dy_a, rec_x_a = expert_move(sib_dy_a, dc=1), expert_move(sib_x_a, dc=1)
    near_packed = (own_dy_a, rec_dy_a, own_x_a, rec_x_a)

    last_up, last_down = tail(up2, down2, own_x_a)
    last_up2 = expert_move(last_up, dy=1)
    last_down2 = expert_move(last_down, dy=-1)

    grads_a, row_own_a, row_sib_a = expert_rows(
        scalars, near_packed, w_in_e, w_out_e, (last_up,), "expert_near"
    )
    row_rec_a = expert_move(row_sib_a, dc=1)

    own_dy_b, sib_dy_b, own_x_b, sib_x_b, pos_b = packed(
        far_blocks, (up2, down2, over2, last_up2, last_down2), grads_a, "pack_far"
    )
    rec_dy_b, rec_x_b = expert_move(sib_dy_b, dc=1), expert_move(sib_x_b, dc=1)
    far_packed = (own_dy_b, rec_dy_b, own_x_b, rec_x_b)
    grads, row_own_b, row_sib_b, w_up, w_down, w_over, w_keep = expert_rows(
        scalars, far_packed, w_in_e, w_out_e, (grads_a, *near_packed), "expert_far"
    )
    row_rec_b = expert_move(row_sib_b, dc=1)

    xs = (*near_packed[:2], *far_packed[:2], *near_packed[2:], *far_packed[2:])
    w_up1 = dp_move(w_up, dy=1)
    w_down1 = dp_move(w_down, dy=-1)
    w_over1 = dp_move(w_over, dx=1)
    straight = weight_grads(scalars, 9, 1, xs, grads, w_keep, "weights_straight")

    half_pair, block = (2, half, model + 128), (tok_rows, model + 128)
    r_up, r_down, across_plus, across_minus = unpack(
        unpack_far_kernel, pos_b, row_own_b, row_rec_b, straight, [half_pair] * 2 + [block] * 2, "unpack_far"
    )
    r_up1 = expert_move(r_up, dy=1)
    r_down1 = expert_move(r_down, dy=-1)

    w_up, w_down = second(w_keep, w_up1, w_down1, straight, across_plus, 64, "second_w")
    w_up2 = dp_move(w_up, dy=1)
    w_down2 = dp_move(w_down, dy=-1)

    r_plus, r_minus, r_here, r_across = unpack(
        unpack_near_kernel, pos_a, row_own_a, row_rec_a, w_up, [block] * 4, "unpack_near"
    )
    r_up, r_down = second_rows(r_plus, across_plus, r_minus, across_minus, r_up1, r_down1)
    r_up2 = expert_move(r_up, dy=1)
    r_down2 = expert_move(r_down, dy=-1)

    w_rest = weight_grads(scalars, 5, 4, xs, grads, r_up, "weights_rest")
    w_up, w_down, w_over = third(w_rest, w_up2, w_down2, w_over1, w_rest, 64, "third_w")
    w_up3 = dp_move(w_up, dy=1)
    w_down3 = dp_move(w_down, dy=-1)
    w_over3 = dp_move(w_over, dx=1)

    r_over = expert_move(third_rows(r_across, r_up2, r_down2, w_over), dx=1)
    d_tokens, d_combine = last_rows(r_here, r_up2, r_down2, r_over, model, routed)
    d_w_in, d_w_out = last_weights(w_rest, w_up3, w_down3, w_over3, d_tokens)
    return d_tokens, d_combine, d_w_in, d_w_out


def solution(mesh):
    rows = P(("dp", "expert"), None)
    return jax.shard_map(
        body,
        mesh=mesh,
        in_specs=(rows, rows, rows, rows, P("expert", None, None), P("expert", None, None)),
        out_specs=(rows, rows, P("expert", "dp", None), P("expert", "dp", None)),
        check_vma=False,
    )
```

```python
import functools

import jax
import jax.numpy as jnp
from jax import lax
from jax.experimental import pallas as pl
from jax.experimental.pallas import tpu as pltpu
from jax.sharding import PartitionSpec as P

BF = jnp.bfloat16
F32 = jnp.float32
CAP = 48
SIDE = 4
VMEM_LIMIT = 58 * 1024 * 1024


def params(**kw):
    return pltpu.CompilerParams(vmem_limit_bytes=VMEM_LIMIT, **kw)


def cost(flops, nbytes):
    return pl.CostEstimate(flops=int(flops) // 10, bytes_accessed=int(nbytes) // 10, transcendentals=0)


def spec(shape, index=None):
    zeros = (0,) * len(shape)
    return pl.BlockSpec(shape, index if index is not None else (lambda *_: zeros))


def smem():
    return pl.BlockSpec(memory_space=pltpu.SMEM)


def unread(count):
    return [pl.BlockSpec(memory_space=pl.ANY)] * count


def col(rows, cols, first=0):
    return pl.BlockSpec((rows, cols), lambda j: (0, j + first))


def fixed(rows, cols, at):
    return pl.BlockSpec((rows, cols), lambda j: (0, at))


def shaped(*shape, dtype=BF):
    return jax.ShapeDtypeStruct(shape, dtype)


def expert_index(x, y, c):
    return (x % 2) * 8 + (y % SIDE) * 2 + c % 2


def expert_move(value, dx=0, dy=0, dc=0):
    pairs = [
        (expert_index(x, y, c), expert_index(x + dx, y + dy, c + dc))
        for x in range(2)
        for y in range(SIDE)
        for c in range(2)
    ]
    return lax.ppermute(value, "expert", pairs)


def dp_move(value, dx=0, dy=0):
    pairs = [
        (x * SIDE + z, ((x + dx) % 2) * SIDE + (z + dy) % SIDE)
        for x in range(2)
        for z in range(SIDE)
    ]
    return lax.ppermute(value, "dp", pairs)


def attach_kernel(grad_out, tokens, ids, weights, out):
    width = tokens.shape[1]
    out[:, :width] = grad_out[...]
    out[:, width : 2 * width] = tokens[...]
    rows, routed = ids.shape[1], ids.shape[0]
    turned = jnp.concatenate(
        [ids[...].astype(F32), weights[...].astype(F32), jnp.zeros((128 - 2 * routed, rows), F32)], axis=0
    )
    out[:, 2 * width :] = turned.T.astype(BF)


def attach(grad_out, tokens, ids, weights):
    rows, width = tokens.shape
    wide = 2 * width + 128
    vmem = pl.BlockSpec(memory_space=pltpu.VMEM)
    return pl.pallas_call(
        attach_kernel,
        in_specs=[vmem] * 4,
        out_specs=vmem,
        out_shape=shaped(rows, wide),
        cost_estimate=cost(0, 4 * rows * wide),
        compiler_params=params(),
        name="attach",
    )(grad_out, tokens, ids.T, weights.T)


def halves(value):
    return value.reshape(2, value.shape[0] // 2, value.shape[1])


def mix_kernel(minus, plus, across, up, down, over):
    up[0] = minus[0]
    up[1] = across[0]
    down[0] = plus[1]
    down[1] = across[1]
    over[0] = plus[0]
    over[1] = minus[1]


def mix(minus, plus, across):
    rows, width = minus.shape
    half, part = rows // 2, 32
    one = pl.BlockSpec((2, part, width), lambda j: (0, j, 0))
    outs = pl.pallas_call(
        mix_kernel,
        grid=(half // part,),
        in_specs=[one] * 3,
        out_specs=[one] * 3,
        out_shape=[shaped(2, half, width)] * 3,
        cost_estimate=cost(0, 6 * minus.size * 2),
        compiler_params=params(),
        name="mix",
    )(halves(minus), halves(plus), halves(across))
    return [v.reshape(rows, width) for v in outs]


def tail_kernel(up, down, after, last_up, last_down):
    last_up[...] = up[0]
    last_down[...] = down[0]


def tail(up, down, after):
    rows, width = up.shape
    half, part = rows // 2, 32
    one = pl.BlockSpec((1, part, width), lambda j: (1, j, 0))
    out = pl.BlockSpec((part, width), lambda j: (j, 0))
    return pl.pallas_call(
        tail_kernel,
        grid=(half // part,),
        in_specs=[one] * 2 + unread(1),
        out_specs=[out] * 2,
        out_shape=[shaped(half, width)] * 2,
        cost_estimate=cost(0, 8 * half * width),
        compiler_params=params(),
        name="tail",
    )(halves(up), halves(down), after)


def slot_one_hot(pos):
    slots = lax.broadcasted_iota(jnp.int32, (CAP, pos.shape[1]), 0).astype(F32)
    return jnp.where(slots == pos, 1.0, 0.0)


def both_hot(pos_ref, r):
    return jnp.concatenate(
        [slot_one_hot(pos_ref[r : r + 1, :]), slot_one_hot(pos_ref[r + 4 : r + 5, :])], axis=0
    ).astype(BF)


def place_slots(experts, routes, pos_ref, hot_ref):
    tokens = routes[0].shape[0]
    turned = [route.astype(F32).T for route in routes]
    rows = []
    for which in range(2):
        expert = experts[which].astype(F32)
        for t in turned:
            hit = (t[0:1] == expert) | (t[1:2] == expert) | (t[2:3] == expert)
            rows.append(jnp.where(hit, 1.0, 0.0))
    hits = jnp.concatenate(rows, axis=0)
    earlier = lax.broadcasted_iota(jnp.int32, (tokens, tokens), 0) < lax.broadcasted_iota(
        jnp.int32, (tokens, tokens), 1
    )
    rank = jnp.dot(hits.astype(BF), jnp.where(earlier, 1.0, 0.0).astype(BF), preferred_element_type=F32)
    pos_ref[...] = jnp.where(hits > 0.5, rank, -1.0)
    for r in range(4):
        hot_ref[r] = both_hot(pos_ref, r)


def pack_rows(hot_ref, blocks, own, sib, columns):
    for r, block in enumerate(blocks):
        rows = jnp.dot(hot_ref[r], block, preferred_element_type=F32).astype(BF)
        own[r * CAP : (r + 1) * CAP, columns] = rows[:CAP]
        sib[r * CAP : (r + 1) * CAP, columns] = rows[CAP:]


def near_blocks(refs):
    return [ref[...] for ref in refs]


def far_blocks(refs):
    up, down, over, last_up, last_down = [ref[...] for ref in refs]
    half = last_up.shape[0]
    return [
        jnp.concatenate([up[:half], down[:half]], axis=0),
        jnp.concatenate([up[half:], over[half:]], axis=0),
        jnp.concatenate([over[:half], down[half:]], axis=0),
        jnp.concatenate([last_up, last_down], axis=0),
    ]


def pack_kernel(blocks_of, count, experts, *refs):
    routes, dys, xs = refs[:count], refs[count : 2 * count], refs[2 * count : 3 * count]
    own_dy, sib_dy, own_x, sib_x, pos, hot = refs[3 * count + 1 :]
    step = pl.program_id(0)
    cols = dys[0].shape[1]

    @pl.when(step == 0)
    def _():
        route = blocks_of(routes)
        place_slots((experts[0], experts[1]), route, pos, hot)
        pack_rows(hot, route, own_x, sib_x, pl.ds(4 * cols, 128))

    pack_rows(hot, blocks_of(dys), own_dy, sib_dy, slice(None))
    pack_rows(hot, blocks_of(xs), own_x, sib_x, pl.ds(pl.multiple_of(step * cols, cols), cols))


def pack(blocks_of, experts, routes, dys, xs, width, after, name):
    operands = [*routes, *dys, *xs]
    rows = 4 * CAP
    tokens = 128
    return pl.pallas_call(
        functools.partial(pack_kernel, blocks_of, len(dys)),
        grid=(4,),
        in_specs=[smem()] + [s for _, s in operands] + unread(1),
        out_specs=[col(rows, width // 4)] * 2 + [spec((rows, width + 128))] * 2 + [spec((8, tokens))],
        out_shape=[shaped(rows, width)] * 2
        + [shaped(rows, width + 128)] * 2
        + [shaped(8, tokens, dtype=F32)],
        scratch_shapes=[pltpu.VMEM((4, 2 * CAP, tokens), BF)],
        cost_estimate=cost(8 * 2 * 96 * 128 * width, 8 * 128 * width * 2 + 8 * rows * width),
        compiler_params=params(),
        name=name,
    )(experts, *[a for a, _ in operands], after)


def expert_kernel(count, scalars, own_dy, rec_dy, own_x, rec_x, w_in, w_out, *refs):
    near, refs = refs[: 5 if count else 1], refs[5 if count else 1 :]
    grads, own_row, sib_row = refs[:3]
    first, refs = refs[3 : 3 + (5 if count else 0)], refs[3 + (5 if count else 0) :]
    x_all, dy_all, w_all, w_out_all, a_all, b_all, g_all, sems = refs[:8]
    half, (model, hidden) = own_dy.shape[0], w_out.shape
    block = model // 8
    base = grads.shape[0] - 2 * half
    me = scalars[0].astype(F32)
    low, high = pl.ds(0, half), pl.ds(half, half)
    gate, up_cols = pl.ds(0, hidden), pl.ds(hidden, hidden)
    moves = [
        (own_x, x_all.at[low]),
        (rec_x, x_all.at[high]),
        (w_in.at[:, gate], w_all.at[:, gate]),
        (w_in.at[:, up_cols], w_all.at[:, up_cols]),
        (own_dy, dy_all.at[low]),
        (rec_dy, dy_all.at[high]),
        (w_out, w_out_all),
    ]
    if count:
        near_grads, near_packed = near[0], near[1:]
        near_cols, x_turned, dy_turned = refs[8:]
        moves.append((near_grads, grads.at[pl.ds(0, base)]))
        for i in range(count):
            columns = pl.ds(pl.multiple_of(scalars[2 + i] * block, block), block)
            for k, value in enumerate(near_packed):
                moves.append((value.at[:, columns], near_cols.at[4 * i + k]))
    copies = [pltpu.make_async_copy(a, b, sems.at[i]) for i, (a, b) in enumerate(moves)]
    for copy in copies:
        copy.start()

    for copy in copies[:2]:
        copy.wait()
    routes = [x_all[rows, model:].astype(F32) for rows in (slice(0, half), slice(half, 2 * half))]
    weights = []
    for route in routes:
        weight = jnp.zeros((half, 1), F32)
        for k in range(3):
            weight += jnp.where(route[:, k : k + 1] == me, route[:, 3 + k : 4 + k], 0.0)
        weights.append(weight)
    p = jnp.concatenate(weights, axis=0)

    copies[2].wait()
    a_all[...] = jnp.dot(x_all[:, :model], w_all[:, :hidden], preferred_element_type=F32)
    copies[3].wait()
    b_all[...] = jnp.dot(x_all[:, :model], w_all[:, hidden:], preferred_element_type=F32)
    for copy in copies[4:7]:
        copy.wait()
    g_all[...] = jnp.dot(dy_all[...], w_out_all[...], preferred_element_type=F32)

    d_prob = jnp.zeros((2 * half, 1), F32)
    chunk = 256
    for f in range(hidden // chunk):
        at = slice(f * chunk, (f + 1) * chunk)
        a, b, g = a_all[:, at], b_all[:, at], g_all[:, at]
        s = jax.nn.sigmoid(a)
        silu = a * s
        value = silu * b
        d_prob += jnp.sum(value.astype(BF).astype(F32) * g, axis=1, keepdims=True)
        d_hidden = g * p
        grads[base:, at] = (d_hidden * b * (s * (1.0 + a * (1.0 - s)))).astype(BF)
        grads[base:, f * chunk + hidden : (f + 1) * chunk + hidden] = (d_hidden * silu).astype(BF)
        grads[base:, f * chunk + 2 * hidden : (f + 1) * chunk + 2 * hidden] = (value * p).astype(BF)

    for route, at, out in zip(routes, (0, half), (own_row, sib_row)):
        lane = lax.broadcasted_iota(jnp.int32, route.shape, 1)
        out[:, model:] = jnp.where((route == me) & (lane < 3), d_prob[at : at + half], 0.0).astype(BF)

    if count:
        up, down, over, keep, straight = first
        for copy in copies[7:]:
            copy.wait()
        for i in range(count):
            columns = pl.ds(pl.multiple_of(scalars[2 + i] * block, block), block)
            dy = jnp.concatenate([near_cols[4 * i], near_cols[4 * i + 1], dy_all[:, columns]], axis=0)
            x = jnp.concatenate([near_cols[4 * i + 2], near_cols[4 * i + 3], x_all[:, columns]], axis=0)
            x_turned[i * block : (i + 1) * block, :] = x.T
            dy_turned[i * block : (i + 1) * block, :] = dy.T
        part = block // 2
        places = (
            (up, 0), (down, 0), (keep, 0), (over, 0), (over, part), (keep, part), (straight, 0), (straight, part),
        )
        for k, turned in enumerate((x_turned, x_turned, dy_turned)):
            at = slice(k * hidden, (k + 1) * hidden)
            value = jnp.dot(turned[...], grads[:, at], preferred_element_type=F32).astype(BF)
            for i, (ref, to) in enumerate(places):
                ref[to : to + part, at] = value[i * part : (i + 1) * part]

    chunk = 512
    dims = (((1,), (1,)), ((), ()))
    for n in range(model // chunk):
        at = slice(n * chunk, (n + 1) * chunk)
        rows = lax.dot_general(
            grads[base:, : 2 * hidden], w_all[at, :], dims, preferred_element_type=F32
        ).astype(BF)
        own_row[:, at] = rows[:half]
        sib_row[:, at] = rows[half:]


def expert_rows(scalars, packed, w_in, w_out, near, name):
    model, hidden = w_out.shape
    rows, block = 2 * packed[0].shape[0], model // 8
    count = 4 if len(near) > 1 else 0
    vmem = pl.BlockSpec(memory_space=pltpu.VMEM)
    total = 2 * rows if count else rows
    out_shape = [shaped(total, 3 * hidden)] + [shaped(rows // 2, model + 128)] * 2
    scratch = [
        pltpu.VMEM((rows, model + 128), BF),
        pltpu.VMEM((rows, model), BF),
        pltpu.VMEM((model, 2 * hidden), BF),
        pltpu.VMEM((model, hidden), BF),
        pltpu.VMEM((rows, hidden), F32),
        pltpu.VMEM((rows, hidden), F32),
        pltpu.VMEM((rows, hidden), F32),
        pltpu.SemaphoreType.DMA((8 + 4 * count,)),
    ]
    if count:
        out_shape += [shaped(block // 2, 3 * hidden)] * 2 + [shaped(block, 3 * hidden)] * 3
        scratch += [
            pltpu.VMEM((4 * count, rows // 2, block), BF),
            pltpu.VMEM((count * block, 2 * rows), BF),
            pltpu.VMEM((count * block, 2 * rows), BF),
        ]
    return pl.pallas_call(
        functools.partial(expert_kernel, count),
        in_specs=[smem()] + unread(6 + len(near)),
        out_specs=[vmem] * len(out_shape),
        out_shape=out_shape,
        scratch_shapes=scratch,
        cost_estimate=cost(2 * rows * model * 5 * hidden, 2 * model * 3 * hidden + 8 * rows * model),
        compiler_params=params(),
        name=name,
    )(scalars, *packed, w_in, w_out, *near)


def unpack_rows(pos_ref, own, rec, r):
    hot = jnp.concatenate(
        [slot_one_hot(pos_ref[r : r + 1, :]), slot_one_hot(pos_ref[r + 4 : r + 5, :])], axis=0
    ).astype(BF)
    rows = jnp.concatenate([own[r * CAP : (r + 1) * CAP], rec[r * CAP : (r + 1) * CAP]], axis=0)
    dims = (((0,), (0,)), ((), ()))
    return lax.dot_general(hot, rows, dims, preferred_element_type=F32).astype(BF)


def unpack_near_kernel(pos, own, rec, after, plus, minus, here, across):
    for r, ref in enumerate((here, minus, plus, across)):
        ref[...] = unpack_rows(pos, own, rec, r)


def unpack_far_kernel(pos, own, rec, after, up, down, across_plus, across_minus):
    half = up.shape[1]
    for i, r in enumerate((0, 3)):
        value = unpack_rows(pos, own, rec, r)
        up[i] = value[:half]
        down[i] = value[half:]
    across_minus[...] = unpack_rows(pos, own, rec, 1)
    across_plus[...] = unpack_rows(pos, own, rec, 2)


def unpack(kernel, pos, own, rec, after, shapes, name):
    wide = own.shape[1]
    vmem = pl.BlockSpec(memory_space=pltpu.VMEM)
    return pl.pallas_call(
        kernel,
        in_specs=[vmem] * 3 + unread(1),
        out_specs=[vmem] * len(shapes),
        out_shape=[shaped(*shape) for shape in shapes],
        cost_estimate=cost(4 * 2 * 128 * 96 * wide, 2 * wide * (2 * own.shape[0] + 512)),
        compiler_params=params(),
        name=name,
    )(pos, own, rec, after)


def weight_block(all_grads, xs):
    dy = jnp.concatenate([ref[...] for ref in xs[:4]], axis=0)
    x = jnp.concatenate([ref[...] for ref in xs[4:]], axis=0)
    wide = 2 * all_grads.shape[1] // 3
    dims = (((0,), (0,)), ((), ()))
    into = lax.dot_general(x, all_grads[:, :wide], dims, preferred_element_type=F32)
    out = lax.dot_general(dy, all_grads[:, wide:], dims, preferred_element_type=F32)
    return into.astype(BF), out.astype(BF)


def weight_rest_kernel(dest, *refs):
    xs, all_grads, block = refs[:8], refs[8], refs[10]
    into, out = weight_block(all_grads, xs)
    wide = into.shape[1]
    block[0, :, :wide] = into
    block[0, :, wide:] = out


def weight_grads(scalars, at, steps, xs, grads, after, name):
    model = xs[0].shape[1]
    rows, wide = grads.shape
    block = model // 8
    return pl.pallas_call(
        weight_rest_kernel,
        grid_spec=pltpu.PrefetchScalarGridSpec(
            num_scalar_prefetch=1,
            grid=(steps,),
            in_specs=[pl.BlockSpec((x.shape[0], block), lambda i, d: (0, d[at + i])) for x in xs]
            + [pl.BlockSpec(grads.shape, lambda i, d: (0, 0))]
            + unread(1),
            out_specs=pl.BlockSpec((1, block, wide), lambda i, d: (i, 0, 0)),
        ),
        out_shape=shaped(steps, block, wide),
        cost_estimate=cost(2 * rows * block * wide * steps, 2 * steps * block * (wide + 2 * rows) + 2 * rows * wide),
        compiler_params=params(),
        name=name,
    )(scalars, *xs, grads, after)


def added(a, b):
    return a.astype(F32) + b.astype(F32)


def second_kernel(keep, from_minus, from_plus, straight, after, up, down):
    up[0] = added(keep[0], from_minus[...]).astype(BF)
    up[1] = straight[0, 0]
    down[0] = added(keep[1], from_plus[...]).astype(BF)
    down[1] = straight[0, 1]


def second(keep, from_minus, from_plus, blocks, after, part, name):
    rows, width = keep.shape
    half = rows // 2
    count = blocks.shape[0]
    pair = pl.BlockSpec((2, part, width), lambda j: (0, j, 0))
    single = pl.BlockSpec((part, width), lambda j: (j, 0))
    up, down = pl.pallas_call(
        second_kernel,
        grid=(half // part,),
        in_specs=[
            pair,
            single,
            single,
            pl.BlockSpec((1, 2, part, width), lambda j: (count - 1, 0, j, 0)),
            *unread(1),
        ],
        out_specs=[pair] * 2,
        out_shape=[shaped(2, half, width)] * 2,
        cost_estimate=cost(2 * rows * width, 10 * rows * width),
        compiler_params=params(),
        name=name,
    )(halves(keep), from_minus, from_plus, blocks.reshape(count, 2, half, width), after)
    return up.reshape(rows, width), down.reshape(rows, width)


def third_kernel(blocks, from_minus, from_plus, from_over, after, up, down, over):
    up[0] = added(blocks[0, 0], from_minus[1]).astype(BF)
    up[1] = added(blocks[0, 1], from_over[0]).astype(BF)
    down[0] = added(blocks[1, 0], from_over[1]).astype(BF)
    down[1] = added(blocks[1, 1], from_plus[1]).astype(BF)
    over[0] = added(blocks[2, 0], from_minus[0]).astype(BF)
    over[1] = added(blocks[2, 1], from_plus[0]).astype(BF)


def third(blocks, from_minus, from_plus, from_over, after, part, name):
    count, rows, width = blocks.shape
    half = rows // 2
    pair = pl.BlockSpec((2, part, width), lambda j: (0, j, 0))
    outs = pl.pallas_call(
        third_kernel,
        grid=(half // part,),
        in_specs=[pl.BlockSpec((3, 2, part, width), lambda j: (0, 0, j, 0))] + [pair] * 3 + unread(1),
        out_specs=[pair] * 3,
        out_shape=[shaped(2, half, width)] * 3,
        cost_estimate=cost(3 * rows * width, 18 * rows * width),
        compiler_params=params(),
        name=name,
    )(blocks.reshape(count, 2, half, width), halves(from_minus), halves(from_plus), halves(from_over), after)
    return [v.reshape(rows, width) for v in outs]


def second_rows_kernel(plus, across_plus, minus, across_minus, from_minus, from_plus, after, up, down):
    half = from_minus.shape[1]
    for i, (above, below) in enumerate(((plus, minus), (across_plus, across_minus))):
        up[i, :half] = added(above[:half], from_minus[i]).astype(BF)
        up[i, half:] = above[half:]
        down[i, :half] = below[:half]
        down[i, half:] = added(below[half:], from_plus[i]).astype(BF)


def third_rows_kernel(across, from_minus, from_plus, after, out):
    out[...] = (added(from_minus[0], from_plus[0]) + across[...].astype(F32)).astype(BF)


def last_rows_kernel(here, from_minus, from_plus, from_over, after, out, prob):
    total = added(here[...], from_minus[0]) + added(from_plus[0], from_over[...])
    width, routed = out.shape[1], prob.shape[0]
    out[...] = total[:, :width].astype(BF)
    prob[...] = total[:, width:].T[:routed].astype(BF)


def second_rows(plus, across_plus, minus, across_minus, from_minus, from_plus, after):
    rows, width = plus.shape
    vmem = pl.BlockSpec(memory_space=pltpu.VMEM)
    return pl.pallas_call(
        second_rows_kernel,
        in_specs=[vmem] * 6 + unread(1),
        out_specs=[vmem] * 2,
        out_shape=[shaped(2, rows, width)] * 2,
        cost_estimate=cost(2 * rows * width, 20 * rows * width),
        compiler_params=params(),
        name="second_rows",
    )(plus, across_plus, minus, across_minus, from_minus, from_plus, after)


def third_rows(across, from_minus, from_plus, after):
    rows, width = across.shape
    part = rows // 2
    row = pl.BlockSpec((part, width), lambda j: (j, 0))
    other = pl.BlockSpec((1, part, width), lambda j: (1, j, 0))
    return pl.pallas_call(
        third_rows_kernel,
        grid=(2,),
        in_specs=[row, other, other] + unread(1),
        out_specs=row,
        out_shape=shaped(rows, width),
        cost_estimate=cost(2 * rows * width, 8 * rows * width),
        compiler_params=params(),
        name="third_rows",
    )(across, from_minus, from_plus, after)


def last_rows(here, from_minus, from_plus, from_over, after, width, routed):
    rows, wide = here.shape
    whole = lambda *shape: pl.BlockSpec(shape, lambda j: (0,) * len(shape))
    return pl.pallas_call(
        last_rows_kernel,
        grid=(1,),
        in_specs=[whole(rows, wide), whole(1, rows, wide), whole(1, rows, wide), whole(rows, wide)] + unread(1),
        out_specs=[whole(rows, width), whole(routed, rows)],
        out_shape=[shaped(rows, width), shaped(routed, rows)],
        cost_estimate=cost(3 * rows * wide, 10 * rows * wide),
        compiler_params=params(),
        name="last_rows",
    )(here, from_minus, from_plus, from_over, after)


def last_weights_kernel(block, a, b, c, after, into, out):
    total = added(block[0], a[...]) + added(b[...], c[...])
    wide = into.shape[2]
    into[0] = total[:, :wide]
    out[0] = total[:, wide:]


def last_weights(blocks, a, b, c, after):
    count, rows, width = blocks.shape
    wide, part = 2 * width // 3, 128
    row = pl.BlockSpec((part, width), lambda j: (j, 0))
    return pl.pallas_call(
        last_weights_kernel,
        grid=(rows // part,),
        in_specs=[pl.BlockSpec((1, part, width), lambda j: (3, j, 0))] + [row] * 3 + unread(1),
        out_specs=[
            pl.BlockSpec((1, part, wide), lambda j: (0, j, 0)),
            pl.BlockSpec((1, part, width - wide), lambda j: (0, j, 0)),
        ],
        out_shape=[shaped(1, rows, wide, dtype=F32), shaped(1, rows, width - wide, dtype=F32)],
        cost_estimate=cost(3 * rows * width, 12 * rows * width),
        compiler_params=params(),
        name="last_weights",
    )(blocks, a, b, c, after)


def body(tokens, grad_out, combine_weights, expert_ids, w_in, w_out):
    me = lax.axis_index("expert")
    group = lax.axis_index("dp")
    gx, gz = group // SIDE, group % SIDE

    def dest(dx, dz):
        return ((gx + dx) % 2) * SIDE + (gz + dz + SIDE) % SIDE

    first = [dest(1, 2), dest(1, 1), dest(1, -1), dest(0, 2)]
    rest = [dest(0, 1), dest(0, -1), dest(1, 0), dest(0, 0)]
    scalars = jnp.stack([me, me + 1 - 2 * (me % 2), *first, *rest]).astype(jnp.int32)
    tok_rows, routed = expert_ids.shape
    model = tokens.shape[1]
    w_in_e, w_out_e = w_in[0], w_out[0]
    half = tok_rows // 2

    mine = attach(grad_out, tokens, expert_ids, combine_weights)
    minus, plus, across = expert_move(mine, dy=1), expert_move(mine, dy=-1), expert_move(mine, dx=1)
    up, down, over = mix(minus, plus, across)
    up2 = expert_move(up, dy=1)
    down2 = expert_move(down, dy=-1)
    over2 = expert_move(over, dx=1)

    cols = model // 4

    def packed(blocks_of, values, after, name):
        return pack(
            blocks_of, scalars,
            [(v, fixed(v.shape[0], 128, 2 * model // 128)) for v in values],
            [(v, col(v.shape[0], cols)) for v in values],
            [(v, col(v.shape[0], cols, 4)) for v in values],
            model, after, name,
        )

    own_dy_a, sib_dy_a, own_x_a, sib_x_a, pos_a = packed(
        near_blocks, (mine, minus, plus, across), over, "pack_near"
    )
    rec_dy_a, rec_x_a = expert_move(sib_dy_a, dc=1), expert_move(sib_x_a, dc=1)
    near_packed = (own_dy_a, rec_dy_a, own_x_a, rec_x_a)

    last_up, last_down = tail(up2, down2, own_x_a)
    last_up2 = expert_move(last_up, dy=1)
    last_down2 = expert_move(last_down, dy=-1)

    grads_a, row_own_a, row_sib_a = expert_rows(
        scalars, near_packed, w_in_e, w_out_e, (last_up,), "expert_near"
    )
    row_rec_a = expert_move(row_sib_a, dc=1)

    own_dy_b, sib_dy_b, own_x_b, sib_x_b, pos_b = packed(
        far_blocks, (up2, down2, over2, last_up2, last_down2), grads_a, "pack_far"
    )
    rec_dy_b, rec_x_b = expert_move(sib_dy_b, dc=1), expert_move(sib_x_b, dc=1)
    far_packed = (own_dy_b, rec_dy_b, own_x_b, rec_x_b)
    grads, row_own_b, row_sib_b, w_up, w_down, w_over, w_keep, straight = expert_rows(
        scalars, far_packed, w_in_e, w_out_e, (grads_a, *near_packed), "expert_far"
    )
    row_rec_b = expert_move(row_sib_b, dc=1)

    xs = (*near_packed[:2], *far_packed[:2], *near_packed[2:], *far_packed[2:])
    w_up1 = dp_move(w_up, dy=1)
    w_down1 = dp_move(w_down, dy=-1)
    w_over1 = dp_move(w_over, dx=1)

    half_pair, block = (2, half, model + 128), (tok_rows, model + 128)
    r_up, r_down, across_plus, across_minus = unpack(
        unpack_far_kernel, pos_b, row_own_b, row_rec_b, w_keep, [half_pair] * 2 + [block] * 2, "unpack_far"
    )
    r_up1 = expert_move(r_up, dy=1)
    r_down1 = expert_move(r_down, dy=-1)

    w_up, w_down = second(w_keep, w_up1, w_down1, straight[None], across_plus, 64, "second_w")
    w_up2 = dp_move(w_up, dy=1)
    w_down2 = dp_move(w_down, dy=-1)

    r_plus, r_minus, r_here, r_across = unpack(
        unpack_near_kernel, pos_a, row_own_a, row_rec_a, w_up, [block] * 4, "unpack_near"
    )
    w_rest = weight_grads(scalars, 6, 4, xs, grads, r_plus, "weights_rest")
    r_up, r_down = second_rows(r_plus, across_plus, r_minus, across_minus, r_up1, r_down1, w_rest)
    r_up2 = expert_move(r_up, dy=1)
    r_down2 = expert_move(r_down, dy=-1)

    w_up, w_down, w_over = third(w_rest, w_up2, w_down2, w_over1, r_up, 64, "third_w")
    w_up3 = dp_move(w_up, dy=1)
    w_down3 = dp_move(w_down, dy=-1)
    w_over3 = dp_move(w_over, dx=1)

    r_over = expert_move(third_rows(r_across, r_up2, r_down2, w_over), dx=1)
    d_w_in, d_w_out = last_weights(w_rest, w_up3, w_down3, w_over3, w_over)
    d_tokens, d_combine = last_rows(r_here, r_up2, r_down2, r_over, d_w_out, model, routed)
    return d_tokens, d_combine.T, d_w_in, d_w_out


def solution(mesh):
    rows = P(("dp", "expert"), None)
    return jax.shard_map(
        body,
        mesh=mesh,
        in_specs=(rows, rows, rows, rows, P("expert", None, None), P("expert", None, None)),
        out_specs=(rows, rows, P("expert", "dp", None), P("expert", "dp", None)),
        check_vma=False,
    )
```

```python
import functools

import jax
import jax.numpy as jnp
from jax import lax
from jax.experimental import pallas as pl
from jax.experimental.pallas import tpu as pltpu
from jax.sharding import PartitionSpec as P

BF = jnp.bfloat16
F32 = jnp.float32
CAP = 48
SIDE = 4
VMEM_LIMIT = 63 * 1024 * 1024


def params(**kw):
    return pltpu.CompilerParams(vmem_limit_bytes=VMEM_LIMIT, **kw)


def cost(flops, nbytes):
    return pl.CostEstimate(flops=int(flops) // 10, bytes_accessed=int(nbytes) // 10, transcendentals=0)


def spec(shape, index=None):
    zeros = (0,) * len(shape)
    return pl.BlockSpec(shape, index if index is not None else (lambda *_: zeros))


def smem():
    return pl.BlockSpec(memory_space=pltpu.SMEM)


def unread(count):
    return [pl.BlockSpec(memory_space=pl.ANY)] * count


def col(rows, cols, first=0):
    return pl.BlockSpec((rows, cols), lambda j: (0, j + first))


def fixed(rows, cols, at):
    return pl.BlockSpec((rows, cols), lambda j: (0, at))


def shaped(*shape, dtype=BF):
    return jax.ShapeDtypeStruct(shape, dtype)


def expert_index(x, y, c):
    return (x % 2) * 8 + (y % SIDE) * 2 + c % 2


def expert_move(value, dx=0, dy=0, dc=0):
    pairs = [
        (expert_index(x, y, c), expert_index(x + dx, y + dy, c + dc))
        for x in range(2)
        for y in range(SIDE)
        for c in range(2)
    ]
    return lax.ppermute(value, "expert", pairs)


def dp_move(value, dx=0, dy=0):
    pairs = [
        (x * SIDE + z, ((x + dx) % 2) * SIDE + (z + dy) % SIDE)
        for x in range(2)
        for z in range(SIDE)
    ]
    return lax.ppermute(value, "dp", pairs)


def attach_kernel(grad_out, tokens, ids, weights, out):
    width = tokens.shape[1]
    out[:, :width] = grad_out[...]
    out[:, width : 2 * width] = tokens[...]
    rows, routed = ids.shape[1], ids.shape[0]
    turned = jnp.concatenate(
        [ids[...].astype(F32), weights[...].astype(F32), jnp.zeros((128 - 2 * routed, rows), F32)], axis=0
    )
    out[:, 2 * width :] = turned.T.astype(BF)


def attach(grad_out, tokens, ids, weights):
    rows, width = tokens.shape
    wide = 2 * width + 128
    vmem = pl.BlockSpec(memory_space=pltpu.VMEM)
    return pl.pallas_call(
        attach_kernel,
        in_specs=[vmem] * 4,
        out_specs=vmem,
        out_shape=shaped(rows, wide),
        cost_estimate=cost(0, 4 * rows * wide),
        compiler_params=params(),
        name="attach",
    )(grad_out, tokens, ids.T, weights.T)


def halves(value):
    return value.reshape(2, value.shape[0] // 2, value.shape[1])


def mix_kernel(minus, plus, across, up, down, over):
    up[0] = minus[0]
    up[1] = across[0]
    down[0] = plus[1]
    down[1] = across[1]
    over[0] = plus[0]
    over[1] = minus[1]


def mix(minus, plus, across):
    rows, width = minus.shape
    half, part = rows // 2, 32
    one = pl.BlockSpec((2, part, width), lambda j: (0, j, 0))
    outs = pl.pallas_call(
        mix_kernel,
        grid=(half // part,),
        in_specs=[one] * 3,
        out_specs=[one] * 3,
        out_shape=[shaped(2, half, width)] * 3,
        cost_estimate=cost(0, 6 * minus.size * 2),
        compiler_params=params(),
        name="mix",
    )(halves(minus), halves(plus), halves(across))
    return [v.reshape(rows, width) for v in outs]


def tail_kernel(up, down, after, last_up, last_down):
    last_up[...] = up[0]
    last_down[...] = down[0]


def tail(up, down, after):
    rows, width = up.shape
    half, part = rows // 2, 32
    one = pl.BlockSpec((1, part, width), lambda j: (1, j, 0))
    out = pl.BlockSpec((part, width), lambda j: (j, 0))
    return pl.pallas_call(
        tail_kernel,
        grid=(half // part,),
        in_specs=[one] * 2 + unread(1),
        out_specs=[out] * 2,
        out_shape=[shaped(half, width)] * 2,
        cost_estimate=cost(0, 8 * half * width),
        compiler_params=params(),
        name="tail",
    )(halves(up), halves(down), after)


def slot_one_hot(pos):
    slots = lax.broadcasted_iota(jnp.int32, (CAP, pos.shape[1]), 0).astype(F32)
    return jnp.where(slots == pos, 1.0, 0.0)


def both_hot(pos_ref, r):
    return jnp.concatenate(
        [slot_one_hot(pos_ref[r : r + 1, :]), slot_one_hot(pos_ref[r + 4 : r + 5, :])], axis=0
    ).astype(BF)


def place_slots(experts, routes, pos_ref, hot_ref):
    tokens = routes[0].shape[0]
    turned = [route.astype(F32).T for route in routes]
    rows = []
    for which in range(2):
        expert = experts[which].astype(F32)
        for t in turned:
            hit = (t[0:1] == expert) | (t[1:2] == expert) | (t[2:3] == expert)
            rows.append(jnp.where(hit, 1.0, 0.0))
    hits = jnp.concatenate(rows, axis=0)
    earlier = lax.broadcasted_iota(jnp.int32, (tokens, tokens), 0) < lax.broadcasted_iota(
        jnp.int32, (tokens, tokens), 1
    )
    rank = jnp.dot(hits.astype(BF), jnp.where(earlier, 1.0, 0.0).astype(BF), preferred_element_type=F32)
    pos_ref[...] = jnp.where(hits > 0.5, rank, -1.0)
    for r in range(4):
        hot_ref[r] = both_hot(pos_ref, r)


def pack_rows(hot_ref, blocks, own, sib, columns):
    for r, block in enumerate(blocks):
        rows = jnp.dot(hot_ref[r], block, preferred_element_type=F32).astype(BF)
        own[r * CAP : (r + 1) * CAP, columns] = rows[:CAP]
        sib[r * CAP : (r + 1) * CAP, columns] = rows[CAP:]


def near_blocks(refs):
    return [ref[...] for ref in refs]


def far_blocks(refs):
    up, down, over, last_up, last_down = [ref[...] for ref in refs]
    half = last_up.shape[0]
    return [
        jnp.concatenate([up[:half], down[:half]], axis=0),
        jnp.concatenate([up[half:], over[half:]], axis=0),
        jnp.concatenate([over[:half], down[half:]], axis=0),
        jnp.concatenate([last_up, last_down], axis=0),
    ]


def pack_kernel(blocks_of, count, experts, *refs):
    routes, dys, xs = refs[:count], refs[count : 2 * count], refs[2 * count : 3 * count]
    own_dy, sib_dy, own_x, sib_x, pos, hot = refs[3 * count + 1 :]
    step = pl.program_id(0)
    cols = dys[0].shape[1]

    @pl.when(step == 0)
    def _():
        route = blocks_of(routes)
        place_slots((experts[0], experts[1]), route, pos, hot)
        pack_rows(hot, route, own_x, sib_x, pl.ds(4 * cols, 128))

    pack_rows(hot, blocks_of(dys), own_dy, sib_dy, slice(None))
    pack_rows(hot, blocks_of(xs), own_x, sib_x, pl.ds(pl.multiple_of(step * cols, cols), cols))


def pack(blocks_of, experts, routes, dys, xs, width, after, name):
    operands = [*routes, *dys, *xs]
    rows = 4 * CAP
    tokens = 128
    return pl.pallas_call(
        functools.partial(pack_kernel, blocks_of, len(dys)),
        grid=(4,),
        in_specs=[smem()] + [s for _, s in operands] + unread(1),
        out_specs=[col(rows, width // 4)] * 2 + [spec((rows, width + 128))] * 2 + [spec((8, tokens))],
        out_shape=[shaped(rows, width)] * 2
        + [shaped(rows, width + 128)] * 2
        + [shaped(8, tokens, dtype=F32)],
        scratch_shapes=[pltpu.VMEM((4, 2 * CAP, tokens), BF)],
        cost_estimate=cost(8 * 2 * 96 * 128 * width, 8 * 128 * width * 2 + 8 * rows * width),
        compiler_params=params(),
        name=name,
    )(experts, *[a for a, _ in operands], after)


def expert_kernel(count, scalars, own_dy, rec_dy, own_x, rec_x, w_in, w_out, *refs):
    near, refs = refs[: 6 if count else 1], refs[6 if count else 1 :]
    grads, refs = refs[0], refs[1:]
    probs = refs[: 1 if count else 2]
    first, refs = refs[len(probs) : 6 if count else 2], refs[6 if count else 2 :]
    x_all, dy_all, w_all, w_out_all, a_all, b_all, g_all, sems = refs[:8]
    half, (model, hidden) = own_dy.shape[0], w_out.shape
    block = model // 8
    base = grads.shape[0] - 2 * half
    me = scalars[0].astype(F32)
    low, high = pl.ds(0, half), pl.ds(half, half)
    gate, up_cols = pl.ds(0, hidden), pl.ds(hidden, hidden)
    moves = [
        (own_x, x_all.at[low]),
        (rec_x, x_all.at[high]),
        (w_in.at[:, gate], w_all.at[:, gate]),
        (w_in.at[:, up_cols], w_all.at[:, up_cols]),
        (own_dy, dy_all.at[low]),
        (rec_dy, dy_all.at[high]),
        (w_out, w_out_all),
    ]
    if count:
        near_grads, near_packed = near[0], near[1:5]
        near_cols, x_turned, dy_turned = refs[8:]
        moves.append((near_grads, grads.at[pl.ds(0, base)]))
        for i in range(count):
            columns = pl.ds(pl.multiple_of(scalars[2 + i] * block, block), block)
            for k, value in enumerate(near_packed):
                moves.append((value.at[:, columns], near_cols.at[4 * i + k]))
    copies = [pltpu.make_async_copy(a, b, sems.at[i]) for i, (a, b) in enumerate(moves)]
    for copy in copies:
        copy.start()

    for copy in copies[:2]:
        copy.wait()
    routes = [x_all[rows, model:].astype(F32) for rows in (slice(0, half), slice(half, 2 * half))]
    weights = []
    for route in routes:
        weight = jnp.zeros((half, 1), F32)
        for k in range(3):
            weight += jnp.where(route[:, k : k + 1] == me, route[:, 3 + k : 4 + k], 0.0)
        weights.append(weight)
    p = jnp.concatenate(weights, axis=0)

    copies[2].wait()
    a_all[...] = jnp.dot(x_all[:, :model], w_all[:, :hidden], preferred_element_type=F32)
    copies[3].wait()
    b_all[...] = jnp.dot(x_all[:, :model], w_all[:, hidden:], preferred_element_type=F32)
    for copy in copies[4:7]:
        copy.wait()
    g_all[...] = jnp.dot(dy_all[...], w_out_all[...], preferred_element_type=F32)

    d_prob = jnp.zeros((2 * half, 1), F32)
    chunk = 256
    for f in range(hidden // chunk):
        at = slice(f * chunk, (f + 1) * chunk)
        a, b, g = a_all[:, at], b_all[:, at], g_all[:, at]
        s = jax.nn.sigmoid(a)
        silu = a * s
        value = silu * b
        d_prob += jnp.sum(value.astype(BF).astype(F32) * g, axis=1, keepdims=True)
        d_hidden = g * p
        grads[base:, at] = (d_hidden * b * (s * (1.0 + a * (1.0 - s)))).astype(BF)
        grads[base:, f * chunk + hidden : (f + 1) * chunk + hidden] = (d_hidden * silu).astype(BF)
        grads[base:, f * chunk + 2 * hidden : (f + 1) * chunk + 2 * hidden] = (value * p).astype(BF)

    for k, route in enumerate(routes):
        lane = lax.broadcasted_iota(jnp.int32, route.shape, 1)
        value = jnp.where((route == me) & (lane < 3), d_prob[k * half : (k + 1) * half], 0.0).astype(BF)
        if count:
            probs[0][k * half : (k + 1) * half] = value
        else:
            probs[k][:, model:] = value

    if count:
        up, down, over, keep, straight = first
        for copy in copies[7:]:
            copy.wait()
        for i in range(count):
            columns = pl.ds(pl.multiple_of(scalars[2 + i] * block, block), block)
            dy = jnp.concatenate([near_cols[4 * i], near_cols[4 * i + 1], dy_all[:, columns]], axis=0)
            x = jnp.concatenate([near_cols[4 * i + 2], near_cols[4 * i + 3], x_all[:, columns]], axis=0)
            x_turned[i * block : (i + 1) * block, :] = x.T
            dy_turned[i * block : (i + 1) * block, :] = dy.T
        part = block // 2
        places = (
            (up, 0), (down, 0), (keep, 0), (over, 0), (over, part), (keep, part), (straight, 0), (straight, part),
        )
        for k, turned in enumerate((x_turned, x_turned, dy_turned)):
            at = slice(k * hidden, (k + 1) * hidden)
            value = jnp.dot(turned[...], grads[:, at], preferred_element_type=F32).astype(BF)
            for i, (ref, to) in enumerate(places):
                ref[to : to + part, at] = value[i * part : (i + 1) * part]

    if not count:
        own_row, sib_row = probs
        chunk = 512
        dims = (((1,), (1,)), ((), ()))
        for n in range(model // chunk):
            at = slice(n * chunk, (n + 1) * chunk)
            rows = lax.dot_general(
                grads[base:, : 2 * hidden], w_all[at, :], dims, preferred_element_type=F32
            ).astype(BF)
            own_row[:, at] = rows[:half]
            sib_row[:, at] = rows[half:]


def expert_rows(scalars, packed, w_in, w_out, near, name):
    model, hidden = w_out.shape
    rows, block = 2 * packed[0].shape[0], model // 8
    count = 4 if len(near) > 1 else 0
    vmem = pl.BlockSpec(memory_space=pltpu.VMEM)
    total = 2 * rows if count else rows
    out_shape = [shaped(total, 3 * hidden)]
    out_shape += [shaped(rows, 128)] if count else [shaped(rows // 2, model + 128)] * 2
    scratch = [
        pltpu.VMEM((rows, model + 128), BF),
        pltpu.VMEM((rows, model), BF),
        pltpu.VMEM((model, 2 * hidden), BF),
        pltpu.VMEM((model, hidden), BF),
        pltpu.VMEM((rows, hidden), F32),
        pltpu.VMEM((rows, hidden), F32),
        pltpu.VMEM((rows, hidden), F32),
        pltpu.SemaphoreType.DMA((8 + 4 * count,)),
    ]
    if count:
        out_shape += [shaped(block // 2, 3 * hidden)] * 2 + [shaped(block, 3 * hidden)] * 3
        scratch += [
            pltpu.VMEM((4 * count, rows // 2, block), BF),
            pltpu.VMEM((count * block, 2 * rows), BF),
            pltpu.VMEM((count * block, 2 * rows), BF),
        ]
    return pl.pallas_call(
        functools.partial(expert_kernel, count),
        in_specs=[smem()] + unread(6 + len(near)),
        out_specs=[vmem] * len(out_shape),
        out_shape=out_shape,
        scratch_shapes=scratch,
        cost_estimate=cost(2 * rows * model * 5 * hidden, 2 * model * 3 * hidden + 8 * rows * model),
        compiler_params=params(),
        name=name,
    )(scalars, *packed, w_in, w_out, *near)


def row_grad_kernel(grads, prob, w_in, own_low, own_high, sib_low, sib_high):
    half, width = own_low.shape[0], own_low.shape[1]
    dims = (((1,), (1,)), ((), ()))
    rows = lax.dot_general(grads[...], w_in[...], dims, preferred_element_type=F32).astype(BF)
    step = pl.program_id(0)

    @pl.when(step == 0)
    def _():
        own_low[...] = rows[:half]
        sib_low[...] = rows[half:]

    @pl.when(step == 1)
    def _():
        own_high[:, :width] = rows[:half]
        own_high[:, width:] = prob[:half]
        sib_high[:, :width] = rows[half:]
        sib_high[:, width:] = prob[half:]


def row_grad(grads, prob, w_in):
    model, wide = w_in.shape
    rows, chunk = grads.shape[0] // 2, model // 2
    shapes = [(rows // 2, chunk), (rows // 2, chunk + 128)] * 2
    return pl.pallas_call(
        row_grad_kernel,
        grid=(2,),
        in_specs=[
            pl.BlockSpec((rows, wide), lambda j: (1, 0)),
            spec(prob.shape),
            pl.BlockSpec((chunk, wide), lambda j: (j, 0)),
        ],
        out_specs=[spec(shape) for shape in shapes],
        out_shape=[shaped(*shape) for shape in shapes],
        cost_estimate=cost(2 * rows * model * wide, 2 * model * wide + 2 * rows * (model + wide)),
        compiler_params=params(),
        name="row_grad",
    )(grads, prob, w_in)


def unpack_rows(pos_ref, parts, r):
    hot = jnp.concatenate(
        [slot_one_hot(pos_ref[r : r + 1, :]), slot_one_hot(pos_ref[r + 4 : r + 5, :])], axis=0
    ).astype(BF)
    dims = (((0,), (0,)), ((), ()))
    values = []
    for own, rec in parts:
        rows = jnp.concatenate([own[r * CAP : (r + 1) * CAP], rec[r * CAP : (r + 1) * CAP]], axis=0)
        values.append(lax.dot_general(hot, rows, dims, preferred_element_type=F32).astype(BF))
    return jnp.concatenate(values, axis=1)


def unpack_near_kernel(pos, own, rec, after, plus, minus, here, across):
    for r, ref in enumerate((here, minus, plus, across)):
        ref[...] = unpack_rows(pos, [(own, rec)], r)


def unpack_far_kernel(pos, own_low, own_high, rec_low, rec_high, after, up, down, across_plus, across_minus):
    half = up.shape[1]
    parts = [(own_low, rec_low), (own_high, rec_high)]
    for i, r in enumerate((0, 3)):
        value = unpack_rows(pos, parts, r)
        up[i] = value[:half]
        down[i] = value[half:]
    across_minus[...] = unpack_rows(pos, parts, 1)
    across_plus[...] = unpack_rows(pos, parts, 2)


def unpack(kernel, pos, packed, after, shapes, name):
    wide = shapes[-1][-1]
    vmem = pl.BlockSpec(memory_space=pltpu.VMEM)
    return pl.pallas_call(
        kernel,
        in_specs=[vmem] * (1 + len(packed)) + unread(1),
        out_specs=[vmem] * len(shapes),
        out_shape=[shaped(*shape) for shape in shapes],
        cost_estimate=cost(4 * 2 * 128 * 96 * wide, 2 * wide * 900),
        compiler_params=params(),
        name=name,
    )(pos, *packed, after)


def weight_block(all_grads, xs):
    dy = jnp.concatenate([ref[...] for ref in xs[:4]], axis=0)
    x = jnp.concatenate([ref[...] for ref in xs[4:]], axis=0)
    wide = 2 * all_grads.shape[1] // 3
    dims = (((0,), (0,)), ((), ()))
    into = lax.dot_general(x, all_grads[:, :wide], dims, preferred_element_type=F32)
    out = lax.dot_general(dy, all_grads[:, wide:], dims, preferred_element_type=F32)
    return into.astype(BF), out.astype(BF)


def weight_rest_kernel(dest, *refs):
    xs, all_grads, block = refs[:8], refs[8], refs[10]
    into, out = weight_block(all_grads, xs)
    wide = into.shape[1]
    block[0, :, :wide] = into
    block[0, :, wide:] = out


def weight_grads(scalars, at, steps, xs, grads, after, name):
    model = xs[0].shape[1]
    rows, wide = grads.shape
    block = model // 8
    return pl.pallas_call(
        weight_rest_kernel,
        grid_spec=pltpu.PrefetchScalarGridSpec(
            num_scalar_prefetch=1,
            grid=(steps,),
            in_specs=[pl.BlockSpec((x.shape[0], block), lambda i, d: (0, d[at + i])) for x in xs]
            + [pl.BlockSpec(grads.shape, lambda i, d: (0, 0))]
            + unread(1),
            out_specs=pl.BlockSpec((1, block, wide), lambda i, d: (i, 0, 0)),
        ),
        out_shape=shaped(steps, block, wide),
        cost_estimate=cost(2 * rows * block * wide * steps, 2 * steps * block * (wide + 2 * rows) + 2 * rows * wide),
        compiler_params=params(),
        name=name,
    )(scalars, *xs, grads, after)


def added(a, b):
    return a.astype(F32) + b.astype(F32)


def second_kernel(keep, from_minus, from_plus, straight, after, up, down):
    up[0] = added(keep[0], from_minus[...]).astype(BF)
    up[1] = straight[0, 0]
    down[0] = added(keep[1], from_plus[...]).astype(BF)
    down[1] = straight[0, 1]


def second(keep, from_minus, from_plus, blocks, after, part, name):
    rows, width = keep.shape
    half = rows // 2
    count = blocks.shape[0]
    pair = pl.BlockSpec((2, part, width), lambda j: (0, j, 0))
    single = pl.BlockSpec((part, width), lambda j: (j, 0))
    up, down = pl.pallas_call(
        second_kernel,
        grid=(half // part,),
        in_specs=[
            pair,
            single,
            single,
            pl.BlockSpec((1, 2, part, width), lambda j: (count - 1, 0, j, 0)),
            *unread(1),
        ],
        out_specs=[pair] * 2,
        out_shape=[shaped(2, half, width)] * 2,
        cost_estimate=cost(2 * rows * width, 10 * rows * width),
        compiler_params=params(),
        name=name,
    )(halves(keep), from_minus, from_plus, blocks.reshape(count, 2, half, width), after)
    return up.reshape(rows, width), down.reshape(rows, width)


def third_kernel(blocks, from_minus, from_plus, from_over, after, up, down, over):
    up[0] = added(blocks[0, 0], from_minus[1]).astype(BF)
    up[1] = added(blocks[0, 1], from_over[0]).astype(BF)
    down[0] = added(blocks[1, 0], from_over[1]).astype(BF)
    down[1] = added(blocks[1, 1], from_plus[1]).astype(BF)
    over[0] = added(blocks[2, 0], from_minus[0]).astype(BF)
    over[1] = added(blocks[2, 1], from_plus[0]).astype(BF)


def third(blocks, from_minus, from_plus, from_over, after, part, name):
    count, rows, width = blocks.shape
    half = rows // 2
    pair = pl.BlockSpec((2, part, width), lambda j: (0, j, 0))
    outs = pl.pallas_call(
        third_kernel,
        grid=(half // part,),
        in_specs=[pl.BlockSpec((3, 2, part, width), lambda j: (0, 0, j, 0))] + [pair] * 3 + unread(1),
        out_specs=[pair] * 3,
        out_shape=[shaped(2, half, width)] * 3,
        cost_estimate=cost(3 * rows * width, 18 * rows * width),
        compiler_params=params(),
        name=name,
    )(blocks.reshape(count, 2, half, width), halves(from_minus), halves(from_plus), halves(from_over), after)
    return [v.reshape(rows, width) for v in outs]


def second_rows_kernel(plus, across_plus, minus, across_minus, from_minus, from_plus, after, up, down):
    half = from_minus.shape[1]
    for i, (above, below) in enumerate(((plus, minus), (across_plus, across_minus))):
        up[i, :half] = added(above[:half], from_minus[i]).astype(BF)
        up[i, half:] = above[half:]
        down[i, :half] = below[:half]
        down[i, half:] = added(below[half:], from_plus[i]).astype(BF)


def third_rows_kernel(across, from_minus, from_plus, after, out):
    out[...] = (added(from_minus[0], from_plus[0]) + across[...].astype(F32)).astype(BF)


def last_rows_kernel(here, from_minus, from_plus, from_over, after, out, prob):
    total = added(here[...], from_minus[0]) + added(from_plus[0], from_over[...])
    width, routed = out.shape[1], prob.shape[0]
    out[...] = total[:, :width].astype(BF)
    prob[...] = total[:, width:].T[:routed].astype(BF)


def second_rows(plus, across_plus, minus, across_minus, from_minus, from_plus, after):
    rows, width = plus.shape
    vmem = pl.BlockSpec(memory_space=pltpu.VMEM)
    return pl.pallas_call(
        second_rows_kernel,
        in_specs=[vmem] * 6 + unread(1),
        out_specs=[vmem] * 2,
        out_shape=[shaped(2, rows, width)] * 2,
        cost_estimate=cost(2 * rows * width, 20 * rows * width),
        compiler_params=params(),
        name="second_rows",
    )(plus, across_plus, minus, across_minus, from_minus, from_plus, after)


def third_rows(across, from_minus, from_plus, after):
    rows, width = across.shape
    part = rows // 2
    row = pl.BlockSpec((part, width), lambda j: (j, 0))
    other = pl.BlockSpec((1, part, width), lambda j: (1, j, 0))
    return pl.pallas_call(
        third_rows_kernel,
        grid=(2,),
        in_specs=[row, other, other] + unread(1),
        out_specs=row,
        out_shape=shaped(rows, width),
        cost_estimate=cost(2 * rows * width, 8 * rows * width),
        compiler_params=params(),
        name="third_rows",
    )(across, from_minus, from_plus, after)


def last_rows(here, from_minus, from_plus, from_over, after, width, routed):
    rows, wide = here.shape
    whole = lambda *shape: pl.BlockSpec(shape, lambda j: (0,) * len(shape))
    return pl.pallas_call(
        last_rows_kernel,
        grid=(1,),
        in_specs=[whole(rows, wide), whole(1, rows, wide), whole(1, rows, wide), whole(rows, wide)] + unread(1),
        out_specs=[whole(rows, width), whole(routed, rows)],
        out_shape=[shaped(rows, width), shaped(routed, rows)],
        cost_estimate=cost(3 * rows * wide, 10 * rows * wide),
        compiler_params=params(),
        name="last_rows",
    )(here, from_minus, from_plus, from_over, after)


def last_weights_kernel(block, a, b, c, after, into, out):
    total = added(block[0], a[...]) + added(b[...], c[...])
    wide = into.shape[2]
    into[0] = total[:, :wide]
    out[0] = total[:, wide:]


def last_weights(blocks, a, b, c, after):
    count, rows, width = blocks.shape
    wide, part = 2 * width // 3, 128
    row = pl.BlockSpec((part, width), lambda j: (j, 0))
    return pl.pallas_call(
        last_weights_kernel,
        grid=(rows // part,),
        in_specs=[pl.BlockSpec((1, part, width), lambda j: (3, j, 0))] + [row] * 3 + unread(1),
        out_specs=[
            pl.BlockSpec((1, part, wide), lambda j: (0, j, 0)),
            pl.BlockSpec((1, part, width - wide), lambda j: (0, j, 0)),
        ],
        out_shape=[shaped(1, rows, wide, dtype=F32), shaped(1, rows, width - wide, dtype=F32)],
        cost_estimate=cost(3 * rows * width, 12 * rows * width),
        compiler_params=params(),
        name="last_weights",
    )(blocks, a, b, c, after)


def body(tokens, grad_out, combine_weights, expert_ids, w_in, w_out):
    me = lax.axis_index("expert")
    group = lax.axis_index("dp")
    gx, gz = group // SIDE, group % SIDE

    def dest(dx, dz):
        return ((gx + dx) % 2) * SIDE + (gz + dz + SIDE) % SIDE

    first = [dest(1, 2), dest(1, 1), dest(1, -1), dest(0, 2)]
    rest = [dest(0, 1), dest(0, -1), dest(1, 0), dest(0, 0)]
    scalars = jnp.stack([me, me + 1 - 2 * (me % 2), *first, *rest]).astype(jnp.int32)
    tok_rows, routed = expert_ids.shape
    model = tokens.shape[1]
    w_in_e, w_out_e = w_in[0], w_out[0]
    half = tok_rows // 2

    mine = attach(grad_out, tokens, expert_ids, combine_weights)
    minus, plus, across = expert_move(mine, dy=1), expert_move(mine, dy=-1), expert_move(mine, dx=1)
    up, down, over = mix(minus, plus, across)
    up2 = expert_move(up, dy=1)
    down2 = expert_move(down, dy=-1)
    over2 = expert_move(over, dx=1)

    cols = model // 4

    def packed(blocks_of, values, after, name):
        return pack(
            blocks_of, scalars,
            [(v, fixed(v.shape[0], 128, 2 * model // 128)) for v in values],
            [(v, col(v.shape[0], cols)) for v in values],
            [(v, col(v.shape[0], cols, 4)) for v in values],
            model, after, name,
        )

    own_dy_a, sib_dy_a, own_x_a, sib_x_a, pos_a = packed(
        near_blocks, (mine, minus, plus, across), over, "pack_near"
    )
    rec_dy_a, rec_x_a = expert_move(sib_dy_a, dc=1), expert_move(sib_x_a, dc=1)
    near_packed = (own_dy_a, rec_dy_a, own_x_a, rec_x_a)

    last_up, last_down = tail(up2, down2, own_x_a)
    last_up2 = expert_move(last_up, dy=1)
    last_down2 = expert_move(last_down, dy=-1)

    grads_a, row_own_a, row_sib_a = expert_rows(
        scalars, near_packed, w_in_e, w_out_e, (last_up,), "expert_near"
    )
    row_rec_a = expert_move(row_sib_a, dc=1)

    own_dy_b, sib_dy_b, own_x_b, sib_x_b, pos_b = packed(
        far_blocks, (up2, down2, over2, last_up2, last_down2), grads_a, "pack_far"
    )
    rec_dy_b, rec_x_b = expert_move(sib_dy_b, dc=1), expert_move(sib_x_b, dc=1)
    far_packed = (own_dy_b, rec_dy_b, own_x_b, rec_x_b)
    grads, prob_b, w_up, w_down, w_over, w_keep, straight = expert_rows(
        scalars, far_packed, w_in_e, w_out_e, (grads_a, *near_packed, row_rec_a), "expert_far"
    )

    xs = (*near_packed[:2], *far_packed[:2], *near_packed[2:], *far_packed[2:])
    w_up1 = dp_move(w_up, dy=1)
    w_down1 = dp_move(w_down, dy=-1)
    w_over1 = dp_move(w_over, dx=1)

    own_low, own_high, sib_low, sib_high = row_grad(grads, prob_b, w_in_e)
    row_parts = (own_low, own_high, expert_move(sib_low, dc=1), expert_move(sib_high, dc=1))

    half_pair, block = (2, half, model + 128), (tok_rows, model + 128)
    r_up, r_down, across_plus, across_minus = unpack(
        unpack_far_kernel, pos_b, row_parts, w_keep, [half_pair] * 2 + [block] * 2, "unpack_far"
    )
    r_up1 = expert_move(r_up, dy=1)
    r_down1 = expert_move(r_down, dy=-1)

    w_up, w_down = second(w_keep, w_up1, w_down1, straight[None], across_plus, 64, "second_w")
    w_up2 = dp_move(w_up, dy=1)
    w_down2 = dp_move(w_down, dy=-1)

    r_plus, r_minus, r_here, r_across = unpack(
        unpack_near_kernel, pos_a, (row_own_a, row_rec_a), w_up, [block] * 4, "unpack_near"
    )
    w_rest = weight_grads(scalars, 6, 4, xs, grads, r_plus, "weights_rest")
    r_up, r_down = second_rows(r_plus, across_plus, r_minus, across_minus, r_up1, r_down1, w_rest)
    r_up2 = expert_move(r_up, dy=1)
    r_down2 = expert_move(r_down, dy=-1)

    w_up, w_down, w_over = third(w_rest, w_up2, w_down2, w_over1, r_up, 64, "third_w")
    w_up3 = dp_move(w_up, dy=1)
    w_down3 = dp_move(w_down, dy=-1)
    w_over3 = dp_move(w_over, dx=1)

    r_over = expert_move(third_rows(r_across, r_up2, r_down2, w_over), dx=1)
    d_w_in, d_w_out = last_weights(w_rest, w_up3, w_down3, w_over3, w_over)
    d_tokens, d_combine = last_rows(r_here, r_up2, r_down2, r_over, d_w_out, model, routed)
    return d_tokens, d_combine.T, d_w_in, d_w_out


def solution(mesh):
    rows = P(("dp", "expert"), None)
    return jax.shard_map(
        body,
        mesh=mesh,
        in_specs=(rows, rows, rows, rows, P("expert", None, None), P("expert", None, None)),
        out_specs=(rows, rows, P("expert", "dp", None), P("expert", "dp", None)),
        check_vma=False,
    )
```

```python
import functools

import jax
import jax.numpy as jnp
from jax import lax
from jax.experimental import pallas as pl
from jax.experimental.pallas import tpu as pltpu
from jax.sharding import PartitionSpec as P

BF = jnp.bfloat16
F32 = jnp.float32
CAP = 48
SIDE = 4
VMEM_LIMIT = 63 * 1024 * 1024


def params(**kw):
    return pltpu.CompilerParams(vmem_limit_bytes=VMEM_LIMIT, **kw)


def cost(flops, nbytes):
    return pl.CostEstimate(flops=int(flops) // 10, bytes_accessed=int(nbytes) // 10, transcendentals=0)


def spec(shape, index=None):
    zeros = (0,) * len(shape)
    return pl.BlockSpec(shape, index if index is not None else (lambda *_: zeros))


def smem():
    return pl.BlockSpec(memory_space=pltpu.SMEM)


def unread(count):
    return [pl.BlockSpec(memory_space=pl.ANY)] * count


def col(rows, cols, first=0):
    return pl.BlockSpec((rows, cols), lambda j: (0, j + first))


def fixed(rows, cols, at):
    return pl.BlockSpec((rows, cols), lambda j: (0, at))


def shaped(*shape, dtype=BF):
    return jax.ShapeDtypeStruct(shape, dtype)


def expert_index(x, y, c):
    return (x % 2) * 8 + (y % SIDE) * 2 + c % 2


def expert_move(value, dx=0, dy=0, dc=0):
    pairs = [
        (expert_index(x, y, c), expert_index(x + dx, y + dy, c + dc))
        for x in range(2)
        for y in range(SIDE)
        for c in range(2)
    ]
    return lax.ppermute(value, "expert", pairs)


def dp_move(value, dx=0, dy=0):
    pairs = [
        (x * SIDE + z, ((x + dx) % 2) * SIDE + (z + dy) % SIDE)
        for x in range(2)
        for z in range(SIDE)
    ]
    return lax.ppermute(value, "dp", pairs)


def attach_kernel(grad_out, tokens, ids, weights, out):
    width = tokens.shape[1]
    out[:, :width] = grad_out[...]
    out[:, width : 2 * width] = tokens[...]
    rows, routed = ids.shape[1], ids.shape[0]
    turned = jnp.concatenate(
        [ids[...].astype(F32), weights[...].astype(F32), jnp.zeros((128 - 2 * routed, rows), F32)], axis=0
    )
    out[:, 2 * width :] = turned.T.astype(BF)


def attach(grad_out, tokens, ids, weights):
    rows, width = tokens.shape
    wide = 2 * width + 128
    vmem = pl.BlockSpec(memory_space=pltpu.VMEM)
    return pl.pallas_call(
        attach_kernel,
        in_specs=[vmem] * 4,
        out_specs=vmem,
        out_shape=shaped(rows, wide),
        cost_estimate=cost(0, 4 * rows * wide),
        compiler_params=params(),
        name="attach",
    )(grad_out, tokens, ids.T, weights.T)


def halves(value):
    return value.reshape(2, value.shape[0] // 2, value.shape[1])


def mix_kernel(minus, plus, across, up, down, over):
    up[0] = minus[0]
    up[1] = across[0]
    down[0] = plus[1]
    down[1] = across[1]
    over[0] = plus[0]
    over[1] = minus[1]


def mix(minus, plus, across):
    rows, width = minus.shape
    half, part = rows // 2, 32
    one = pl.BlockSpec((2, part, width), lambda j: (0, j, 0))
    outs = pl.pallas_call(
        mix_kernel,
        grid=(half // part,),
        in_specs=[one] * 3,
        out_specs=[one] * 3,
        out_shape=[shaped(2, half, width)] * 3,
        cost_estimate=cost(0, 6 * minus.size * 2),
        compiler_params=params(),
        name="mix",
    )(halves(minus), halves(plus), halves(across))
    return [v.reshape(rows, width) for v in outs]


def tail_kernel(up, down, after, last_up, last_down):
    last_up[...] = up[0]
    last_down[...] = down[0]


def tail(up, down, after):
    rows, width = up.shape
    half, part = rows // 2, 32
    one = pl.BlockSpec((1, part, width), lambda j: (1, j, 0))
    out = pl.BlockSpec((part, width), lambda j: (j, 0))
    return pl.pallas_call(
        tail_kernel,
        grid=(half // part,),
        in_specs=[one] * 2 + unread(1),
        out_specs=[out] * 2,
        out_shape=[shaped(half, width)] * 2,
        cost_estimate=cost(0, 8 * half * width),
        compiler_params=params(),
        name="tail",
    )(halves(up), halves(down), after)


def slot_one_hot(pos):
    slots = lax.broadcasted_iota(jnp.int32, (CAP, pos.shape[1]), 0).astype(F32)
    return jnp.where(slots == pos, 1.0, 0.0)


def both_hot(pos_ref, r):
    return jnp.concatenate(
        [slot_one_hot(pos_ref[r : r + 1, :]), slot_one_hot(pos_ref[r + 4 : r + 5, :])], axis=0
    ).astype(BF)


def place_slots(experts, routes, pos_ref, hot_ref):
    tokens = routes[0].shape[0]
    turned = [route.astype(F32).T for route in routes]
    rows = []
    for which in range(2):
        expert = experts[which].astype(F32)
        for t in turned:
            hit = (t[0:1] == expert) | (t[1:2] == expert) | (t[2:3] == expert)
            rows.append(jnp.where(hit, 1.0, 0.0))
    hits = jnp.concatenate(rows, axis=0)
    earlier = lax.broadcasted_iota(jnp.int32, (tokens, tokens), 0) < lax.broadcasted_iota(
        jnp.int32, (tokens, tokens), 1
    )
    rank = jnp.dot(hits.astype(BF), jnp.where(earlier, 1.0, 0.0).astype(BF), preferred_element_type=F32)
    pos_ref[...] = jnp.where(hits > 0.5, rank, -1.0)
    for r in range(4):
        hot_ref[r] = both_hot(pos_ref, r)


def pack_rows(hot_ref, blocks, own, sib, columns):
    for r, block in enumerate(blocks):
        rows = jnp.dot(hot_ref[r], block, preferred_element_type=F32).astype(BF)
        own[r * CAP : (r + 1) * CAP, columns] = rows[:CAP]
        sib[r * CAP : (r + 1) * CAP, columns] = rows[CAP:]


def near_blocks(refs):
    return [ref[...] for ref in refs]


def far_blocks(refs):
    up, down, over, last_up, last_down = [ref[...] for ref in refs]
    half = last_up.shape[0]
    return [
        jnp.concatenate([up[:half], down[:half]], axis=0),
        jnp.concatenate([up[half:], over[half:]], axis=0),
        jnp.concatenate([over[:half], down[half:]], axis=0),
        jnp.concatenate([last_up, last_down], axis=0),
    ]


def pack_kernel(blocks_of, count, experts, *refs):
    routes, dys, xs = refs[:count], refs[count : 2 * count], refs[2 * count : 3 * count]
    own_dy, sib_dy, own_x, sib_x, pos, hot = refs[3 * count + 1 :]
    step = pl.program_id(0)
    cols = dys[0].shape[1]

    @pl.when(step == 0)
    def _():
        route = blocks_of(routes)
        place_slots((experts[0], experts[1]), route, pos, hot)
        pack_rows(hot, route, own_x, sib_x, pl.ds(4 * cols, 128))

    pack_rows(hot, blocks_of(dys), own_dy, sib_dy, slice(None))
    pack_rows(hot, blocks_of(xs), own_x, sib_x, pl.ds(pl.multiple_of(step * cols, cols), cols))


def pack(blocks_of, experts, routes, dys, xs, width, after, name):
    operands = [*routes, *dys, *xs]
    rows = 4 * CAP
    tokens = 128
    return pl.pallas_call(
        functools.partial(pack_kernel, blocks_of, len(dys)),
        grid=(4,),
        in_specs=[smem()] + [s for _, s in operands] + unread(1),
        out_specs=[col(rows, width // 4)] * 2 + [spec((rows, width + 128))] * 2 + [spec((8, tokens))],
        out_shape=[shaped(rows, width)] * 2
        + [shaped(rows, width + 128)] * 2
        + [shaped(8, tokens, dtype=F32)],
        scratch_shapes=[pltpu.VMEM((4, 2 * CAP, tokens), BF)],
        cost_estimate=cost(8 * 2 * 96 * 128 * width, 8 * 128 * width * 2 + 8 * rows * width),
        compiler_params=params(),
        name=name,
    )(experts, *[a for a, _ in operands], after)


def expert_kernel(count, scalars, own_dy, rec_dy, own_x, rec_x, w_in, w_out, *refs):
    near, refs = refs[: 6 if count else 1], refs[6 if count else 1 :]
    grads, refs = refs[0], refs[1:]
    probs = refs[: 1 if count else 2]
    first, refs = refs[len(probs) : 6 if count else 2], refs[6 if count else 2 :]
    x_all, dy_all, w_all, w_out_all, a_all, b_all, g_all, sems = refs[:8]
    half, (model, hidden) = own_dy.shape[0], w_out.shape
    block = model // 8
    base = grads.shape[0] - 2 * half
    me = scalars[0].astype(F32)
    low, high = pl.ds(0, half), pl.ds(half, half)
    gate, up_cols = pl.ds(0, hidden), pl.ds(hidden, hidden)
    moves = [
        (own_x, x_all.at[low]),
        (rec_x, x_all.at[high]),
        (w_in.at[:, gate], w_all.at[:, gate]),
        (w_in.at[:, up_cols], w_all.at[:, up_cols]),
        (own_dy, dy_all.at[low]),
        (rec_dy, dy_all.at[high]),
        (w_out, w_out_all),
    ]
    if count:
        near_grads, near_packed = near[0], near[1:5]
        near_cols, x_turned, dy_turned = refs[8:]
        moves.append((near_grads, grads.at[pl.ds(0, base)]))
        for i in range(count):
            columns = pl.ds(pl.multiple_of(scalars[2 + i] * block, block), block)
            for k, value in enumerate(near_packed):
                moves.append((value.at[:, columns], near_cols.at[4 * i + k]))
    copies = [pltpu.make_async_copy(a, b, sems.at[i]) for i, (a, b) in enumerate(moves)]
    for copy in copies:
        copy.start()

    for copy in copies[:2]:
        copy.wait()
    routes = [x_all[rows, model:].astype(F32) for rows in (slice(0, half), slice(half, 2 * half))]
    weights = []
    for route in routes:
        weight = jnp.zeros((half, 1), F32)
        for k in range(3):
            weight += jnp.where(route[:, k : k + 1] == me, route[:, 3 + k : 4 + k], 0.0)
        weights.append(weight)
    p = jnp.concatenate(weights, axis=0)

    copies[2].wait()
    a_all[...] = jnp.dot(x_all[:, :model], w_all[:, :hidden], preferred_element_type=F32)
    copies[3].wait()
    b_all[...] = jnp.dot(x_all[:, :model], w_all[:, hidden:], preferred_element_type=F32)
    for copy in copies[4:7]:
        copy.wait()
    g_all[...] = jnp.dot(dy_all[...], w_out_all[...], preferred_element_type=F32)

    d_prob = jnp.zeros((2 * half, 1), F32)
    chunk = 256
    for f in range(hidden // chunk):
        at = slice(f * chunk, (f + 1) * chunk)
        a, b, g = a_all[:, at], b_all[:, at], g_all[:, at]
        s = jax.nn.sigmoid(a)
        silu = a * s
        value = silu * b
        d_prob += jnp.sum(value.astype(BF).astype(F32) * g, axis=1, keepdims=True)
        d_hidden = g * p
        grads[base:, at] = (d_hidden * b * (s * (1.0 + a * (1.0 - s)))).astype(BF)
        grads[base:, f * chunk + hidden : (f + 1) * chunk + hidden] = (d_hidden * silu).astype(BF)
        grads[base:, f * chunk + 2 * hidden : (f + 1) * chunk + 2 * hidden] = (value * p).astype(BF)

    for k, route in enumerate(routes):
        lane = lax.broadcasted_iota(jnp.int32, route.shape, 1)
        value = jnp.where((route == me) & (lane < 3), d_prob[k * half : (k + 1) * half], 0.0).astype(BF)
        if count:
            probs[0][k * half : (k + 1) * half] = value
        else:
            probs[k][:, model:] = value

    if count:
        up, down, over, keep, straight = first
        for copy in copies[7:]:
            copy.wait()
        for i in range(count):
            columns = pl.ds(pl.multiple_of(scalars[2 + i] * block, block), block)
            dy = jnp.concatenate([near_cols[4 * i], near_cols[4 * i + 1], dy_all[:, columns]], axis=0)
            x = jnp.concatenate([near_cols[4 * i + 2], near_cols[4 * i + 3], x_all[:, columns]], axis=0)
            x_turned[i * block : (i + 1) * block, :] = x.T
            dy_turned[i * block : (i + 1) * block, :] = dy.T
        part = block // 2
        places = (
            (up, 0), (down, 0), (keep, 0), (over, 0), (over, part), (keep, part), (straight, 0), (straight, part),
        )
        for k, turned in enumerate((x_turned, x_turned, dy_turned)):
            at = slice(k * hidden, (k + 1) * hidden)
            value = jnp.dot(turned[...], grads[:, at], preferred_element_type=F32).astype(BF)
            for i, (ref, to) in enumerate(places):
                ref[to : to + part, at] = value[i * part : (i + 1) * part]

    if not count:
        own_row, sib_row = probs
        chunk = 512
        dims = (((1,), (1,)), ((), ()))
        for n in range(model // chunk):
            at = slice(n * chunk, (n + 1) * chunk)
            rows = lax.dot_general(
                grads[base:, : 2 * hidden], w_all[at, :], dims, preferred_element_type=F32
            ).astype(BF)
            own_row[:, at] = rows[:half]
            sib_row[:, at] = rows[half:]


def expert_rows(scalars, packed, w_in, w_out, near, name):
    model, hidden = w_out.shape
    rows, block = 2 * packed[0].shape[0], model // 8
    count = 4 if len(near) > 1 else 0
    vmem = pl.BlockSpec(memory_space=pltpu.VMEM)
    total = 2 * rows if count else rows
    out_shape = [shaped(total, 3 * hidden)]
    out_shape += [shaped(rows, 128)] if count else [shaped(rows // 2, model + 128)] * 2
    scratch = [
        pltpu.VMEM((rows, model + 128), BF),
        pltpu.VMEM((rows, model), BF),
        pltpu.VMEM((model, 2 * hidden), BF),
        pltpu.VMEM((model, hidden), BF),
        pltpu.VMEM((rows, hidden), F32),
        pltpu.VMEM((rows, hidden), F32),
        pltpu.VMEM((rows, hidden), F32),
        pltpu.SemaphoreType.DMA((8 + 4 * count,)),
    ]
    if count:
        out_shape += [shaped(block // 2, 3 * hidden)] * 2 + [shaped(block, 3 * hidden)] * 3
        scratch += [
            pltpu.VMEM((4 * count, rows // 2, block), BF),
            pltpu.VMEM((count * block, 2 * rows), BF),
            pltpu.VMEM((count * block, 2 * rows), BF),
        ]
    return pl.pallas_call(
        functools.partial(expert_kernel, count),
        in_specs=[smem()] + unread(6 + len(near)),
        out_specs=[vmem] * len(out_shape),
        out_shape=out_shape,
        scratch_shapes=scratch,
        cost_estimate=cost(2 * rows * model * 5 * hidden, 2 * model * 3 * hidden + 8 * rows * model),
        compiler_params=params(),
        name=name,
    )(scalars, *packed, w_in, w_out, *near)


def row_grad_kernel(grads, prob, w_in, own_low, own_high, sib_low, sib_high):
    half, width = own_low.shape[0], own_low.shape[1]
    dims = (((1,), (1,)), ((), ()))
    rows = lax.dot_general(grads[...], w_in[...], dims, preferred_element_type=F32).astype(BF)
    step = pl.program_id(0)

    @pl.when(step == 0)
    def _():
        own_low[...] = rows[:half]
        sib_low[...] = rows[half:]

    @pl.when(step == 1)
    def _():
        own_high[:, :width] = rows[:half]
        own_high[:, width:] = prob[:half]
        sib_high[:, :width] = rows[half:]
        sib_high[:, width:] = prob[half:]


def row_grad(grads, prob, w_in):
    model, wide = w_in.shape
    rows, chunk = grads.shape[0] // 2, model // 2
    shapes = [(rows // 2, chunk), (rows // 2, chunk + 128)] * 2
    return pl.pallas_call(
        row_grad_kernel,
        grid=(2,),
        in_specs=[
            pl.BlockSpec((rows, wide), lambda j: (1, 0)),
            spec(prob.shape),
            pl.BlockSpec((chunk, wide), lambda j: (j, 0)),
        ],
        out_specs=[spec(shape) for shape in shapes],
        out_shape=[shaped(*shape) for shape in shapes],
        cost_estimate=cost(2 * rows * model * wide, 2 * model * wide + 2 * rows * (model + wide)),
        compiler_params=params(),
        name="row_grad",
    )(grads, prob, w_in)


def unpack_rows(pos_ref, parts, r):
    hot = jnp.concatenate(
        [slot_one_hot(pos_ref[r : r + 1, :]), slot_one_hot(pos_ref[r + 4 : r + 5, :])], axis=0
    ).astype(BF)
    dims = (((0,), (0,)), ((), ()))
    values = []
    for own, rec in parts:
        rows = jnp.concatenate([own[r * CAP : (r + 1) * CAP], rec[r * CAP : (r + 1) * CAP]], axis=0)
        values.append(lax.dot_general(hot, rows, dims, preferred_element_type=F32).astype(BF))
    return jnp.concatenate(values, axis=1)


def unpack_near_kernel(pos, own, rec, after, plus, minus, here, across):
    for r, ref in enumerate((here, minus, plus, across)):
        ref[...] = unpack_rows(pos, [(own, rec)], r)


def unpack_far_kernel(pos, own_low, own_high, rec_low, rec_high, after, up, down, across_plus, across_minus):
    half = up.shape[1]
    parts = [(own_low, rec_low), (own_high, rec_high)]
    for i, r in enumerate((0, 3)):
        value = unpack_rows(pos, parts, r)
        up[i] = value[:half]
        down[i] = value[half:]
    across_minus[...] = unpack_rows(pos, parts, 1)
    across_plus[...] = unpack_rows(pos, parts, 2)


def unpack(kernel, pos, packed, after, shapes, name):
    wide = shapes[-1][-1]
    vmem = pl.BlockSpec(memory_space=pltpu.VMEM)
    return pl.pallas_call(
        kernel,
        in_specs=[vmem] * (1 + len(packed)) + unread(1),
        out_specs=[vmem] * len(shapes),
        out_shape=[shaped(*shape) for shape in shapes],
        cost_estimate=cost(4 * 2 * 128 * 96 * wide, 2 * wide * 900),
        compiler_params=params(),
        name=name,
    )(pos, *packed, after)


def weight_block(all_grads, xs):
    dy = jnp.concatenate([ref[...] for ref in xs[:4]], axis=0)
    x = jnp.concatenate([ref[...] for ref in xs[4:]], axis=0)
    wide = 2 * all_grads.shape[1] // 3
    dims = (((0,), (0,)), ((), ()))
    into = lax.dot_general(x, all_grads[:, :wide], dims, preferred_element_type=F32)
    out = lax.dot_general(dy, all_grads[:, wide:], dims, preferred_element_type=F32)
    return into.astype(BF), out.astype(BF)


def weight_rest_kernel(dest, *refs):
    xs, all_grads, block = refs[:8], refs[8], refs[10]
    into, out = weight_block(all_grads, xs)
    wide = into.shape[1]
    block[0, :, :wide] = into
    block[0, :, wide:] = out


def weight_grads(scalars, at, steps, xs, grads, after, name):
    model = xs[0].shape[1]
    rows, wide = grads.shape
    block = model // 8
    return pl.pallas_call(
        weight_rest_kernel,
        grid_spec=pltpu.PrefetchScalarGridSpec(
            num_scalar_prefetch=1,
            grid=(steps,),
            in_specs=[pl.BlockSpec((x.shape[0], block), lambda i, d: (0, d[at + i])) for x in xs]
            + [pl.BlockSpec(grads.shape, lambda i, d: (0, 0))]
            + unread(1),
            out_specs=pl.BlockSpec((1, block, wide), lambda i, d: (i, 0, 0)),
        ),
        out_shape=shaped(steps, block, wide),
        cost_estimate=cost(2 * rows * block * wide * steps, 2 * steps * block * (wide + 2 * rows) + 2 * rows * wide),
        compiler_params=params(),
        name=name,
    )(scalars, *xs, grads, after)


def added(a, b):
    return a.astype(F32) + b.astype(F32)


def second_kernel(keep, from_minus, from_plus, straight, after, up, down):
    up[0] = added(keep[0], from_minus[...]).astype(BF)
    up[1] = straight[0, 0]
    down[0] = added(keep[1], from_plus[...]).astype(BF)
    down[1] = straight[0, 1]


def second(keep, from_minus, from_plus, blocks, after, part, name):
    rows, width = keep.shape
    half = rows // 2
    count = blocks.shape[0]
    pair = pl.BlockSpec((2, part, width), lambda j: (0, j, 0))
    single = pl.BlockSpec((part, width), lambda j: (j, 0))
    up, down = pl.pallas_call(
        second_kernel,
        grid=(half // part,),
        in_specs=[
            pair,
            single,
            single,
            pl.BlockSpec((1, 2, part, width), lambda j: (count - 1, 0, j, 0)),
            *unread(1),
        ],
        out_specs=[pair] * 2,
        out_shape=[shaped(2, half, width)] * 2,
        cost_estimate=cost(2 * rows * width, 10 * rows * width),
        compiler_params=params(),
        name=name,
    )(halves(keep), from_minus, from_plus, blocks.reshape(count, 2, half, width), after)
    return up.reshape(rows, width), down.reshape(rows, width)


def third_over_kernel(blocks, from_minus, from_plus, after, over):
    over[0] = added(blocks[0, 0], from_minus[0]).astype(BF)
    over[1] = added(blocks[0, 1], from_plus[0]).astype(BF)


def third_over(blocks, from_minus, from_plus, after):
    count, rows, width = blocks.shape
    half, part = rows // 2, 64
    first = pl.BlockSpec((1, part, width), lambda j: (0, j, 0))
    return pl.pallas_call(
        third_over_kernel,
        grid=(half // part,),
        in_specs=[pl.BlockSpec((1, 2, part, width), lambda j: (2, 0, j, 0)), first, first, *unread(1)],
        out_specs=pl.BlockSpec((2, part, width), lambda j: (0, j, 0)),
        out_shape=shaped(2, half, width),
        cost_estimate=cost(rows * width, 6 * rows * width),
        compiler_params=params(),
        name="third_over",
    )(blocks.reshape(count, 2, half, width), halves(from_minus), halves(from_plus), after).reshape(rows, width)


def third_kernel(blocks, from_minus, from_plus, from_over, after, up, down):
    up[0] = added(blocks[0, 0], from_minus[0]).astype(BF)
    up[1] = added(blocks[0, 1], from_over[0]).astype(BF)
    down[0] = added(blocks[1, 0], from_over[1]).astype(BF)
    down[1] = added(blocks[1, 1], from_plus[0]).astype(BF)


def third(blocks, from_minus, from_plus, from_over, after):
    count, rows, width = blocks.shape
    half, part = rows // 2, 64
    pair = pl.BlockSpec((2, part, width), lambda j: (0, j, 0))
    last = pl.BlockSpec((1, part, width), lambda j: (1, j, 0))
    outs = pl.pallas_call(
        third_kernel,
        grid=(half // part,),
        in_specs=[pl.BlockSpec((2, 2, part, width), lambda j: (0, 0, j, 0)), last, last, pair, *unread(1)],
        out_specs=[pair] * 2,
        out_shape=[shaped(2, half, width)] * 2,
        cost_estimate=cost(2 * rows * width, 12 * rows * width),
        compiler_params=params(),
        name="third",
    )(blocks.reshape(count, 2, half, width), halves(from_minus), halves(from_plus), halves(from_over), after)
    return [v.reshape(rows, width) for v in outs]


def second_rows_kernel(plus, across_plus, minus, across_minus, from_minus, from_plus, after, up, down):
    half = from_minus.shape[1]
    for i, (above, below) in enumerate(((plus, minus), (across_plus, across_minus))):
        up[i, :half] = added(above[:half], from_minus[i]).astype(BF)
        up[i, half:] = above[half:]
        down[i, :half] = below[:half]
        down[i, half:] = added(below[half:], from_plus[i]).astype(BF)


def third_rows_kernel(across, from_minus, from_plus, after, out):
    out[...] = (added(from_minus[0], from_plus[0]) + across[...].astype(F32)).astype(BF)


def last_rows_kernel(here, from_minus, from_plus, from_over, after, out, prob):
    total = added(here[...], from_minus[0]) + added(from_plus[0], from_over[...])
    width, routed = out.shape[1], prob.shape[0]
    out[...] = total[:, :width].astype(BF)
    prob[...] = total[:, width:].T[:routed].astype(BF)


def second_rows(plus, across_plus, minus, across_minus, from_minus, from_plus, after):
    rows, width = plus.shape
    vmem = pl.BlockSpec(memory_space=pltpu.VMEM)
    return pl.pallas_call(
        second_rows_kernel,
        in_specs=[vmem] * 6 + unread(1),
        out_specs=[vmem] * 2,
        out_shape=[shaped(2, rows, width)] * 2,
        cost_estimate=cost(2 * rows * width, 20 * rows * width),
        compiler_params=params(),
        name="second_rows",
    )(plus, across_plus, minus, across_minus, from_minus, from_plus, after)


def third_rows(across, from_minus, from_plus, after):
    rows, width = across.shape
    part = rows // 2
    row = pl.BlockSpec((part, width), lambda j: (j, 0))
    other = pl.BlockSpec((1, part, width), lambda j: (1, j, 0))
    return pl.pallas_call(
        third_rows_kernel,
        grid=(2,),
        in_specs=[row, other, other] + unread(1),
        out_specs=row,
        out_shape=shaped(rows, width),
        cost_estimate=cost(2 * rows * width, 8 * rows * width),
        compiler_params=params(),
        name="third_rows",
    )(across, from_minus, from_plus, after)


def last_rows(here, from_minus, from_plus, from_over, after, width, routed):
    rows, wide = here.shape
    whole = lambda *shape: pl.BlockSpec(shape, lambda j: (0,) * len(shape))
    return pl.pallas_call(
        last_rows_kernel,
        grid=(1,),
        in_specs=[whole(rows, wide), whole(1, rows, wide), whole(1, rows, wide), whole(rows, wide)] + unread(1),
        out_specs=[whole(rows, width), whole(routed, rows)],
        out_shape=[shaped(rows, width), shaped(routed, rows)],
        cost_estimate=cost(3 * rows * wide, 10 * rows * wide),
        compiler_params=params(),
        name="last_rows",
    )(here, from_minus, from_plus, from_over, after)


def last_over_kernel(block, over, total):
    total[...] = added(block[0], over[...])


def last_over(blocks, over):
    count, rows, width = blocks.shape
    part = 128
    row = pl.BlockSpec((part, width), lambda j: (j, 0))
    return pl.pallas_call(
        last_over_kernel,
        grid=(rows // part,),
        in_specs=[pl.BlockSpec((1, part, width), lambda j: (3, j, 0)), row],
        out_specs=row,
        out_shape=shaped(rows, width, dtype=F32),
        cost_estimate=cost(rows * width, 8 * rows * width),
        compiler_params=params(),
        name="last_over",
    )(blocks, over)


def last_weights_kernel(partial, a, b, into, out):
    total = partial[...] + added(a[...], b[...])
    wide = into.shape[2]
    into[0] = total[:, :wide]
    out[0] = total[:, wide:]


def last_weights(partial, a, b):
    rows, width = partial.shape
    wide, part = 2 * width // 3, 128
    row = pl.BlockSpec((part, width), lambda j: (j, 0))
    return pl.pallas_call(
        last_weights_kernel,
        grid=(rows // part,),
        in_specs=[row] * 3,
        out_specs=[
            pl.BlockSpec((1, part, wide), lambda j: (0, j, 0)),
            pl.BlockSpec((1, part, width - wide), lambda j: (0, j, 0)),
        ],
        out_shape=[shaped(1, rows, wide, dtype=F32), shaped(1, rows, width - wide, dtype=F32)],
        cost_estimate=cost(3 * rows * width, 12 * rows * width),
        compiler_params=params(),
        name="last_weights",
    )(partial, a, b)


def body(tokens, grad_out, combine_weights, expert_ids, w_in, w_out):
    me = lax.axis_index("expert")
    group = lax.axis_index("dp")
    gx, gz = group // SIDE, group % SIDE

    def dest(dx, dz):
        return ((gx + dx) % 2) * SIDE + (gz + dz + SIDE) % SIDE

    first = [dest(1, 2), dest(1, 1), dest(1, -1), dest(0, 2)]
    rest = [dest(0, 1), dest(0, -1), dest(1, 0), dest(0, 0)]
    scalars = jnp.stack([me, me + 1 - 2 * (me % 2), *first, *rest]).astype(jnp.int32)
    tok_rows, routed = expert_ids.shape
    model = tokens.shape[1]
    w_in_e, w_out_e = w_in[0], w_out[0]
    half = tok_rows // 2

    mine = attach(grad_out, tokens, expert_ids, combine_weights)
    minus, plus, across = expert_move(mine, dy=1), expert_move(mine, dy=-1), expert_move(mine, dx=1)
    up, down, over = mix(minus, plus, across)
    up2 = expert_move(up, dy=1)
    down2 = expert_move(down, dy=-1)
    over2 = expert_move(over, dx=1)

    cols = model // 4

    def packed(blocks_of, values, after, name):
        return pack(
            blocks_of, scalars,
            [(v, fixed(v.shape[0], 128, 2 * model // 128)) for v in values],
            [(v, col(v.shape[0], cols)) for v in values],
            [(v, col(v.shape[0], cols, 4)) for v in values],
            model, after, name,
        )

    own_dy_a, sib_dy_a, own_x_a, sib_x_a, pos_a = packed(
        near_blocks, (mine, minus, plus, across), over, "pack_near"
    )
    rec_dy_a, rec_x_a = expert_move(sib_dy_a, dc=1), expert_move(sib_x_a, dc=1)
    near_packed = (own_dy_a, rec_dy_a, own_x_a, rec_x_a)

    last_up, last_down = tail(up2, down2, own_x_a)
    last_up2 = expert_move(last_up, dy=1)
    last_down2 = expert_move(last_down, dy=-1)

    grads_a, row_own_a, row_sib_a = expert_rows(
        scalars, near_packed, w_in_e, w_out_e, (last_up,), "expert_near"
    )
    row_rec_a = expert_move(row_sib_a, dc=1)

    own_dy_b, sib_dy_b, own_x_b, sib_x_b, pos_b = packed(
        far_blocks, (up2, down2, over2, last_up2, last_down2), grads_a, "pack_far"
    )
    rec_dy_b, rec_x_b = expert_move(sib_dy_b, dc=1), expert_move(sib_x_b, dc=1)
    far_packed = (own_dy_b, rec_dy_b, own_x_b, rec_x_b)
    grads, prob_b, w_up, w_down, w_over, w_keep, straight = expert_rows(
        scalars, far_packed, w_in_e, w_out_e, (grads_a, *near_packed, row_rec_a), "expert_far"
    )

    xs = (*near_packed[:2], *far_packed[:2], *near_packed[2:], *far_packed[2:])
    w_up1 = dp_move(w_up, dy=1)
    w_down1 = dp_move(w_down, dy=-1)
    w_over1 = dp_move(w_over, dx=1)

    own_low, own_high, sib_low, sib_high = row_grad(grads, prob_b, w_in_e)
    row_parts = (own_low, own_high, expert_move(sib_low, dc=1), expert_move(sib_high, dc=1))

    half_pair, block = (2, half, model + 128), (tok_rows, model + 128)
    r_up, r_down, across_plus, across_minus = unpack(
        unpack_far_kernel, pos_b, row_parts, w_keep, [half_pair] * 2 + [block] * 2, "unpack_far"
    )
    r_up1 = expert_move(r_up, dy=1)
    r_down1 = expert_move(r_down, dy=-1)

    w_up, w_down = second(w_keep, w_up1, w_down1, straight[None], across_plus, 64, "second_w")
    w_up2 = dp_move(w_up, dy=1)
    w_down2 = dp_move(w_down, dy=-1)

    r_plus, r_minus, r_here, r_across = unpack(
        unpack_near_kernel, pos_a, (row_own_a, row_rec_a), w_up, [block] * 4, "unpack_near"
    )
    w_rest = weight_grads(scalars, 6, 4, xs, grads, r_plus, "weights_rest")
    r_up, r_down = second_rows(r_plus, across_plus, r_minus, across_minus, r_up1, r_down1, w_rest)
    r_up2 = expert_move(r_up, dy=1)
    r_down2 = expert_move(r_down, dy=-1)

    w_over = third_over(w_rest, w_up2, w_down2, r_up)
    w_over3 = dp_move(w_over, dx=1)
    w_up, w_down = third(w_rest, w_up2, w_down2, w_over1, w_over)
    w_up3 = dp_move(w_up, dy=1)
    w_down3 = dp_move(w_down, dy=-1)

    r_over = expert_move(third_rows(r_across, r_up2, r_down2, w_up), dx=1)
    d_w_in, d_w_out = last_weights(last_over(w_rest, w_over3), w_up3, w_down3)
    d_tokens, d_combine = last_rows(r_here, r_up2, r_down2, r_over, d_w_out, model, routed)
    return d_tokens, d_combine.T, d_w_in, d_w_out


def solution(mesh):
    rows = P(("dp", "expert"), None)
    return jax.shard_map(
        body,
        mesh=mesh,
        in_specs=(rows, rows, rows, rows, P("expert", None, None), P("expert", None, None)),
        out_specs=(rows, rows, P("expert", "dp", None), P("expert", "dp", None)),
        check_vma=False,
    )
```
